32 devices in a mesh: dp: 16 (over z, y, x), fsdp: 2 (over core).
Axes of the slice: x: 2, y: 2, z: 4, core: 2. Of those that a mesh axis runs over, the one named last changes fastest.
Arguments:
- inputs: bfloat16 [9216, 1024], P(('dp', 'fsdp')), may hold values from -6 to 6
- cotangent: bfloat16 [9216, 1024], P(('dp', 'fsdp')), may hold values from -6 to 6
- lengths: int32 [32, 3], P(('dp', 'fsdp')), may hold values from 0 to 288, as said below
- ffn1_in: bfloat16 [1024, 4096], P('fsdp'), may hold values from -0.1875 to 0.1875
- ffn1_out: bfloat16 [1024, 4096], P('fsdp'), may hold values from -0.09375 to 0.09375
- attn_qkv: bfloat16 [1024, 3072], P('fsdp'), may hold values from -0.1875 to 0.1875
- attn_out: bfloat16 [1024, 1024], P('fsdp'), may hold values from -1.5 to 1.5
- rel_table: bfloat16 [8, 65], P('fsdp'), may hold values from -4 to 4
- conv_in: bfloat16 [1024, 2048], P('fsdp'), may hold values from -0.1875 to 0.1875
- depth_kernel: bfloat16 [1024, 5], P('fsdp'), may hold values from -2.5 to 2.5
- conv_out: bfloat16 [1024, 1024], P('fsdp'), may hold values from -0.1875 to 0.1875
- ffn2_in: bfloat16 [1024, 4096], P('fsdp'), may hold values from -0.1875 to 0.1875
- ffn2_out: bfloat16 [1024, 4096], P('fsdp'), may hold values from -0.09375 to 0.09375
- gains: bfloat16 [1024, 6], P('fsdp'), may hold values from 0.5 to 1.5
- biases: bfloat16 [1024, 3], P('fsdp'), may hold values from -3 to 3
- inner_biases: bfloat16 [1024, 3], P('fsdp'), may hold values from -3 to 3
Outputs:
- layer_out: bfloat16 [9216, 1024], P(('dp', 'fsdp'))
- input_grad: bfloat16 [9216, 1024], P(('dp', 'fsdp'))
- ffn1_in_grad: float32 [1024, 4096], P('fsdp')
- ffn1_out_grad: float32 [1024, 4096], P('fsdp')
- attn_qkv_grad: float32 [1024, 3072], P('fsdp')
- attn_out_grad: float32 [1024, 1024], P('fsdp')
- rel_table_grad: float32 [8, 65], P('fsdp')
- conv_in_grad: float32 [1024, 2048], P('fsdp')
- depth_kernel_grad: float32 [1024, 5], P('fsdp')
- conv_out_grad: float32 [1024, 1024], P('fsdp')
- ffn2_in_grad: float32 [1024, 4096], P('fsdp')
- ffn2_out_grad: float32 [1024, 4096], P('fsdp')
- gains_grad: float32 [1024, 6], P('fsdp')
- biases_grad: float32 [1024, 3], P('fsdp')
- inner_biases_grad: float32 [1024, 3], P('fsdp')
The draws below stay inside these ranges and needn't reach their ends.
Inputs may be any that keep to these rules, and one draw needn't show every extreme that they name: `lengths`: row g lists the utterances of group g: its length bucket holds n = 3, 2 or 1 utterances (the other entries are 0), each of 288 // n // 2 to 288 // n frames, the first of exactly 288 // n; some group has n = 1.
All inputs are finite; a program needn't handle non-finite values.
Results may differ from the reference program's by a relative error of at most 0.035.
Values may be sent and summed in bfloat16 or wider, within the bound.
A program may use at most 320 MiB of HBM per device.

```python
import jax
import jax.numpy as jnp
from jax import lax

D = 1024
HEADS = 8
HEAD = 128
FF = 4096
KERNEL = 5
REL = 32
FRAMES = 288
GROUPS = 32
TOKENS = 9216


def draw_lengths(key, part):
    key = jax.random.fold_in(key, 11)
    key_bucket, key_pick, key_size = jax.random.split(key, 3)
    bucket = jax.random.randint(key_bucket, (GROUPS,), 0, 3)
    chosen = jax.random.randint(key_pick, (), 0, GROUPS)
    bucket = jnp.where(jnp.arange(GROUPS) == chosen, 2, bucket)
    utter_count = 3 - bucket
    longest = FRAMES // utter_count
    slot_index = jnp.arange(3)
    drawn_sizes = jax.random.randint(key_size, (GROUPS, 3), (longest // 2)[:, None], (longest + 1)[:, None])
    lengths_out = jnp.where(slot_index[None, :] == 0, longest[:, None], drawn_sizes)
    return jnp.where(slot_index[None, :] < utter_count[:, None], lengths_out, 0).astype(jnp.int32)


def levels(own_key, extent, shards, smallest, top_value):
    def one(position, parts):
        steps = jax.random.uniform(jax.random.fold_in(jax.random.fold_in(own_key, 6), position), (parts,), jnp.float32, smallest / len(shards), top_value / len(shards))
        return jnp.repeat(jnp.exp(steps), extent[position] // parts).reshape((-1,) + (1,) * (len(extent) - position - 1))

    factor_of = one(*shards[0])
    for cut in shards[1:]:
        factor_of = factor_of * one(*cut)
    return factor_of


def normal_values(stream_key, dims, scale, limit, cuts=(), kind=jnp.bfloat16):
    array = scale * jax.random.normal(stream_key, dims, jnp.float32)
    if cuts:
        array = array * levels(stream_key, dims, cuts, -0.22, 0.18)
    return jnp.clip(array, -limit, limit).astype(kind)


def setup_inputs(seed: int = 0) -> dict:
    key_of = jax.random.split(jax.random.key(seed), 17)
    inputs = normal_values(key_of[0], (TOKENS, D), 1.0, 6.0, ((0, 32),))
    cotangent = normal_values(key_of[1], (TOKENS, D), 1.0, 6.0, ((0, 32),))
    lengths = draw_lengths(jax.random.fold_in(key_of[16], 71), 0)
    ffn1_in = normal_values(key_of[3], (D, FF), D ** -0.5, 0.1875, ((0, 2),))
    ffn1_out = normal_values(key_of[4], (D, FF), FF ** -0.5, 0.09375, ((0, 2),))
    attn_qkv = normal_values(key_of[5], (D, 3 * D), D ** -0.5, 0.1875, ((0, 2),))
    attn_out = normal_values(key_of[6], (D, D), (D // 64) ** -0.5, 1.5, ((0, 2),))
    rel_table = normal_values(key_of[7], (HEADS, 2 * REL + 1), 1.0, 4.0, ((0, 2),))
    conv_in = normal_values(key_of[8], (D, 2 * D), D ** -0.5, 0.1875, ((0, 2),))
    depth_kernel = normal_values(key_of[9], (D, KERNEL), KERNEL ** -0.5, 2.5, ((0, 2),))
    conv_out = normal_values(key_of[10], (D, D), D ** -0.5, 0.1875, ((0, 2),))
    ffn2_in = normal_values(key_of[11], (D, FF), D ** -0.5, 0.1875, ((0, 2),))
    ffn2_out = normal_values(key_of[12], (D, FF), FF ** -0.5, 0.09375, ((0, 2),))
    gains = jnp.clip(1.0 + 0.1 * jax.random.normal(key_of[13], (D, 6), jnp.float32), 0.5, 1.5).astype(jnp.bfloat16)
    biases = normal_values(key_of[14], (D, 3), 0.5, 3.0, ((0, 2),))
    inner_biases = normal_values(key_of[15], (D, 3), 0.5, 3.0, ((0, 2),))
    return dict(inputs=inputs, cotangent=cotangent, lengths=lengths, ffn1_in=ffn1_in, ffn1_out=ffn1_out, attn_qkv=attn_qkv, attn_out=attn_out, rel_table=rel_table, conv_in=conv_in, depth_kernel=depth_kernel, conv_out=conv_out, ffn2_in=ffn2_in, ffn2_out=ffn2_out, gains=gains, biases=biases, inner_biases=inner_biases)


EPSILON = 1e-05
MASKED = -1000000000.0

@jax.custom_vjp
def low(v):
    return lax.optimization_barrier(v.astype(jnp.bfloat16)).astype(jnp.float32)

@jax.custom_vjp
def low_back(v):
    return v

def low_keep(v):
    return (low(v), None)

def low_pass(kept, grad):
    return (grad,)

def back_keep(v):
    return (v, None)

def back_low(kept, grad):
    return (low(grad),)
low.defvjp(low_keep, low_pass)
low_back.defvjp(back_keep, back_low)

def matmul_hi(left, right):
    return jnp.dot(left, right, precision=lax.Precision.HIGHEST)

def rows_norm(values, gain_col, bias_col):
    centre = values - lax.optimization_barrier(jnp.mean(values, axis=-1, keepdims=True))
    spread = lax.optimization_barrier(jnp.mean(centre * centre, axis=-1, keepdims=True))
    return centre * lax.rsqrt(spread + EPSILON) * gain_col + bias_col

def frame_masks(length_row, frames):
    end_one = length_row[0]
    end_two = end_one + length_row[1]
    end_three = end_two + length_row[2]
    places = jnp.arange(frames, dtype=jnp.int32)
    segment = (places >= end_one).astype(jnp.int32) + (places >= end_two).astype(jnp.int32) + (places >= end_three).astype(jnp.int32)
    valid_rows = (places < end_three).astype(jnp.float32)
    return (segment, valid_rows)

def shifted_rows(values, segment, offset):
    frames = values.shape[0]
    if offset > 0:
        moved_rows = jnp.concatenate([values[offset:], jnp.zeros((offset, values.shape[1]), values.dtype)], axis=0)
        moved_seg = jnp.concatenate([segment[offset:], jnp.full((offset,), -1, jnp.int32)])
    elif offset < 0:
        moved_rows = jnp.concatenate([jnp.zeros((-offset, values.shape[1]), values.dtype), values[:frames + offset]], axis=0)
        moved_seg = jnp.concatenate([jnp.full((-offset,), -1, jnp.int32), segment[:frames + offset]])
    else:
        moved_rows, moved_seg = (values, segment)
    return (moved_rows, moved_seg)

def depthwise(gated_rows, kernel, segment):
    tap_count = kernel.shape[1]
    running = jnp.zeros_like(gated_rows)
    for tap_index in range(tap_count):
        moved_rows, moved_seg = shifted_rows(gated_rows, segment, tap_index - tap_count // 2)
        keep_rows = (moved_seg == segment).astype(jnp.float32)
        running = running + kernel[:, tap_index][None, :] * moved_rows * keep_rows[:, None]
    return running

def glu_conv(front_rows, kernel, segment):
    half_width = kernel.shape[0]
    gated_rows = front_rows[:, :half_width] * jax.nn.sigmoid(front_rows[:, half_width:])
    return depthwise(gated_rows, kernel, segment)

def feed_forward(values, gain_col, bias_col, weight_in, weight_out):
    normed = low(rows_norm(values, gain_col, bias_col))
    before = low_back(matmul_hi(normed, weight_in))
    hidden = low(jax.nn.silu(before))
    return low_back(matmul_hi(hidden, weight_out.T))

def self_attention(values, gain_col, bias_col, weight_qkv, weight_out, rel_bias, segment):
    frames = values.shape[0]
    normed = low(rows_norm(values, gain_col, bias_col))
    packed = low(low_back(matmul_hi(normed, weight_qkv))).reshape(frames, 3, HEADS, HEAD)
    queries = packed[:, 0]
    key_rows = packed[:, 1]
    value_rows = packed[:, 2]
    product = jnp.einsum('qhe,khe->hqk', queries, key_rows, precision=lax.Precision.HIGHEST) * HEAD ** (-0.5)
    places = jnp.arange(frames, dtype=jnp.int32)
    rel_index = jnp.clip(places[None, :] - places[:, None], -REL, REL) + REL
    scores = low_back(product) + jnp.take(rel_bias, rel_index, axis=1)
    same_seg = segment[:, None] == segment[None, :]
    scores = jnp.where(same_seg[None], scores, MASKED)
    attend = low(jax.nn.softmax(scores, axis=-1))
    context = low(low_back(jnp.einsum('hqk,khe->qhe', attend, value_rows, precision=lax.Precision.HIGHEST)))
    return low_back(matmul_hi(context.reshape(frames, HEADS * HEAD), weight_out))

def conv_front(values, gain_col, bias_col, weight_conv, kernel, segment):
    normed = low(rows_norm(values, gain_col, bias_col))
    front_rows = low_back(matmul_hi(normed, weight_conv))
    return glu_conv(front_rows, kernel, segment)

def front_group(group_rows, length_row, weights):
    ffn1_in, ffn1_out, attn_qkv, attn_out, rel_table, conv_in, depth_kernel, conv_out, ffn2_in, ffn2_out, gain_cols, bias_cols = weights
    segment, valid_rows = frame_masks(length_row, FRAMES)
    after_ffn = group_rows + 0.5 * feed_forward(group_rows, gain_cols[:, 0], bias_cols[:, 0], ffn1_in, ffn1_out)
    after_attn = after_ffn + self_attention(after_ffn, gain_cols[:, 1], bias_cols[:, 1], attn_qkv, attn_out, rel_table, segment)
    mixed_rows = conv_front(after_attn, gain_cols[:, 2], bias_cols[:, 2], conv_in, depth_kernel, segment)
    return (after_attn, mixed_rows)

def back_group(after_attn, mixed_rows, length_row, bn_mean, bn_rstd, weights):
    ffn1_in, ffn1_out, attn_qkv, attn_out, rel_table, conv_in, depth_kernel, conv_out, ffn2_in, ffn2_out, gain_cols, bias_cols = weights
    valid_rows = frame_masks(length_row, FRAMES)[1]
    bn_hat = (mixed_rows - bn_mean) * bn_rstd
    bn_out = bn_hat * gain_cols[:, 5] + bias_cols[:, 5]
    after_conv = after_attn + low_back(matmul_hi(low(jax.nn.silu(bn_out)), conv_out))
    after_ffn2 = after_conv + 0.5 * feed_forward(after_conv, gain_cols[:, 3], bias_cols[:, 3], ffn2_in, ffn2_out)
    return valid_rows[:, None] * rows_norm(after_ffn2, gain_cols[:, 4], bias_cols[:, 4])

def valid_of(length_row):
    return frame_masks(length_row, FRAMES)[1]

def reference(inputs, cotangent, lengths, ffn1_in, ffn1_out, attn_qkv, attn_out, rel_table, conv_in, depth_kernel, conv_out, ffn2_in, ffn2_out, gains, biases, inner_biases):
    params = tuple((array_in.astype(jnp.float32) for array_in in (ffn1_in, ffn1_out, attn_qkv, attn_out, rel_table, conv_in, depth_kernel, conv_out, ffn2_in, ffn2_out, gains, biases, inner_biases)))
    front_saved = jax.checkpoint(front_group)
    back_saved = jax.checkpoint(back_group)

    def forward(stream_in, weights):
        outer_cols = weights[11]
        inner_cols = weights[12]
        bias_cols = jnp.concatenate([outer_cols[:, 0:2], inner_cols[:, 0:2], outer_cols[:, 2:3], inner_cols[:, 2:3]], axis=1)
        layer_weights = weights[:11] + (bias_cols,)
        grouped = stream_in.reshape(GROUPS, FRAMES, D)
        start_sums = (jnp.zeros((D,), jnp.float32), jnp.zeros((D,), jnp.float32))

        def front_step(running_sums, scan_item):
            middle_rows, mixed_rows = front_saved(scan_item[0], scan_item[1], layer_weights)
            weighted = valid_of(scan_item[1])[:, None] * mixed_rows
            new_sums = (running_sums[0] + lax.optimization_barrier(jnp.sum(weighted, axis=0)), running_sums[1] + lax.optimization_barrier(jnp.sum(weighted * mixed_rows, axis=0)))
            return (new_sums, (middle_rows, mixed_rows))
        channel_sums, (middles, mix_rows) = lax.scan(front_step, start_sums, (grouped, lengths))
        valid_all = jax.vmap(valid_of)(lengths)
        valid_count = jnp.sum(valid_all)
        bn_mean = channel_sums[0] / valid_count
        bn_var = channel_sums[1] / valid_count - bn_mean * bn_mean
        bn_rstd = lax.rsqrt(bn_var + EPSILON)

        def back_step(scan_item):
            return back_saved(scan_item[0], scan_item[1], scan_item[2], bn_mean, bn_rstd, layer_weights)
        outputs = lax.map(back_step, (middles, mix_rows, lengths))
        return outputs.reshape(GROUPS * FRAMES, D)
    layer_out, pull_back = jax.vjp(forward, inputs.astype(jnp.float32), params)
    grad_in, grad_params = pull_back(cotangent.astype(jnp.float32))
    grad_ffn1_in, grad_ffn1_out, grad_qkv, grad_attn_out, grad_rel, grad_conv_in, grad_kernel, grad_conv_out, grad_ffn2_in, grad_ffn2_out, grad_gains, grad_biases, grad_inner = grad_params
    return (layer_out.astype(jnp.bfloat16), grad_in.astype(jnp.bfloat16), grad_ffn1_in, grad_ffn1_out, grad_qkv, grad_attn_out, grad_rel, grad_conv_in, grad_kernel, grad_conv_out, grad_ffn2_in, grad_ffn2_out, grad_gains, grad_biases, grad_inner)
```

```python
import functools

import jax
import jax.numpy as jnp
from jax import lax
from jax.experimental import pallas as pl
from jax.experimental.pallas import tpu as pltpu
from jax.sharding import PartitionSpec as P

EPSILON = 1e-05
MASKED = -1000000000.0
DOWN_DIMS = (((0,), (0,)), ((), ()))
ACROSS_DIMS = (((1,), (1,)), ((), ()))


def rows_norm(values, gain_col, bias_col):
    centre = values - jnp.mean(values, axis=-1, keepdims=True)
    spread = jnp.mean(centre * centre, axis=-1, keepdims=True)
    return centre * lax.rsqrt(spread + EPSILON) * gain_col + bias_col


def frame_masks(length_row, frames):
    end_one = length_row[0]
    end_two = end_one + length_row[1]
    end_three = end_two + length_row[2]
    places = jnp.arange(frames, dtype=jnp.int32)
    segment = (
        (places >= end_one).astype(jnp.int32)
        + (places >= end_two).astype(jnp.int32)
        + (places >= end_three).astype(jnp.int32)
    )
    valid_rows = (places < end_three).astype(jnp.float32)
    return (segment, valid_rows)


def shifted_rows(values, segment, offset):
    frames = values.shape[0]
    if offset > 0:
        moved_rows = jnp.concatenate(
            [values[offset:], jnp.zeros((offset, values.shape[1]), values.dtype)], axis=0
        )
        moved_seg = jnp.concatenate([segment[offset:], jnp.full((offset,), -1, jnp.int32)])
    elif offset < 0:
        moved_rows = jnp.concatenate(
            [jnp.zeros((-offset, values.shape[1]), values.dtype), values[: frames + offset]], axis=0
        )
        moved_seg = jnp.concatenate(
            [jnp.full((-offset,), -1, jnp.int32), segment[: frames + offset]]
        )
    else:
        moved_rows, moved_seg = (values, segment)
    return (moved_rows, moved_seg)


def depthwise(gated_rows, kernel, segment):
    tap_count = kernel.shape[1]
    running = jnp.zeros_like(gated_rows)
    for tap_index in range(tap_count):
        moved_rows, moved_seg = shifted_rows(gated_rows, segment, tap_index - tap_count // 2)
        keep_rows = (moved_seg == segment).astype(jnp.float32)
        running = running + kernel[:, tap_index][None, :] * moved_rows * keep_rows[:, None]
    return running


def glu_conv(front_rows, kernel, segment):
    half_width = kernel.shape[0]
    gated_rows = front_rows[:, :half_width] * jax.nn.sigmoid(front_rows[:, half_width:])
    return depthwise(gated_rows, kernel, segment)


def project(left, right):
    return jnp.dot(left, right, preferred_element_type=jnp.float32)


def project_back(left, right):
    return lax.dot_general(left, right, ACROSS_DIMS, preferred_element_type=jnp.float32)


def weight_grad(left, right):
    return lax.dot_general(left, right, DOWN_DIMS, preferred_element_type=jnp.float32)


def norm_back(grad_out, values, gain_col, bias_col):
    _, pull_back = jax.vjp(rows_norm, values, gain_col, bias_col)
    return pull_back(grad_out)


def silu_back(grad_out, before):
    _, pull_back = jax.vjp(jax.nn.silu, before)
    return pull_back(grad_out)[0]


def pair_kernel(axes, x_ref, o_ref, slots, send_sems, recv_sems):
    partners = []
    for name, size in axes:
        me = lax.axis_index(name)
        bit = 1
        while bit < size:
            partners.append({name: me + bit * (1 - 2 * ((me // bit) % 2))})
            bit *= 2
    barrier = pltpu.get_barrier_semaphore()
    for partner in partners:
        pl.semaphore_signal(barrier, inc=1, device_id=partner, device_id_type=pl.DeviceIdType.MESH)
    pl.semaphore_wait(barrier, len(partners))
    o_ref[...] = x_ref[...]
    for stage, partner in enumerate(partners):
        copy = pltpu.make_async_remote_copy(
            src_ref=o_ref,
            dst_ref=slots.at[stage],
            send_sem=send_sems.at[stage],
            recv_sem=recv_sems.at[stage],
            device_id=partner,
            device_id_type=pl.DeviceIdType.MESH,
        )
        copy.start()
        copy.wait()
        o_ref[...] += slots[stage]


def sum_everywhere(values, axes, collective_id):
    stages = sum(size.bit_length() - 1 for _, size in axes)
    if any(size & (size - 1) for _, size in axes):
        return lax.psum(values, tuple(name for name, _ in axes))
    return pl.pallas_call(
        functools.partial(pair_kernel, axes),
        out_shape=jax.ShapeDtypeStruct(values.shape, values.dtype),
        in_specs=[pl.BlockSpec(memory_space=pltpu.VMEM)],
        out_specs=pl.BlockSpec(memory_space=pltpu.VMEM),
        scratch_shapes=[
            pltpu.VMEM((stages,) + values.shape, values.dtype),
            pltpu.SemaphoreType.DMA((stages,)),
            pltpu.SemaphoreType.DMA((stages,)),
        ],
        compiler_params=pltpu.CompilerParams(collective_id=collective_id, has_side_effects=True),
    )(values)


class Rows:
    def __init__(self, size):
        self.size = size
        self.me = lax.axis_index("fsdp")

    def owner(self, step):
        return lax.rem(self.me + step, self.size)

    def shift(self, values, step):
        return lax.ppermute(
            values, "fsdp", [(j, (j - step) % self.size) for j in range(self.size)]
        )

    def gather(self, block):
        return [(self.me, block)] + [
            (self.owner(step), self.shift(block, step)) for step in range(1, self.size)
        ]

    def columns(self, values, owner):
        width = values.shape[1] // self.size
        return lax.dynamic_slice_in_dim(values, owner * width, width, axis=1)

    def order(self, parts, axis):
        if self.size == 1:
            return parts[0]
        if self.size == 2:
            first = self.me == 0
            return jnp.concatenate(
                [jnp.where(first, parts[0], parts[1]), jnp.where(first, parts[1], parts[0])],
                axis=axis,
            )
        width = parts[0].shape[axis]
        twice = jnp.concatenate(parts + parts, axis=axis)
        start = lax.rem(self.size - self.me, self.size) * width
        return lax.dynamic_slice_in_dim(twice, start, width * self.size, axis=axis)

    def times(self, values, blocks):
        return functools.reduce(
            jnp.add, [project(self.columns(values, owner), block) for owner, block in blocks]
        )

    def times_back(self, values, blocks):
        return self.order([project_back(values, block) for _, block in blocks], 1)

    def all_frames(self, values):
        return jnp.concatenate(
            [values] + [self.shift(values, step) for step in range(1, self.size)], axis=0
        )

    def all_frames_own_columns(self, values):
        return jnp.concatenate(
            [self.columns(values, self.me)]
            + [
                self.shift(self.columns(values, self.owner(self.size - step)), step)
                for step in range(1, self.size)
            ],
            axis=0,
        )


def cube_kernel(plan, *refs):
    me = lax.axis_index("dp")
    arrays = [len(columns) for _, columns, _ in plan]
    inputs, refs = refs[: sum(arrays)], refs[sum(arrays) :]
    outputs, refs = refs[: sum(arrays)], refs[sum(arrays) :]
    kinds, all_bits, first = [], [], 0
    for bits, columns, chunk in plan:
        whole, result, refs = refs[0], refs[1], refs[2:]
        sums, refs = refs[: len(bits)], refs[len(bits) :]
        send_sems, recv_sems, refs = refs[0], refs[1], refs[2:]
        rows = whole.shape[0]
        uppers = [lax.rem(me // bit, 2) for bit in bits]
        partners = [me + bit * (1 - 2 * upper) for bit, upper in zip(bits, uppers)]
        starts, start = [], 0
        for step, upper in enumerate(uppers):
            start = start + upper * (rows >> (step + 1))
            starts.append(start)
        kinds.append(
            dict(
                bits=bits,
                columns=columns,
                chunk=chunk,
                count=sum(columns) // chunk,
                whole=whole,
                result=result,
                sums=sums,
                send=send_sems,
                recv=recv_sems,
                rows=rows,
                uppers=uppers,
                partners=partners,
                starts=starts,
                first=first,
            )
        )
        first += len(columns)
        all_bits += [bit for bit in bits if bit not in all_bits]
    io_sems = refs[0]

    def loads(kind):
        offset = 0
        for place, columns in enumerate(kind["columns"]):
            index = kind["first"] + place
            yield pltpu.make_async_copy(
                inputs[index],
                kind["whole"].at[:, pl.ds(offset, columns)],
                io_sems.at[index],
            )
            offset += columns

    def stores(kind):
        offset = 0
        for place, columns in enumerate(kind["columns"]):
            index = kind["first"] + place
            yield pltpu.make_async_copy(
                kind["result"].at[:, pl.ds(offset, columns)],
                outputs[index],
                io_sems.at[index],
            )
            offset += columns

    for kind in kinds:
        for copy in loads(kind):
            copy.start()
    barrier = pltpu.get_barrier_semaphore()
    for bit in all_bits:
        partner = me + bit * (1 - 2 * lax.rem(me // bit, 2))
        pl.semaphore_signal(
            barrier, inc=1, device_id={"dp": partner}, device_id_type=pl.DeviceIdType.MESH
        )
    pl.semaphore_wait(barrier, len(all_bits))
    for kind in kinds:
        for copy in loads(kind):
            copy.wait()

    def window(kind, index):
        return pl.ds(pl.multiple_of(index * kind["chunk"], kind["chunk"]), kind["chunk"])

    def halving(kind, step, index):
        rows = kind["rows"] >> (step + 1)
        source = kind["whole"] if step == 0 else kind["sums"][step - 1]
        given = pl.multiple_of((1 - kind["uppers"][step]) * rows, rows)
        return pltpu.make_async_remote_copy(
            src_ref=source.at[pl.ds(given, rows), window(kind, index)],
            dst_ref=kind["sums"][step].at[:, window(kind, index)],
            send_sem=kind["send"].at[step, index],
            recv_sem=kind["recv"].at[step, index],
            device_id={"dp": kind["partners"][step]},
            device_id_type=pl.DeviceIdType.MESH,
        )

    def doubling(kind, step, index):
        rows = kind["rows"] >> (step + 1)
        start = pl.multiple_of(kind["starts"][step], rows)
        block = kind["result"].at[pl.ds(start, rows), window(kind, index)]
        slot = 2 * len(kind["bits"]) - 1 - step
        return pltpu.make_async_remote_copy(
            src_ref=block,
            dst_ref=block,
            send_sem=kind["send"].at[slot, index],
            recv_sem=kind["recv"].at[slot, index],
            device_id={"dp": kind["partners"][step]},
            device_id_type=pl.DeviceIdType.MESH,
        )

    def advance(kind, stage, index):
        depth = len(kind["bits"])
        if stage == 0:
            halving(kind, 0, index).start()
        elif stage <= depth:
            step = stage - 1
            halving(kind, step, index).wait()
            rows = kind["rows"] >> (step + 1)
            source = kind["whole"] if step == 0 else kind["sums"][step - 1]
            kept = pl.multiple_of(kind["uppers"][step] * rows, rows)
            columns = window(kind, index)
            total = (
                source[pl.ds(kept, rows), columns].astype(jnp.float32)
                + kind["sums"][step][:, columns].astype(jnp.float32)
            ).astype(kind["whole"].dtype)
            if stage < depth:
                kind["sums"][step][:, columns] = total
                halving(kind, stage, index).start()
            else:
                start = pl.multiple_of(kind["starts"][step], rows)
                kind["result"][pl.ds(start, rows), columns] = total
                doubling(kind, step, index).start()
        else:
            step = 2 * depth - stage
            doubling(kind, step, index).wait()
            if step > 0:
                doubling(kind, step - 1, index).start()

    last = max(kind["count"] + 2 * len(kind["bits"]) for kind in kinds)

    @pl.loop(0, last)
    def _(tick):
        for stage in range(2 * max(len(kind["bits"]) for kind in kinds) + 1):
            for kind in kinds:
                if stage <= 2 * len(kind["bits"]):

                    @pl.when((tick >= stage) & (tick < stage + kind["count"]))
                    def _(kind=kind, stage=stage):
                        advance(kind, stage, tick - stage)

    for kind in kinds:
        for copy in stores(kind):
            copy.start()
    for kind in kinds:
        for copy in stores(kind):
            copy.wait()


def sum_cube(parts, plan, collective_id):
    flat = [part for kind in parts for part in kind]
    scratch = []
    for kind, (bits, columns, chunk) in zip(parts, plan):
        rows, total = kind[0].shape[0], sum(columns)
        scratch += [pltpu.VMEM((rows, total), kind[0].dtype)] * 2
        scratch += [
            pltpu.VMEM((rows >> (step + 1), total), kind[0].dtype) for step in range(len(bits))
        ]
        scratch += [pltpu.SemaphoreType.DMA((2 * len(bits), total // chunk))] * 2
    scratch.append(pltpu.SemaphoreType.DMA((len(flat),)))
    out = pl.pallas_call(
        functools.partial(cube_kernel, plan),
        out_shape=[jax.ShapeDtypeStruct(part.shape, part.dtype) for part in flat],
        in_specs=[pl.BlockSpec(memory_space=pl.ANY)] * len(flat),
        out_specs=[pl.BlockSpec(memory_space=pl.ANY)] * len(flat),
        scratch_shapes=scratch,
        compiler_params=pltpu.CompilerParams(
            collective_id=collective_id, has_side_effects=True, vmem_limit_bytes=60 * 2**20
        ),
    )(*flat)
    result = []
    for kind in parts:
        result.append(out[: len(kind)])
        out = out[len(kind) :]
    return result


class Groups:
    def __init__(self, size):
        self.size = size
        self.me = lax.axis_index("dp")
        bits = [1 << k for k in range(size.bit_length() - 1)]
        self.plain = size & (size - 1) != 0 or not bits
        self.orders = [
            [bits[k]] + bits[:k] + bits[k + 1 :] for k in (0, min(1, len(bits) - 1), min(2, len(bits) - 1))
        ] if bits else []

    def swap(self, values, bit):
        return lax.ppermute(values, "dp", [(j, j ^ bit) for j in range(self.size)])

    def upper(self, bit):
        return lax.rem(self.me // bit, 2)

    def give(self, kind, pieces):
        if self.plain:
            return None
        bit = self.orders[kind][0]
        return self.product(pieces, 1 - self.upper(bit), 2).astype(jnp.bfloat16)

    def product(self, pieces, part, parts):
        count = pieces[0][0].shape[1] // parts
        products = [
            weight_grad(lax.dynamic_slice_in_dim(left, part * count, count, axis=1), right)
            for left, right in pieces
        ]
        return products[0] if len(products) == 1 else jnp.concatenate(products, axis=1)

    def keep(self, kind, pieces, given):
        if self.plain:
            return self.product(pieces, 0, 1).astype(jnp.bfloat16)
        bit = self.orders[kind][0]
        other = self.swap(given, bit)
        mine = self.product(pieces, self.upper(bit), 2)
        return (mine + other.astype(jnp.float32)).astype(jnp.bfloat16)

    def middle(self, parts, collective_id):
        if self.plain:
            return parts
        plan, fits = [], True
        for order, arrays in zip(self.orders, parts):
            columns = tuple(array.shape[1] for array in arrays)
            blocks = sum(columns) // 128
            chunk = 128 * max([k for k in range(1, blocks + 1) if blocks % k == 0 and blocks // k >= 16], default=1)
            plan.append((tuple(order[1:]), columns, chunk))
            fits &= all(count % 128 == 0 for count in columns) and blocks > 0
            fits &= (arrays[0].shape[0] >> len(order[1:])) % 16 == 0 and len(order) > 1
        if fits:
            return sum_cube(parts, plan, collective_id)
        return [
            [self.rounds(order[1:], array) for array in arrays]
            for order, arrays in zip(self.orders, parts)
        ]

    def rounds(self, bits, total):
        for bit in bits:
            count = total.shape[0] // 2
            given = lax.dynamic_slice_in_dim(total, (1 - self.upper(bit)) * count, count, axis=0)
            mine = lax.dynamic_slice_in_dim(total, self.upper(bit) * count, count, axis=0)
            other = self.swap(given, bit)
            total = (mine.astype(jnp.float32) + other.astype(jnp.float32)).astype(jnp.bfloat16)
        for bit in reversed(bits):
            total = self.double(bit, total)
        return total

    def double(self, bit, total):
        other = self.swap(total, bit)
        low = self.upper(bit) == 0
        return jnp.concatenate(
            [jnp.where(low, total, other), jnp.where(low, other, total)], axis=0
        )

    def gather(self, kind, total):
        if self.plain:
            return lax.psum(total, "dp").astype(jnp.float32)
        return self.double(self.orders[kind][0], total).astype(jnp.float32)


def attn_scores(queries, key_rows, rel_bias, onehot, same_seg, score_scale):
    product = (
        jnp.einsum("qhe,khe->hqk", queries, key_rows, preferred_element_type=jnp.float32)
        * score_scale
    )
    relative = jnp.einsum("hr,rqk->hqk", rel_bias, onehot, precision=lax.Precision.HIGHEST)
    return jnp.where(same_seg[None], product + relative, MASKED)


def attn_core(packed, rel_bias, onehot, same_seg):
    frames = packed.shape[0]
    head_count = rel_bias.shape[0]
    head_size = packed.shape[1] // 3 // head_count
    score_scale = head_size ** (-0.5)
    packed = packed.reshape(frames, 3, head_count, head_size)
    queries = packed[:, 0]
    key_rows = packed[:, 1]
    value_rows = packed[:, 2]
    scores = attn_scores(queries, key_rows, rel_bias, onehot, same_seg, score_scale)
    top_score = jnp.max(scores, axis=-1, keepdims=True)
    log_total = top_score + jnp.log(jnp.sum(jnp.exp(scores - top_score), axis=-1, keepdims=True))
    attend = jnp.exp(scores - log_total).astype(jnp.bfloat16)
    context = jnp.einsum("hqk,khe->qhe", attend, value_rows, preferred_element_type=jnp.float32)
    context = context.astype(jnp.bfloat16).reshape(frames, head_count * head_size)
    return context, (queries, key_rows, value_rows, log_total)


def attn_core_back(grad_context, rel_bias, onehot, same_seg, kept):
    queries, key_rows, value_rows, log_total = kept
    frames, head_count, head_size = queries.shape
    score_scale = head_size ** (-0.5)
    grad_context = grad_context.reshape(frames, head_count, head_size)
    scores = attn_scores(queries, key_rows, rel_bias, onehot, same_seg, score_scale)
    attend = jnp.exp(scores - log_total)
    grad_attend = jnp.einsum(
        "qhe,khe->hqk", grad_context, value_rows, preferred_element_type=jnp.float32
    )
    grad_value = jnp.einsum(
        "hqk,qhe->khe",
        attend.astype(jnp.bfloat16),
        grad_context,
        preferred_element_type=jnp.float32,
    )
    grad_scores = attend * (grad_attend - jnp.sum(grad_attend * attend, axis=-1, keepdims=True))
    grad_rel = jnp.einsum("hqk,rqk->hr", grad_scores, onehot, precision=lax.Precision.HIGHEST)
    scores_low = grad_scores.astype(jnp.bfloat16)
    grad_query = (
        jnp.einsum("hqk,khe->qhe", scores_low, key_rows, preferred_element_type=jnp.float32)
        * score_scale
    )
    grad_key = (
        jnp.einsum("hqk,qhe->khe", scores_low, queries, preferred_element_type=jnp.float32)
        * score_scale
    )
    grad_packed = jnp.stack([grad_query, grad_key, grad_value], axis=1)
    grad_packed = grad_packed.reshape(frames, 3 * head_count * head_size).astype(jnp.bfloat16)
    return grad_packed, grad_rel


def per_device(
    sizes,
    inputs,
    cotangent,
    lengths,
    ffn1_in,
    ffn1_out,
    attn_qkv,
    attn_out,
    rel_table,
    conv_in,
    depth_kernel,
    conv_out,
    ffn2_in,
    ffn2_out,
    gains,
    biases,
    inner_biases,
):
    dp_size, fsdp_size = sizes
    axes = (("fsdp", fsdp_size), ("dp", dp_size))
    rows = Rows(fsdp_size)
    groups = Groups(dp_size)
    frames, width = inputs.shape
    taps = depth_kernel.shape[1]
    segment, valid_rows = frame_masks(lengths[0], frames)
    valid_col = valid_rows[:, None]

    small = jnp.concatenate([gains, biases, inner_biases, depth_kernel], axis=1).T
    small = rows.order([block for _, block in rows.gather(small)], 1).astype(jnp.float32)
    rel_bias = rows.order([block for _, block in rows.gather(rel_table)], 0).astype(jnp.float32)
    w_ffn1_in = rows.gather(ffn1_in)
    w_ffn1_out = rows.gather(ffn1_out)
    w_qkv = rows.gather(attn_qkv)
    w_attn_out = rows.gather(attn_out)
    w_conv_in = rows.gather(conv_in)
    w_conv_out = rows.gather(conv_out)
    w_ffn2_in = rows.gather(ffn2_in)
    w_ffn2_out = rows.gather(ffn2_out)
    gain = [small[k] for k in range(6)]
    bias = [small[k] for k in (6, 7, 9, 10, 8, 11)]
    kernel = small[12 : 12 + taps].T

    places = jnp.arange(frames, dtype=jnp.int32)
    reach = (rel_bias.shape[1] - 1) // 2
    rel_index = jnp.clip(places[None, :] - places[:, None], -reach, reach) + reach
    onehot = (
        rel_index[None] == jnp.arange(rel_bias.shape[1], dtype=jnp.int32)[:, None, None]
    ).astype(jnp.float32)
    same_seg = segment[:, None] == segment[None, :]

    stream_in = inputs.astype(jnp.float32)
    normed_one = rows_norm(stream_in, gain[0], bias[0]).astype(jnp.bfloat16)
    before_one = rows.times(normed_one, w_ffn1_in)
    hidden_one = jax.nn.silu(before_one).astype(jnp.bfloat16)
    after_ffn = stream_in + 0.5 * rows.times_back(hidden_one, w_ffn1_out)

    normed_attn = rows_norm(after_ffn, gain[1], bias[1]).astype(jnp.bfloat16)
    packed = rows.times(normed_attn, w_qkv).astype(jnp.bfloat16)
    context, kept_attn = attn_core(packed, rel_bias, onehot, same_seg)
    after_attn = after_ffn + rows.times(context, w_attn_out)

    normed_conv = rows_norm(after_attn, gain[2], bias[2]).astype(jnp.bfloat16)
    front_rows = rows.times(normed_conv, w_conv_in)
    mixed_rows = glu_conv(front_rows, kernel, segment)
    weighted = valid_col * mixed_rows
    totals = sum_everywhere(
        jnp.stack(
            [
                jnp.sum(weighted, axis=0),
                jnp.sum(weighted * mixed_rows, axis=0),
                jnp.full((width,), jnp.sum(valid_rows)),
            ]
            + [jnp.zeros((width,), jnp.float32)] * 5
        ),
        axes,
        0,
    )
    valid_count = totals[2]
    bn_mean = totals[0] / valid_count
    bn_var = totals[1] / valid_count - bn_mean * bn_mean
    bn_rstd = lax.rsqrt(bn_var + EPSILON)
    bn_hat = (mixed_rows - bn_mean) * bn_rstd
    bn_out = bn_hat * gain[5] + bias[5]
    swish_low = jax.nn.silu(bn_out).astype(jnp.bfloat16)
    after_conv = after_attn + rows.times(swish_low, w_conv_out)

    normed_two = rows_norm(after_conv, gain[3], bias[3]).astype(jnp.bfloat16)
    before_two = rows.times(normed_two, w_ffn2_in)
    hidden_two = jax.nn.silu(before_two).astype(jnp.bfloat16)
    after_ffn2 = after_conv + 0.5 * rows.times_back(hidden_two, w_ffn2_out)
    layer_out = (valid_col * rows_norm(after_ffn2, gain[4], bias[4])).astype(jnp.bfloat16)

    grad_final = valid_col * cotangent.astype(jnp.float32)
    grad_after_ffn2, grad_gain_final, grad_bias_final = norm_back(
        grad_final, after_ffn2, gain[4], bias[4]
    )
    low_two = (0.5 * grad_after_ffn2).astype(jnp.bfloat16)
    left_out = rows.all_frames_own_columns(low_two)
    right_out = rows.all_frames(hidden_two)
    main = right_out.shape[1] * 3 // 4
    two_a = [(left_out, right_out[:, :main])]
    give_two_a = groups.give(0, two_a)
    grad_before = silu_back(rows.times(low_two, w_ffn2_out), before_two).astype(jnp.bfloat16)
    left_in = rows.all_frames_own_columns(normed_two)
    right_in = rows.all_frames(grad_before)
    two_b = [(left_in, right_in[:, :main])]
    give_two_b = groups.give(1, two_b)
    two_c = [(left_out, right_out[:, main:]), (left_in, right_in[:, main:])]
    give_two_c = groups.give(2, two_c)
    branch_grad, grad_gain_two, grad_bias_two = norm_back(
        rows.times_back(grad_before, w_ffn2_in), after_conv, gain[3], bias[3]
    )
    grad_after_conv = grad_after_ffn2 + branch_grad
    grad_after_conv, give_two_a, give_two_b, give_two_c = lax.optimization_barrier(
        (grad_after_conv, give_two_a, give_two_b, give_two_c)
    )

    conv_low = grad_after_conv.astype(jnp.bfloat16)
    conv_c = [(rows.all_frames_own_columns(swish_low), rows.all_frames(conv_low))]
    give_conv_c = groups.give(2, conv_c)
    grad_bn_out = silu_back(rows.times_back(conv_low, w_conv_out), bn_out)
    grad_gain_bn = jnp.sum(grad_bn_out * bn_hat, axis=0)
    grad_bias_bn = jnp.sum(grad_bn_out, axis=0)
    grad_hat = grad_bn_out * gain[5]
    back_sums = sum_everywhere(
        jnp.stack(
            [jnp.sum(grad_hat, axis=0), jnp.sum(grad_hat * bn_hat, axis=0)]
            + [jnp.zeros((width,), jnp.float32)] * 6
        ),
        axes,
        1,
    )
    grad_var = -0.5 * bn_rstd * bn_rstd * back_sums[1]
    grad_mean = -bn_rstd * back_sums[0] - 2.0 * bn_mean * grad_var
    grad_mixed = (
        grad_hat * bn_rstd + valid_col * (grad_mean + 2.0 * mixed_rows * grad_var) / valid_count
    )

    def conv_local(front_in, kernel_in):
        return glu_conv(front_in, kernel_in, segment)

    _, pull_back = jax.vjp(conv_local, front_rows, kernel)
    grad_front, grad_kernel = pull_back(grad_mixed)
    front_low = grad_front.astype(jnp.bfloat16)
    left_conv = rows.all_frames_own_columns(normed_conv)
    right_conv = rows.all_frames(front_low)
    conv_a = [(left_conv, right_conv[:, :width])]
    give_conv_a = groups.give(0, conv_a)
    conv_b = [(left_conv, right_conv[:, width:])]
    give_conv_b = groups.give(1, conv_b)
    branch_grad, grad_gain_conv, grad_bias_conv = norm_back(
        rows.times_back(front_low, w_conv_in), after_attn, gain[2], bias[2]
    )
    grad_after_attn = grad_after_conv + branch_grad
    grad_after_attn, give_conv_a, give_conv_b, give_conv_c = lax.optimization_barrier(
        (grad_after_attn, give_conv_a, give_conv_b, give_conv_c)
    )

    attn_low = grad_after_attn.astype(jnp.bfloat16)
    attn_c = [(rows.all_frames_own_columns(context), rows.all_frames(attn_low))]
    give_attn_c = groups.give(2, attn_c)
    grad_context = rows.times_back(attn_low, w_attn_out).astype(jnp.bfloat16)
    grad_packed, grad_rel = attn_core_back(grad_context, rel_bias, onehot, same_seg, kept_attn)
    left_qkv = rows.all_frames_own_columns(normed_attn)
    right_qkv = rows.all_frames(grad_packed)
    half = right_qkv.shape[1] // 2
    attn_a = [(left_qkv, right_qkv[:, :half])]
    give_attn_a = groups.give(0, attn_a)
    attn_b = [(left_qkv, right_qkv[:, half:])]
    give_attn_b = groups.give(1, attn_b)
    branch_grad, grad_gain_attn, grad_bias_attn = norm_back(
        rows.times_back(grad_packed, w_qkv), after_ffn, gain[1], bias[1]
    )
    grad_after_ffn = grad_after_attn + branch_grad
    grad_after_ffn, give_attn_a, give_attn_b, give_attn_c = lax.optimization_barrier(
        (grad_after_ffn, give_attn_a, give_attn_b, give_attn_c)
    )

    low_one = (0.5 * grad_after_ffn).astype(jnp.bfloat16)
    left_out = rows.all_frames_own_columns(low_one)
    right_out = rows.all_frames(hidden_one)
    one_a = [(left_out, right_out[:, :main])]
    give_one_a = groups.give(0, one_a)
    grad_before = silu_back(rows.times(low_one, w_ffn1_out), before_one).astype(jnp.bfloat16)
    left_in = rows.all_frames_own_columns(normed_one)
    right_in = rows.all_frames(grad_before)
    one_b = [(left_in, right_in[:, :main])]
    give_one_b = groups.give(1, one_b)
    one_c = [(left_out, right_out[:, main:]), (left_in, right_in[:, main:])]
    give_one_c = groups.give(2, one_c)
    branch_grad, grad_gain_one, grad_bias_one = norm_back(
        rows.times_back(grad_before, w_ffn1_in), stream_in, gain[0], bias[0]
    )
    input_grad = (grad_after_ffn + branch_grad).astype(jnp.bfloat16)

    lines = [
        grad_gain_one,
        grad_gain_attn,
        grad_gain_conv,
        grad_gain_two,
        grad_gain_final,
        grad_gain_bn,
        grad_bias_one,
        grad_bias_attn,
        grad_bias_final,
        grad_bias_conv,
        grad_bias_two,
        grad_bias_bn,
    ] + [grad_kernel[:, k] for k in range(taps)]
    flat_rel = grad_rel.reshape(-1)
    rel_lines = -(-flat_rel.shape[0] // width)
    flat_rel = jnp.pad(flat_rel, (0, rel_lines * width - flat_rel.shape[0]))
    count = len(lines) + rel_lines
    sums = jnp.concatenate(
        [jnp.stack(lines), flat_rel.reshape(rel_lines, width)]
        + ([jnp.zeros((-count % 8, width), jnp.float32)] if count % 8 else [])
    )
    sums = sum_everywhere(sums, axes, 2)
    own = lax.dynamic_slice_in_dim(
        sums[: len(lines)], rows.me * gains.shape[0], gains.shape[0], axis=1
    )
    rel_sum = sums[len(lines) : count].reshape(-1)[: grad_rel.size].reshape(grad_rel.shape)
    rel_sum = lax.dynamic_slice_in_dim(
        rel_sum, rows.me * rel_table.shape[0], rel_table.shape[0], axis=0
    )

    middle = groups.middle(
        [
            [
                groups.keep(0, two_a, give_two_a),
                groups.keep(0, conv_a, give_conv_a),
                groups.keep(0, attn_a, give_attn_a),
                groups.keep(0, one_a, give_one_a),
            ],
            [
                groups.keep(1, two_b, give_two_b),
                groups.keep(1, conv_b, give_conv_b),
                groups.keep(1, attn_b, give_attn_b),
                groups.keep(1, one_b, give_one_b),
            ],
            [
                groups.keep(2, two_c, give_two_c),
                groups.keep(2, conv_c, give_conv_c),
                groups.keep(2, attn_c, give_attn_c),
                groups.keep(2, one_c, give_one_c),
            ],
        ],
        3,
    )
    (two_a, conv_a, attn_a, one_a), (two_b, conv_b, attn_b, one_b), (two_c, conv_c, attn_c, one_c) = [
        [groups.gather(kind, array) for array in arrays] for kind, arrays in enumerate(middle)
    ]
    rest = two_c.shape[1] // 2
    sum_ffn2_out = jnp.concatenate([two_a, two_c[:, :rest]], axis=1)
    sum_ffn2_in = jnp.concatenate([two_b, two_c[:, rest:]], axis=1)
    sum_conv_in = jnp.concatenate([conv_a, conv_b], axis=1)
    sum_conv_out = conv_c
    sum_qkv = jnp.concatenate([attn_a, attn_b], axis=1)
    sum_attn_out = attn_c
    sum_ffn1_out = jnp.concatenate([one_a, one_c[:, :rest]], axis=1)
    sum_ffn1_in = jnp.concatenate([one_b, one_c[:, rest:]], axis=1)
    return (
        layer_out,
        input_grad,
        sum_ffn1_in,
        sum_ffn1_out,
        sum_qkv,
        sum_attn_out,
        rel_sum,
        sum_conv_in,
        own[12 : 12 + taps].T,
        sum_conv_out,
        sum_ffn2_in,
        sum_ffn2_out,
        own[0:6].T,
        own[6:9].T,
        own[9:12].T,
    )


def solution(mesh):
    frame_spec = P(("dp", "fsdp"), None)
    row_spec = P("fsdp", None)
    sizes = (mesh.shape["dp"], mesh.shape["fsdp"])
    return jax.shard_map(
        functools.partial(per_device, sizes),
        mesh=mesh,
        in_specs=(frame_spec,) * 3 + (row_spec,) * 13,
        out_specs=(frame_spec,) * 2 + (row_spec,) * 13,
        check_vma=False,
    )
```

```python
import functools

import jax
import jax.numpy as jnp
from jax import lax
from jax.experimental import pallas as pl
from jax.experimental.pallas import tpu as pltpu
from jax.sharding import PartitionSpec as P

EPSILON = 1e-05
MASKED = -1000000000.0
AHEAD = 4
DOWN_DIMS = (((0,), (0,)), ((), ()))
ACROSS_DIMS = (((1,), (1,)), ((), ()))


def pair_partners(axes):
    partners = []
    for name, size in axes:
        me = lax.axis_index(name)
        bit = 1
        while bit < size:
            partners.append({name: me + bit * (1 - 2 * ((me // bit) % 2))})
            bit *= 2
    return partners


def sum_stages(axes):
    stages = []
    for name, size in axes:
        bits = [1 << k for k in range(size.bit_length() - 1)]
        stages += [(name, bits[k : k + 2]) for k in range(0, len(bits), 2)]
    return stages


def stage_partners(name, bits):
    me = lax.axis_index(name)
    low, count = bits[0], 2 ** len(bits)
    place = lax.rem(me // low, count)
    return place, [{name: me + low * (other - place)} for other in range(count)]


def pair_kernel(axes, modes, *refs):
    refs = list(refs)

    def pick(count):
        picked = refs[:count]
        del refs[:count]
        return picked

    size = dict(axes)["fsdp"]
    (x_ref,), shared, (o_ref,) = pick(1), pick(len(modes)), pick(1)
    outs = [pick(size - 1) for _ in modes]
    slots, send_sems, recv_sems, share_send, share_recv = refs
    stages = [stage_partners(name, bits) for name, bits in sum_stages(axes)]
    near = len([name for name, _ in sum_stages(axes) if name == "fsdp"])
    me = lax.axis_index("fsdp")
    peers = [{"fsdp": lax.rem(me + size - step, size)} for step in range(1, size)]
    barrier = pltpu.get_barrier_semaphore()
    greeted = 0
    for place, devices in stages:
        for other, device in enumerate(devices):

            @pl.when(other != place)
            def _(device=device):
                pl.semaphore_signal(
                    barrier, inc=1, device_id=device, device_id_type=pl.DeviceIdType.MESH
                )

        greeted += len(devices) - 1
    if modes and size > 4:
        for peer in peers:
            pl.semaphore_signal(barrier, inc=1, device_id=peer, device_id_type=pl.DeviceIdType.MESH)
        greeted += size - 1
    pl.semaphore_wait(barrier, greeted)
    copies = []
    for index, (mode, source) in enumerate(zip(modes, shared)):
        for step, peer in enumerate(peers):
            if mode == "columns":
                width = source.shape[1] // size
                start = pl.multiple_of(peer["fsdp"] * width, width)
                source_now = source.at[:, pl.ds(start, width)]
            else:
                source_now = source
            copies.append(
                pltpu.make_async_remote_copy(
                    src_ref=source_now,
                    dst_ref=outs[index][step],
                    send_sem=share_send.at[index, step],
                    recv_sem=share_recv.at[index, step],
                    device_id=peer,
                    device_id_type=pl.DeviceIdType.MESH,
                )
            )
    o_ref[...] = x_ref[...]
    started = False
    for stage, (place, devices) in enumerate(stages):

        def exchange(other, device, stage=stage, place=place):
            return pltpu.make_async_remote_copy(
                src_ref=o_ref,
                dst_ref=slots.at[stage, place],
                send_sem=send_sems.at[stage, other],
                recv_sem=recv_sems.at[stage, place],
                device_id=device,
                device_id_type=pl.DeviceIdType.MESH,
            )

        def arrival(other, device, stage=stage):
            return pltpu.make_async_remote_copy(
                src_ref=o_ref,
                dst_ref=slots.at[stage, other],
                send_sem=send_sems.at[stage, other],
                recv_sem=recv_sems.at[stage, other],
                device_id=device,
                device_id_type=pl.DeviceIdType.MESH,
            )

        for other, device in enumerate(devices):
            pl.when(other != place)(exchange(other, device).start)
        if not started and stage + 1 >= near:
            started = True
            for copy in copies:
                copy.start()
        for other, device in enumerate(devices):
            pl.when(other != place)(arrival(other, device).wait)
        slots[stage, pl.ds(place, 1)] = o_ref[...][None]
        total = slots[stage, 0]
        for other in range(1, len(devices)):
            total += slots[stage, other]
        o_ref[...] = total
    for copy in copies:
        copy.wait()


def sum_and_share(rows, axes, values, shared, collective_id):
    size = dict(axes)["fsdp"]
    stages = len(sum_stages(axes))
    if any(count & (count - 1) for _, count in axes) or stages == 0:
        total = lax.psum(values, tuple(name for name, _ in axes))
        return total, [
            (rows.all_frames if mode == "all" else rows.all_frames_own_columns)(array)[1:]
            for array, mode in shared
        ]
    shapes = [
        array.shape if mode == "all" else (array.shape[0], array.shape[1] // size)
        for array, mode in shared
    ]
    out = pl.pallas_call(
        functools.partial(pair_kernel, axes, [mode for _, mode in shared]),
        out_shape=[jax.ShapeDtypeStruct(values.shape, values.dtype)]
        + [
            jax.ShapeDtypeStruct(shape, array.dtype)
            for shape, (array, _) in zip(shapes, shared)
            for _ in range(size - 1)
        ],
        in_specs=[pl.BlockSpec(memory_space=pltpu.VMEM)]
        + [pl.BlockSpec(memory_space=pl.ANY)] * len(shared),
        out_specs=[pl.BlockSpec(memory_space=pltpu.VMEM)]
        + [pl.BlockSpec(memory_space=pl.ANY)] * (len(shared) * (size - 1)),
        scratch_shapes=[
            pltpu.VMEM((stages, 4) + values.shape, values.dtype),
            pltpu.SemaphoreType.DMA((stages, 4)),
            pltpu.SemaphoreType.DMA((stages, 4)),
            pltpu.SemaphoreType.DMA((max(len(shared), 1), max(size - 1, 1))),
            pltpu.SemaphoreType.DMA((max(len(shared), 1), max(size - 1, 1))),
        ],
        compiler_params=pltpu.CompilerParams(
            collective_id=collective_id, has_side_effects=True, vmem_limit_bytes=60 * 2**20
        ),
    )(values, *[array for array, _ in shared])
    return out[0], [
        out[1 + k * (size - 1) : 1 + (k + 1) * (size - 1)] for k in range(len(shared))
    ]


class Rows:
    def __init__(self, size):
        self.size = size
        self.me = lax.axis_index("fsdp")

    def owner(self, step):
        return lax.rem(self.me + step, self.size)

    def shift(self, values, step):
        return lax.ppermute(
            values, "fsdp", [(j, (j - step) % self.size) for j in range(self.size)]
        )

    def gather(self, block):
        return [(self.me, block)] + [
            (self.owner(step), self.shift(block, step)) for step in range(1, self.size)
        ]

    def columns(self, values, owner):
        width = values.shape[1] // self.size
        return lax.dynamic_slice_in_dim(values, owner * width, width, axis=1)

    def order(self, parts, axis):
        if self.size == 1:
            return parts[0]
        width = parts[0].shape[axis]
        twice = jnp.concatenate(parts + parts, axis=axis)
        start = lax.rem(self.size - self.me, self.size) * width
        return lax.dynamic_slice_in_dim(twice, start, width * self.size, axis=axis)

    def all_frames(self, values):
        return [values] + [self.shift(values, step) for step in range(1, self.size)]

    def all_frames_own_columns(self, values):
        return [self.columns(values, self.me)] + [
            self.shift(self.columns(values, self.owner(self.size - step)), step)
            for step in range(1, self.size)
        ]


def cube_rounds(bits):
    if len(bits) > 2 and bits[-1] == 2 * bits[-2]:
        return tuple(("swap", bit) for bit in bits[:-2]) + (("give", bits[-2]), ("mid", bits[-2]))
    return tuple(("swap", bit) for bit in bits)


def cube_kernel(axes, plan, lines, *refs):
    me = lax.axis_index("dp")
    refs = list(refs)

    def pick(count):
        picked = refs[:count]
        del refs[:count]
        return picked

    arrays = [len(columns) for _, columns, _ in plan]
    inputs, small_refs = pick(2 * sum(arrays)), pick(len(lines))
    outputs, (small_out,) = pick(sum(arrays)), pick(1)
    kinds, first = [], 0
    for rounds, columns, chunk in plan:
        whole, other, result = pick(3)
        sums = pick(len(rounds))
        send_sems, recv_sems = pick(2)
        rows, start, steps = whole.shape[0], 0, []
        for name, bit in rounds:
            step = dict(name=name, rows=rows, before=start)
            if name == "swap":
                step["upper"] = lax.rem(me // bit, 2)
                step["partner"] = me + bit * (1 - 2 * step["upper"])
                step["sends"] = step["takes"] = None
            else:
                place = lax.rem(me // bit, 4)
                inner = (place == 1) | (place == 2)
                if name == "give":
                    step["partner"] = me + bit * (1 - 2 * lax.rem(place, 2))
                    step["sends"], step["takes"] = jnp.logical_not(inner), inner
                else:
                    step["upper"] = place // 2
                    step["partner"] = me + bit * (1 - 2 * step["upper"])
                    step["sends"] = step["takes"] = inner
            if name != "give":
                rows //= 2
                start = start + step["upper"] * rows
            step["after"] = start
            steps.append(step)
        edges = [sum(columns[:k]) for k in range(len(columns) + 1)]
        kinds.append(
            dict(
                steps=steps,
                columns=columns,
                edges=edges,
                chunk=chunk,
                count=edges[-1] // chunk,
                whole=whole,
                other=other,
                result=result,
                sums=sums,
                send=send_sems,
                recv=recv_sems,
                first=first,
            )
        )
        first += len(columns)
    load_sems, store_sems, slots, small_send, small_recv = refs
    partners = pair_partners(axes)

    def loads(kind, place):
        index = kind["first"] + place
        columns = pl.ds(kind["edges"][place], kind["columns"][place])
        return [
            pltpu.make_async_copy(
                inputs[2 * index + term],
                kind[name].at[:, columns],
                load_sems.at[2 * index + term],
            )
            for term, name in enumerate(("whole", "other"))
        ]

    def store(kind, place):
        index = kind["first"] + place
        columns = pl.ds(kind["edges"][place], kind["columns"][place])
        return pltpu.make_async_copy(
            kind["result"].at[:, columns], outputs[index], store_sems.at[index]
        )

    for place in range(max(arrays)):
        for kind in kinds:
            if place < len(kind["columns"]):
                for copy in loads(kind, place):
                    copy.start()
    small_out[...] = jnp.zeros_like(small_out)
    line = 0
    for ref, rows in zip(small_refs, lines):
        for row in rows:
            small_out[line : line + 1, : ref.shape[1]] = ref[row : row + 1, :]
            line += 1
    barrier = pltpu.get_barrier_semaphore()
    lines = sorted({bit for rounds, _, _ in plan for name, bit in rounds if name == "mid"})
    for partner in partners:
        pl.semaphore_signal(barrier, inc=1, device_id=partner, device_id_type=pl.DeviceIdType.MESH)
    if lines:
        (bit,) = lines
        place = lax.rem(me // bit, 4)
        inner = (place == 1) | (place == 2)

        @pl.when(inner)
        def _():
            pl.semaphore_signal(
                barrier,
                inc=1,
                device_id={"dp": me + bit * (1 - 2 * (place // 2))},
                device_id_type=pl.DeviceIdType.MESH,
            )
            pl.semaphore_wait(barrier, len(partners) + 1)

        @pl.when(jnp.logical_not(inner))
        def _():
            pl.semaphore_wait(barrier, len(partners))

    else:
        pl.semaphore_wait(barrier, len(partners))

    def window(kind, index):
        return pl.ds(pl.multiple_of(index * kind["chunk"], kind["chunk"]), kind["chunk"])

    def aligned(start, rows):
        return pl.ds(start if isinstance(start, int) else pl.multiple_of(start, rows), rows)

    def source(kind, number):
        return kind["whole"] if number == 0 else kind["sums"][number - 1]

    def copy_in(kind, number, index):
        step, columns = kind["steps"][number], window(kind, index)
        rows = step["rows"]
        given = pl.ds(0, rows)
        if step["name"] != "give":
            given = aligned((1 - step["upper"]) * (rows // 2), rows // 2)
        return pltpu.make_async_remote_copy(
            src_ref=source(kind, number).at[given, columns],
            dst_ref=kind["sums"][number].at[:, columns],
            send_sem=kind["send"].at[number, index],
            recv_sem=kind["recv"].at[number, index],
            device_id={"dp": step["partner"]},
            device_id_type=pl.DeviceIdType.MESH,
        )

    def copy_out(kind, number, index):
        step = kind["steps"][number]
        rows = step["rows"] if step["name"] == "give" else step["rows"] // 2
        start = step["before"] if step["name"] == "give" else step["after"]
        block = kind["result"].at[aligned(start, rows), window(kind, index)]
        slot = 2 * len(kind["steps"]) - 1 - number
        return pltpu.make_async_remote_copy(
            src_ref=block,
            dst_ref=block,
            send_sem=kind["send"].at[slot, index],
            recv_sem=kind["recv"].at[slot, index],
            device_id={"dp": step["partner"]},
            device_id_type=pl.DeviceIdType.MESH,
        )

    def when(condition, action):
        if condition is None:
            action()
        else:
            pl.when(condition)(action)

    def end_in(kind, number, index):
        step, columns = kind["steps"][number], window(kind, index)
        copy = copy_in(kind, number, index)
        last = number == len(kind["steps"]) - 1

        def add():
            copy.wait_recv()
            rows = step["rows"]
            kept = pl.ds(0, rows)
            if step["name"] != "give":
                rows //= 2
                kept = aligned(step["upper"] * rows, rows)
            total = (
                source(kind, number)[kept, columns].astype(jnp.float32)
                + kind["sums"][number][:, columns].astype(jnp.float32)
            ).astype(kind["whole"].dtype)
            if last:
                kind["result"][aligned(step["after"], rows), columns] = total
            else:
                kind["sums"][number][:, columns] = total

        when(step["sends"], copy.wait_send)
        when(step["takes"], add)

    def advance(kind, stage, index):
        depth = len(kind["steps"])
        if stage == 0:
            for place, edge in enumerate(kind["edges"][:-1]):

                @pl.when(index == edge // kind["chunk"])
                def _(place=place):
                    for copy in loads(kind, place):
                        copy.wait()

            columns = window(kind, index)
            kind["whole"][:, columns] = (
                kind["whole"][:, columns].astype(jnp.float32)
                + kind["other"][:, columns].astype(jnp.float32)
            ).astype(kind["whole"].dtype)
        elif stage <= depth:
            end_in(kind, stage - 1, index)
        else:
            number = 2 * depth - stage
            step = kind["steps"][number]
            copy = copy_out(kind, number, index)
            when(step["takes"], copy.wait_send)
            when(step["sends"], copy.wait_recv)
        if stage < depth:
            when(kind["steps"][stage]["sends"], copy_in(kind, stage, index).start)
        elif stage < 2 * depth:
            number = 2 * depth - 1 - stage
            when(kind["steps"][number]["takes"], copy_out(kind, number, index).start)
        else:
            for place, edge in enumerate(kind["edges"][1:]):

                @pl.when(index == edge // kind["chunk"] - 1)
                def _(place=place):
                    store(kind, place).start()

    def exchange(stage):
        return pltpu.make_async_remote_copy(
            src_ref=small_out,
            dst_ref=slots.at[stage],
            send_sem=small_send.at[stage],
            recv_sem=small_recv.at[stage],
            device_id=partners[stage],
            device_id_type=pl.DeviceIdType.MESH,
        )

    last = max(kind["count"] + 2 * len(kind["steps"]) for kind in kinds)
    last = max(last, len(partners) + 1)

    @pl.loop(0, last)
    def _(tick):
        for stage in range(len(partners) + 1):

            @pl.when(tick == stage)
            def _(stage=stage):
                if stage > 0:
                    exchange(stage - 1).wait()
                    small_out[...] += slots[stage - 1]
                if stage < len(partners):
                    exchange(stage).start()

        for stage in range(2 * max(len(kind["steps"]) for kind in kinds) + 1):
            for kind in kinds:
                if stage <= 2 * len(kind["steps"]):

                    @pl.when((tick >= stage) & (tick < stage + kind["count"]))
                    def _(kind=kind, stage=stage):
                        advance(kind, stage, tick - stage)

    for kind in kinds:
        for place in range(len(kind["columns"])):
            store(kind, place).wait()


def sum_cube(axes, parts, plan, small, lines, width, collective_id):
    shape = (-(-sum(len(rows) for rows in lines) // 8) * 8, width)
    flat = [term for kind in parts for pair in kind for term in pair]
    scratch = []
    for kind, (rounds, columns, chunk) in zip(parts, plan):
        rows, total, dtype = kind[0][0].shape[0], sum(columns), kind[0][0].dtype
        scratch += [pltpu.VMEM((rows, total), dtype)] * 3
        for name, _ in rounds:
            rows = rows if name == "give" else rows // 2
            scratch.append(pltpu.VMEM((rows, total), dtype))
        scratch += [pltpu.SemaphoreType.DMA((2 * len(rounds), total // chunk))] * 2
    stages = sum(size.bit_length() - 1 for _, size in axes)
    scratch += [
        pltpu.SemaphoreType.DMA((len(flat),)),
        pltpu.SemaphoreType.DMA((len(flat) // 2,)),
        pltpu.VMEM((stages,) + shape, jnp.float32),
        pltpu.SemaphoreType.DMA((stages,)),
        pltpu.SemaphoreType.DMA((stages,)),
    ]
    *out, sums = pl.pallas_call(
        functools.partial(cube_kernel, axes, plan, lines),
        out_shape=[jax.ShapeDtypeStruct(own.shape, own.dtype) for kind in parts for own, _ in kind]
        + [jax.ShapeDtypeStruct(shape, jnp.float32)],
        in_specs=[pl.BlockSpec(memory_space=pl.ANY)] * len(flat)
        + [pl.BlockSpec(memory_space=pltpu.VMEM)] * len(small),
        out_specs=[pl.BlockSpec(memory_space=pl.ANY)] * (len(flat) // 2)
        + [pl.BlockSpec(memory_space=pltpu.VMEM)],
        scratch_shapes=scratch,
        compiler_params=pltpu.CompilerParams(
            collective_id=collective_id, has_side_effects=True, vmem_limit_bytes=60 * 2**20
        ),
    )(*flat, *small)
    result = []
    for kind in parts:
        result.append(out[: len(kind)])
        out = out[len(kind) :]
    return result, sums


class Groups:
    def __init__(self, axes):
        self.axes = axes
        self.size = dict(axes)["dp"]
        self.me = lax.axis_index("dp")
        bits = [1 << k for k in range(self.size.bit_length() - 1)]
        self.plain = any(size & (size - 1) for _, size in axes) or not bits
        first, rest = bits[:3], bits[3:]
        self.orders = [[1]] * 4
        if first:
            one, two, three = first[0], first[1 % len(first)], first[2 % len(first)]
            for kind, order in enumerate(
                ((one, two, three), (two, one, three), (three, one, two), (three, two, one))
            ):
                self.orders[kind] = list(dict.fromkeys(order)) + rest

    def swap(self, values, bit):
        return lax.ppermute(values, "dp", [(j, j ^ bit) for j in range(self.size)])

    def upper(self, bit):
        return lax.rem(self.me // bit, 2)

    def in_order(self, bit, mine, other):
        low = self.upper(bit) == 0
        return jnp.concatenate([jnp.where(low, mine, other), jnp.where(low, other, mine)], axis=0)

    def along(self, jobs, call, **arguments):
        bits = [order[0] for order in self.orders]
        lefts = jobs[0][0]
        if self.plain or lefts[0].shape[1] // len(lefts) % 256:
            results, received, _ = call(**arguments)
            pairs = {
                key: (keep, give if self.plain else self.swap(give, bits[key[1]]))
                for key, (give, keep) in halves_plainly(jobs, bits).items()
            }
        else:
            results, received, pairs = call(**arguments, jobs=jobs, bits=bits)
        bundles = {}
        for (bundle, kind), pair in pairs.items():
            bundles.setdefault(bundle, {})[kind] = pair
        return results, received, bundles

    def middle(self, parts, small, lines, width, collective_id):
        if self.plain:
            sums = self.stacked(small, lines, width)
            return parts, lax.psum(sums, tuple(name for name, _ in self.axes))
        plan, fits = [], True
        for order, arrays in zip(self.orders, parts):
            columns = tuple(own.shape[1] for own, _ in arrays)
            blocks = sum(columns) // 128
            chunk = 512 if blocks >= 48 else 256
            plan.append((cube_rounds(order[1:]), columns, chunk))
            fits &= all(count % chunk == 0 for count in columns)
            fits &= (arrays[0][0].shape[0] >> len(order[1:])) % 16 == 0 and len(order) > 1
        if fits:
            return sum_cube(self.axes, parts, plan, small, lines, width, collective_id)
        sums = [
            [self.rounds(order[1:], own, other) for own, other in arrays]
            for order, arrays in zip(self.orders, parts)
        ]
        small = self.stacked(small, lines, width)
        return sums, sum_and_share(None, self.axes, small, [], collective_id)[0]

    def stacked(self, small, lines, width):
        rows = [
            jnp.pad(array[row], (0, width - array.shape[1]))
            for array, picked in zip(small, lines)
            for row in picked
        ]
        return eight_lines(*rows)

    def rounds(self, bits, own, other):
        total = (own.astype(jnp.float32) + other.astype(jnp.float32)).astype(jnp.bfloat16)
        for bit in bits:
            count = total.shape[0] // 2
            given = lax.dynamic_slice_in_dim(total, (1 - self.upper(bit)) * count, count, axis=0)
            mine = lax.dynamic_slice_in_dim(total, self.upper(bit) * count, count, axis=0)
            other = self.swap(given, bit)
            total = (mine.astype(jnp.float32) + other.astype(jnp.float32)).astype(jnp.bfloat16)
        for bit in reversed(bits):
            total = self.in_order(bit, total, self.swap(total, bit))
        return total

    def finish(self, bundle):
        if self.plain:
            return {kind: (self.orders[kind][0], *pair) for kind, pair in bundle.items()}
        return {
            kind: (self.orders[kind][0], total, self.swap(total, self.orders[kind][0]))
            for kind, total in bundle.items()
        }

    def join(self, *parts):
        if self.plain:
            return jnp.concatenate(
                [
                    lax.psum(
                        self.in_order(*halves)[:, first : first + columns].astype(jnp.float32),
                        "dp",
                    )
                    for halves, first, columns in parts
                ],
                axis=1,
            )
        return join([(*halves, first, columns) for halves, first, columns in parts])


class Flow:
    def __init__(self, sources, held, in_sems, results, staged, out_sems, chunks):
        self.sources, self.held, self.in_sems = sources, held, in_sems
        self.results, self.staged, self.out_sems = results, staged, out_sems
        self.chunks = chunks
        self.sent, self.shared = [], []

    def copy_in(self, index, part):
        width = self.chunks[index]
        columns = pl.ds(part * width, width)
        first = sum(
            source.shape[1] // chunk for source, chunk in zip(self.sources[:index], self.chunks)
        )
        return pltpu.make_async_copy(
            self.sources[index].at[:, columns],
            self.held[index].at[:, columns],
            self.in_sems.at[first + part],
        )

    def start(self, order):
        for index, part in order:
            self.copy_in(index, part).start()

    def pulls(self, held, outs, sems, small):
        self.pull_held, self.pull_outs, self.pull_sems, self.pull_small = held, outs, sems, small
        self.pull_slots, self.pulled = {}, []

    def push(self, order):
        me = lax.axis_index("fsdp")
        for own, places in self.pull_small:
            for step, peer in enumerate(self.peers):
                self.push_one(("small", id(places)), 0, step, peer, own, places[step])
        for index, part in order:
            if index in self.pull_held:
                columns = pl.ds(part * self.chunks[index], self.chunks[index])
                for step, peer in enumerate(self.peers):
                    target = self.pull_held[index][step].at[:, columns]
                    source = self.sources[index].at[:, columns]
                    self.push_one(index, part, step, peer, source, target)

    def carry(self, sources, modes, outs, sems):
        for index, (source, mode) in enumerate(zip(sources, modes)):
            for step, peer in enumerate(self.peers):
                given = source
                if mode == "columns":
                    width = source.shape[1] // self.size
                    given = source.at[:, pl.ds(pl.multiple_of(peer * width, width), width)]
                copy = pltpu.make_async_remote_copy(
                    src_ref=given,
                    dst_ref=outs[index][step],
                    send_sem=sems[0].at[index, step],
                    recv_sem=sems[1].at[index, step],
                    device_id={"fsdp": peer},
                    device_id_type=pl.DeviceIdType.MESH,
                )
                copy.start()
                self.shared.append(copy)

    def push_one(self, index, part, step, peer, source, target):
        send_sems, recv_sems, _ = self.pull_sems
        slot = len(self.pull_slots)
        copy = pltpu.make_async_remote_copy(
            src_ref=source,
            dst_ref=target,
            send_sem=send_sems.at[slot],
            recv_sem=recv_sems.at[slot],
            device_id={"fsdp": peer},
            device_id_type=pl.DeviceIdType.MESH,
        )
        self.pull_slots[index, part, step] = (slot, copy)
        copy.start()

    def take_small(self, places):
        for step in range(len(self.peers)):
            self.pull_slots[("small", id(places)), 0, step][1].wait_recv()
        return places

    def take_all(self, index, part=0):
        blocks = [self.take(index, part)]
        width = self.chunks[index]
        columns = pl.ds(part * width, width)
        for step in range(len(self.peers)):
            slot, copy = self.pull_slots[index, part, step]
            copy.wait_recv()
            block = self.pull_held[index][step].at[:, columns]
            blocks.append(block)
            if not self.pull_outs:
                continue
            out = pltpu.make_async_copy(
                block, self.pull_outs[index][step].at[:, columns], self.pull_sems[2].at[slot]
            )
            out.start()
            self.pulled.append(out)
        return blocks

    def held_all(self, index, part):
        columns = pl.ds(part * self.chunks[index], self.chunks[index])
        return [block.at[:, columns] for block in [self.held[index], *self.pull_held[index]]]

    def take(self, index, part=0):
        self.copy_in(index, part).wait()
        width = self.chunks[index]
        return self.held[index].at[:, pl.ds(part * width, width)]

    def put(self, index, columns=None):
        columns = slice(None) if columns is None else columns
        copy = pltpu.make_async_copy(
            self.staged[index].at[:, columns],
            self.results[index].at[:, columns],
            self.out_sems.at[len(self.sent)],
        )
        copy.start()
        self.sent.append(copy)

    def greet(self, shares, outs, sems, size):
        me = lax.axis_index("fsdp")
        self.shares, self.share_outs, self.share_sems, self.size = shares, outs, sems, size
        self.peers = [lax.rem(me + size - step, size) for step in range(1, size)]

    def share(self, index):
        place = list(self.shares).index(index)
        send_sems, recv_sems = self.share_sems
        for step, peer in enumerate(self.peers):
            source = self.staged[index]
            if self.shares[index] == "columns":
                width = source.shape[1] // self.size
                source = source.at[:, pl.ds(pl.multiple_of(peer * width, width), width)]
            copy = pltpu.make_async_remote_copy(
                src_ref=source,
                dst_ref=self.share_outs[place][step],
                send_sem=send_sems.at[place, step],
                recv_sem=recv_sems.at[place, step],
                device_id={"fsdp": peer},
                device_id_type=pl.DeviceIdType.MESH,
            )
            copy.start()
            self.shared.append(copy)

    def finish(self):
        for copy in self.sent + self.shared + self.pulled:
            copy.wait()
        for _, copy in self.pull_slots.values():
            copy.wait_send()


class Grads:
    AHEAD = 6

    def __init__(self, plan, lefts, rights, outs, lefts_held, scratch):
        self.steps, self.bits, self.count, self.tile = plan
        self.lefts, self.rights, self.outs, self.lefts_held = lefts, rights, outs, lefts_held
        self.rights_held, self.staged, *sems = scratch
        self.left_sems, self.right_sems, self.out_sems, self.send_sems, self.recv_sems = sems
        self.frames, self.rows = rights[0][0].shape[0], self.staged.shape[0]
        self.half = self.rows // 2
        self.me = lax.axis_index("dp")

    def partners(self):
        bits = sorted({self.bits[step[3][1]] for step in self.steps})
        return [{"dp": self.me + bit * (1 - 2 * lax.rem(self.me // bit, 2))} for bit in bits]

    def left_in(self, group, place):
        source = self.lefts[group][place]
        return pltpu.make_async_copy(
            source.at[:, own_columns(self.count, 0, self.rows)] if place == 0 else source,
            self.lefts_held[group].at[pl.ds(place * self.frames, self.frames)],
            self.left_sems.at[group, place],
        )

    def right_in(self, index, place):
        _, right, first, _, _ = self.steps[index]
        return pltpu.make_async_copy(
            self.rights[right][place].at[:, pl.ds(first, self.tile)],
            self.rights_held.at[index % self.AHEAD, pl.ds(place * self.frames, self.frames)],
            self.right_sems.at[index, place],
        )

    def halves_out(self, index):
        _, _, _, key, start = self.steps[index]
        bit = self.bits[key[1]]
        upper = lax.rem(self.me // bit, 2)
        source, columns = [
            self.staged.at[
                pl.ds(pl.multiple_of(part * self.half, self.half), self.half),
                pl.ds(index * self.tile, self.tile),
            ]
            for part in (1 - upper, upper)
        ], pl.ds(start, self.tile)
        keep, recv = self.outs[key]
        return (
            pltpu.make_async_remote_copy(
                src_ref=source[0],
                dst_ref=recv.at[:, columns],
                send_sem=self.send_sems.at[index],
                recv_sem=self.recv_sems.at[index],
                device_id={"dp": self.me + bit * (1 - 2 * upper)},
                device_id_type=pl.DeviceIdType.MESH,
            ),
            pltpu.make_async_copy(source[1], keep.at[:, columns], self.out_sems.at[index]),
        )

    def begin(self):
        loaded = set()
        for index in range(min(self.AHEAD, len(self.steps))):
            self.load(index, loaded)
        self.loaded = loaded

    def load(self, index, loaded):
        group = self.steps[index][0]
        for place in range(self.count):
            if group not in loaded:
                self.left_in(group, place).start()
            self.right_in(index, place).start()
        loaded.add(group)

    def run(self, then):
        waited = set()
        for index, step in enumerate(self.steps):
            for place in range(self.count):
                if step[0] not in waited:
                    self.left_in(step[0], place).wait()
                self.right_in(index, place).wait()
            waited.add(step[0])
            right = self.rights_held[index % self.AHEAD]
            product = dot_down(self.lefts_held[step[0]][...], right)
            self.staged[:, pl.ds(index * self.tile, self.tile)] = product.astype(jnp.bfloat16)
            for copy in self.halves_out(index):
                copy.start()
            if index + self.AHEAD < len(self.steps):
                self.load(index + self.AHEAD, self.loaded)
            if index == max(len(self.steps) - self.AHEAD - 1, 0):
                then()

    def finish(self):
        for index in range(len(self.steps)):
            for copy in self.halves_out(index):
                copy.wait()


def gradient_plan(jobs, tile, spread):
    lefts, rights, steps, totals = [], [], [], {}
    for job_lefts, job_rights, first, columns, key in jobs:
        for known, group in ((lefts, job_lefts), (rights, job_rights)):
            if not any(group is other for other in known):
                known.append(group)
        left = [group is job_lefts for group in lefts].index(True)
        right = [group is job_rights for group in rights].index(True)
        for start in range(0, columns, tile):
            steps.append((left, right, first + start, key, totals.setdefault(key, 0)))
            totals[key] += tile
    turns = {key: 0 for key in totals}
    ranks = []
    for step in steps:
        turns[step[3]] += 1
        ranks.append((turns[step[3]] - 0.5) / (totals[step[3]] // tile))
    if spread:
        steps = [steps[k] for k in sorted(range(len(steps)), key=lambda k: ranks[k])]
    return lefts, rights, steps, totals


def fused(
    body,
    small,
    large,
    results,
    order=None,
    scratch=(),
    shares=None,
    size=1,
    collective_id=None,
    jobs=(),
    bits=(),
    pulls=(),
    small_pulls=(),
    carried=(),
    pulls_stay=False,
    spread=False,
):
    shares = {} if shares is None or size == 1 else shares
    chunks = [width for _, width in large]
    parts = [array.shape[1] // width for array, width in large]
    if order is None:
        order = [(index, part) for index, count in enumerate(parts) for part in range(count)]
    share_shapes = [
        (shape if mode == "all" else (shape[0], shape[1] // size), dtype)
        for (shape, dtype), mode in ((results[index], mode) for index, mode in shares.items())
        for _ in range(size - 1)
    ]
    pulls = list(pulls) if size > 1 else []
    pull_shapes = [
        (large[index][0].shape, large[index][0].dtype) for index in pulls for _ in range(size - 1)
    ]
    carried = list(carried) if size > 1 else []
    carry_shapes = [
        (array.shape if mode == "all" else (array.shape[0], array.shape[1] // size), array.dtype)
        for array, mode in carried
        for _ in range(size - 1)
    ]
    pull_count = (sum(parts[index] for index in pulls) + len(small_pulls)) * (size - 1)
    tile = 512
    lefts, rights, steps, totals = gradient_plan(jobs, tile, spread)
    flat = [array for group in lefts + rights for array in group]
    half_shapes, grad_scratch = [], []
    if jobs:
        count, frames = len(lefts[0]), lefts[0][0].shape[0]
        rows = lefts[0][0].shape[1] // count
        half_shapes = [
            ((rows // 2, columns), jnp.bfloat16) for columns in totals.values() for _ in range(2)
        ]
        grad_scratch = [pltpu.VMEM((count * frames, rows), jnp.bfloat16) for _ in lefts] + [
            pltpu.VMEM((Grads.AHEAD, count * frames, tile), jnp.bfloat16),
            pltpu.VMEM((rows, len(steps) * tile), jnp.bfloat16),
            pltpu.SemaphoreType.DMA((len(lefts), count)),
            pltpu.SemaphoreType.DMA((len(steps), count)),
        ] + [pltpu.SemaphoreType.DMA((len(steps),))] * 3

    def kernel(*refs):
        refs = list(refs)

        def pick(count):
            picked = refs[:count]
            del refs[:count]
            return picked

        small_refs, sources = pick(len(small)), pick(len(large))
        left_refs, right_refs = [pick(len(group)) for group in lefts], [
            pick(len(group)) for group in rights
        ]
        carry_refs = pick(len(carried))
        outs = pick(len(results))
        share_outs = [pick(size - 1) for _ in shares]
        half_outs = {key: pick(2) for key in totals}
        pull_outs = {} if pulls_stay else {index: pick(size - 1) for index in pulls}
        carry_outs = [pick(size - 1) for _ in carried]
        held, staged, rest = pick(len(large)), pick(len(results)), pick(len(scratch))
        in_sems, out_sems = pick(2)
        share_sems = pick(2) if shares else []
        pull_held = {index: pick(size - 1) for index in pulls}
        pull_small = [(small_refs[index], pick(size - 1)) for index in small_pulls]
        pull_sems = pick(3) if pull_count else []
        carry_sems = pick(2) if carried else []
        flow = Flow(sources, held, in_sems, outs, staged, out_sems, chunks)
        greeted = []
        if jobs:
            plan = (steps, bits, len(lefts[0]), tile)
            grads = Grads(plan, left_refs, right_refs, half_outs, pick(len(lefts)), refs)
            grads.begin()
            greeted = grads.partners()
        flow.greet(shares, share_outs, share_sems, size)
        flow.pulls(pull_held, pull_outs, pull_sems, pull_small)
        if pull_count:
            flow.start(order)
        if shares or pull_count or carried:
            greeted += [{"fsdp": peer} for peer in flow.peers]
        if greeted:
            barrier = pltpu.get_barrier_semaphore()
            for device in greeted:
                pl.semaphore_signal(
                    barrier, inc=1, device_id=device, device_id_type=pl.DeviceIdType.MESH
                )
            pl.semaphore_wait(barrier, len(greeted))
        if carried:
            modes = [mode for _, mode in carried]
            flow.carry(carry_refs, modes, carry_outs, carry_sems)
        if jobs:
            grads.run(functools.partial(flow.start, order))
        elif pull_count:
            flow.push(order)
        else:
            flow.start(order)
        if body is not None:
            body(flow, small_refs, rest)
        flow.finish()
        if jobs:
            grads.finish()

    semaphores = [
        pltpu.SemaphoreType.DMA((max(sum(parts), 1),)),
        pltpu.SemaphoreType.DMA((64,)),
    ]
    params = dict(vmem_limit_bytes=60 * 2**20)
    if shares:
        semaphores += [pltpu.SemaphoreType.DMA((len(shares), size - 1))] * 2
    pull_scratch = []
    if pull_count:
        pull_scratch = [pltpu.VMEM(shape, dtype) for shape, dtype in pull_shapes] + [
            pltpu.VMEM(small[index].shape, small[index].dtype)
            for index in small_pulls
            for _ in range(size - 1)
        ]
        pull_scratch += [pltpu.SemaphoreType.DMA((pull_count,))] * 3
    if carried:
        pull_scratch += [pltpu.SemaphoreType.DMA((len(carried), size - 1))] * 2
    if shares or jobs or pull_count or carried:
        params.update(collective_id=collective_id, has_side_effects=True)
    pull_results = [] if pulls_stay else pull_shapes
    shapes = results + share_shapes + half_shapes + pull_results + carry_shapes
    out = pl.pallas_call(
        kernel,
        out_shape=[jax.ShapeDtypeStruct(shape, dtype) for shape, dtype in shapes],
        in_specs=[
            pl.BlockSpec(memory_space=pltpu.SMEM if array.dtype == jnp.int32 else pltpu.VMEM)
            for array in small
        ]
        + [pl.BlockSpec(memory_space=pl.ANY)] * (len(large) + len(flat) + len(carried)),
        out_specs=[pl.BlockSpec(memory_space=pl.ANY)] * len(shapes),
        scratch_shapes=[pltpu.VMEM(array.shape, array.dtype) for array, _ in large]
        + [pltpu.VMEM(shape, dtype) for shape, dtype in results]
        + list(scratch)
        + semaphores
        + pull_scratch
        + grad_scratch,
        compiler_params=pltpu.CompilerParams(**params),
    )(*small, *[array for array, _ in large], *flat, *[array for array, _ in carried])
    others = out[len(results) : len(results) + len(share_shapes)]
    received = [others[k * (size - 1) : (k + 1) * (size - 1)] for k in range(len(shares))]
    halves = out[len(results) + len(share_shapes) :]
    others = out[len(shapes) - len(pull_results) - len(carry_shapes) :]
    received += [
        others[k : k + size - 1] for k in range(0, len(others), max(size - 1, 1)) if size > 1
    ]
    return (
        out[: len(results)],
        received or [[] for _ in range(16)],
        {key: (halves[2 * k], halves[2 * k + 1]) for k, key in enumerate(totals)},
    )


def dot(left, right):
    return jnp.dot(left, right, preferred_element_type=jnp.float32)


def dot_across(left, right):
    return lax.dot_general(left, right, ACROSS_DIMS, preferred_element_type=jnp.float32)


def dot_down(left, right):
    return lax.dot_general(left, right, DOWN_DIMS, preferred_element_type=jnp.float32)


def own_columns(size, place, width):
    owner = lax.rem(lax.axis_index("fsdp") + place, size)
    return pl.ds(pl.multiple_of(owner * width, width), width)


def times_blocks(values_ref, blocks):
    total = None
    for place, block in enumerate(blocks):
        columns = own_columns(len(blocks), place, block.shape[0])
        part = dot(values_ref[:, columns], block[...])
        total = part if total is None else total + part
    return total


def add_back(total_ref, values, blocks, scale=None):
    for place, block in enumerate(blocks):
        columns = own_columns(len(blocks), place, block.shape[0])
        part = dot_across(values, block[...])
        total_ref[:, columns] += part if scale is None else scale * part


def centred(values):
    centre = values - jnp.mean(values, axis=-1, keepdims=True)
    spread = jnp.mean(centre * centre, axis=-1, keepdims=True)
    scale = lax.rsqrt(spread + EPSILON)
    return centre * scale, scale


BIAS_LINES = (6, 7, 9, 10, 8, 11)
TAP_LINE = 12


def gain_line(lines_ref, norm):
    return lines_ref[norm : norm + 1, :]


def bias_line(lines_ref, norm):
    return lines_ref[BIAS_LINES[norm] : BIAS_LINES[norm] + 1, :]


def tap_line(lines_ref, tap):
    return lines_ref[TAP_LINE + tap : TAP_LINE + tap + 1, :]


def norm_low(values, lines_ref, norm):
    hat, _ = centred(values)
    return (hat * gain_line(lines_ref, norm) + bias_line(lines_ref, norm)).astype(jnp.bfloat16)


def norm_grad(grad, values, gain_row):
    hat, scale = centred(values)
    inner = grad * gain_row
    first = jnp.mean(inner, axis=-1, keepdims=True)
    second = jnp.mean(inner * hat, axis=-1, keepdims=True)
    return (
        (inner - first - hat * second) * scale,
        jnp.sum(grad * hat, axis=0, keepdims=True),
        jnp.sum(grad, axis=0, keepdims=True),
    )


def put_rows(ref, *lines):
    for place, line in enumerate(lines):
        ref[pl.ds(place, 1), :] = line
    ref[pl.ds(len(lines), ref.shape[0] - len(lines)), :] = jnp.zeros(
        (ref.shape[0] - len(lines), ref.shape[1]), ref.dtype
    )


def segment_of(lengths_ref, places):
    ends = lengths_ref[0, 0]
    segment = (places >= ends).astype(jnp.int32)
    for index in range(1, lengths_ref.shape[1]):
        ends = ends + lengths_ref[0, index]
        segment += (places >= ends).astype(jnp.int32)
    return segment


def frame_marks(lengths_ref, frames, taps=0):
    places = lax.broadcasted_iota(jnp.int32, (frames, 1), 0)
    segment = segment_of(lengths_ref, places)
    valid = (segment < lengths_ref.shape[1]).astype(jnp.float32)
    marks = []
    for tap in range(taps):
        moved = places + (tap - taps // 2)
        same = (segment_of(lengths_ref, moved) == segment) & (moved >= 0) & (moved < frames)
        marks.append(same.astype(jnp.float32))
    return valid, marks


def same_segment(lengths_ref, frames):
    down = segment_of(lengths_ref, lax.broadcasted_iota(jnp.int32, (frames, 1), 0))
    across = segment_of(lengths_ref, lax.broadcasted_iota(jnp.int32, (1, frames), 1))
    return down == across


TILE = 1024


def feed_forward(w_in, w_out, flow, normed_ref, hidden, slope_ref, y_ref):
    inner = slope_ref.shape[1]
    for part in range(inner // TILE):
        columns = pl.ds(part * TILE, TILE)
        before = times_blocks(normed_ref, w_in(part))
        gate = jax.nn.sigmoid(before)
        value = (before * gate).astype(jnp.bfloat16)
        flow.staged[hidden][:, columns] = value
        flow.put(hidden, columns)
        slope_ref[:, columns] = (gate * (1.0 + before * (1.0 - gate))).astype(jnp.bfloat16)
        add_back(y_ref, value, w_out(part), 0.5)


def feed_forward_back(blocks_in, blocks_out, low_ref, slope_ref, flow, result, normed_ref):
    inner = slope_ref.shape[1]
    normed_ref[...] = jnp.zeros_like(normed_ref)
    for part in range(inner // TILE):
        columns = pl.ds(part * TILE, TILE)
        grad = times_blocks(low_ref, blocks_out(part)) * slope_ref[:, columns].astype(jnp.float32)
        grad = grad.astype(jnp.bfloat16)
        flow.staged[result][:, columns] = grad
        flow.put(result, columns)
        add_back(normed_ref, grad, blocks_in(part))


def head_scores(query, key, bias_row, same, scale):
    frames = query.shape[0]
    spread = jnp.broadcast_to(bias_row, (frames, bias_row.shape[1]))
    relative = pltpu.roll(spread, 0, 1, stride=1, stride_axis=0)[:, :frames]
    return jnp.where(same, dot_across(query, key) * scale + relative, MASKED)


def softmax_rows(scores):
    powers = jnp.exp(scores - jnp.max(scores, axis=-1, keepdims=True))
    return powers / jnp.sum(powers, axis=-1, keepdims=True)


def split(items, count):
    items = list(items)
    return [items[k : k + count] for k in range(0, len(items), count)]


def front(
    x, own_lines, own_bias, lengths, heads, taps, weights, size, collective_id
):
    frames, width = x.shape
    inner = weights[0].shape[1]
    head = width // heads
    small = [own_lines, own_bias, lengths]
    large = [(x, width)]
    large += [(block, TILE) for block in weights[:2]] + [(block, width) for block in weights[2:]]
    order = [(0, 0)]
    order += [(index, part) for part in range(inner // TILE) for index in (1, 2)]
    order += [(3, part) for part in range(3)] + [(4, 0), (5, 1), (5, 0)]
    low, full = jnp.bfloat16, jnp.float32
    results = [
        ((frames, width), low),
        ((frames, inner), low),
        ((frames, inner), low),
        ((frames, width), full),
        ((frames, width), low),
        ((frames, width), low),
        ((frames, width), low),
        ((frames, width), low),
        ((frames, width), low),
        ((frames, width), full),
        ((frames, width), low),
        ((frames, width), full),
        ((frames, width), full),
        ((frames, width), full),
        ((8, width), full),
        ((own_lines.shape[0], width), full),
        ((-(-heads // 8) * 8, own_bias.shape[1]), full),
    ]

    def body(flow, small_refs, _):
        own_lines_ref, own_bias_ref, lengths_ref = small_refs
        valid, marks = frame_marks(lengths_ref, frames, taps)
        (
            normed_one,
            hidden,
            slope,
            x1,
            normed_attn,
            query_ref,
            key_ref,
            value_ref,
            context,
            x2,
            normed_conv,
            gated_ref,
            gate_ref,
            mixed_ref,
            sums_ref,
            lines_ref,
            bias_ref,
        ) = flow.staged
        small_places = [places for _, places in flow.pull_small]
        blocks = [own_lines_ref] + (flow.take_small(small_places[0]) if size > 1 else [])
        for place, block in enumerate(blocks):
            lines_ref[:, own_columns(size, place, block.shape[1])] = block[...]
        flow.put(15)
        blocks = [own_bias_ref] + (flow.take_small(small_places[1]) if size > 1 else [])
        for place, block in enumerate(blocks):
            owner = lax.rem(lax.axis_index("fsdp") + place, size)
            for row in range(heads // size):
                bias_ref[pl.ds(owner * (heads // size) + row, 1), :] = block[row : row + 1, :]
        flow.put(16)
        values = flow.take(0)[...].astype(jnp.float32)
        normed_one[...] = norm_low(values, lines_ref, 0)
        flow.put(0)
        x1[...] = values
        feed_forward(
            lambda part: flow.take_all(1, part),
            lambda part: flow.take_all(2, part),
            flow,
            normed_one,
            1,
            slope,
            x1,
        )
        flow.put(2)
        flow.put(3)

        normed_attn[...] = norm_low(x1[...], lines_ref, 1)
        flow.put(4)
        for part, ref in enumerate((query_ref, key_ref, value_ref)):
            ref[...] = times_blocks(normed_attn, flow.take_all(3, part)).astype(jnp.bfloat16)
            flow.put(5 + part)
        same = same_segment(lengths_ref, frames)
        for place in range(heads):
            columns = slice(place * head, (place + 1) * head)
            scores = head_scores(
                query_ref[:, columns],
                key_ref[:, columns],
                bias_ref[place : place + 1, :],
                same,
                head**-0.5,
            )
            attend = softmax_rows(scores).astype(jnp.bfloat16)
            context[:, columns] = dot(attend, value_ref[:, columns]).astype(jnp.bfloat16)
        flow.put(8)
        x2[...] = x1[...] + times_blocks(context, flow.take_all(4))
        flow.put(9)

        normed_conv[...] = norm_low(x2[...], lines_ref, 2)
        flow.put(10)
        gate = jax.nn.sigmoid(times_blocks(normed_conv, flow.take_all(5, 1)))
        gate_ref[...] = gate
        flow.put(12)
        gated_ref[...] = times_blocks(normed_conv, flow.take_all(5, 0)) * gate
        flow.put(11)
        mixed = jnp.zeros((frames, width), jnp.float32)
        for tap in range(taps):
            offset = tap - taps // 2
            gated = gated_ref[...]
            moved = gated if offset == 0 else pltpu.roll(gated, -offset % frames, 0)
            mixed += tap_line(lines_ref, tap) * (moved * marks[tap])
        mixed_ref[...] = mixed
        flow.put(13)
        weighted = valid * mixed
        put_rows(
            sums_ref,
            jnp.sum(weighted, axis=0, keepdims=True),
            jnp.sum(weighted * mixed, axis=0, keepdims=True),
            jnp.broadcast_to(jnp.sum(valid, axis=0, keepdims=True), (1, width)),
        )
        flow.put(14)

    results, pulled, _ = fused(
        body,
        small,
        large,
        results,
        order,
        size=size,
        collective_id=collective_id,
        pulls=range(1, 6),
        small_pulls=(0, 1),
    )
    return results, [[own, *others] for own, others in zip(weights, pulled)]


def batch_stats(totals_ref):
    count = totals_ref[2:3, :]
    mean = totals_ref[0:1, :] / count
    rstd = lax.rsqrt(totals_ref[1:2, :] / count - mean * mean + EPSILON)
    return count, mean, rstd


def turn(x, mixed, totals, cotangent, lengths, lines, w_conv, w_in, w_out, size, collective_id):
    frames, width = x.shape
    inner = w_in.shape[1]
    small = [totals, lengths, lines]
    large = [(mixed, width), (x, width), (w_conv, width), (w_in, TILE), (w_out, TILE)]
    large += [(cotangent, width)]
    order = [(0, 0), (1, 0), (2, 0)]
    order += [(index, part) for part in range(inner // TILE) for index in (3, 4)]
    order += [(5, 0)]
    low, full = jnp.bfloat16, jnp.float32
    results = [
        ((frames, width), low),
        ((frames, width), low),
        ((frames, inner), low),
        ((frames, width), low),
        ((frames, width), low),
        ((frames, inner), low),
        ((frames, width), low),
        ((frames, width), full),
        ((frames, width), full),
        ((8, width), full),
        ((8, width), full),
        ((8, width), full),
    ]
    scratch = [
        pltpu.VMEM((frames, inner), low),
        pltpu.VMEM((frames, width), full),
        pltpu.VMEM((frames, width), full),
        pltpu.VMEM((frames, width), full),
    ]

    def body(flow, small_refs, rest):
        totals_ref, lengths_ref, lines_ref = small_refs
        valid, _ = frame_marks(lengths_ref, frames)
        slope, x3, x4, normed_grad = rest
        (
            swish,
            normed,
            hidden,
            out_ref,
            low_two,
            before,
            low_conv,
            grad_ref,
            hat_grad,
            sums_final,
            sums_two,
            sums_batch,
        ) = flow.staged
        _, mean, rstd = batch_stats(totals_ref)
        mixed_ref = flow.take(0)
        z = (mixed_ref[...] - mean) * rstd * gain_line(lines_ref, 5) + bias_line(lines_ref, 5)
        swish[...] = (z * jax.nn.sigmoid(z)).astype(jnp.bfloat16)
        flow.put(0)
        x2_ref = flow.take(1)
        conv_blocks = flow.take_all(2)
        x3[...] = x2_ref[...] + times_blocks(swish, conv_blocks)
        normed[...] = norm_low(x3[...], lines_ref, 3)
        flow.put(1)
        x4[...] = x3[...]
        feed_forward(
            functools.partial(flow.take_all, 3),
            functools.partial(flow.take_all, 4),
            flow,
            normed,
            2,
            slope,
            x4,
        )

        gain_row = gain_line(lines_ref, 4)
        hat, _ = centred(x4[...])
        out_ref[...] = (valid * (hat * gain_row + bias_line(lines_ref, 4))).astype(jnp.bfloat16)
        flow.put(3)
        grad = valid * flow.take(len(large) - 1)[...].astype(jnp.float32)
        grad_values, grad_gain, grad_bias = norm_grad(grad, x4[...], gain_row)
        grad_ref[...] = grad_values
        low_two[...] = (0.5 * grad_values).astype(jnp.bfloat16)
        flow.put(4)
        put_rows(sums_final, grad_gain, grad_bias)
        flow.put(9)

        feed_forward_back(
            functools.partial(flow.held_all, 3),
            functools.partial(flow.held_all, 4),
            low_two,
            slope,
            flow,
            5,
            normed_grad,
        )
        branch, grad_gain, grad_bias = norm_grad(
            normed_grad[...], x3[...], gain_line(lines_ref, 3)
        )
        total = grad_ref[...] + branch
        grad_ref[...] = total
        flow.put(7)
        low_conv[...] = total.astype(jnp.bfloat16)
        flow.put(6)
        put_rows(sums_two, grad_gain, grad_bias)
        flow.put(10)

        for place, block in enumerate(conv_blocks):
            columns = own_columns(size, place, block.shape[0])
            hat_grad[:, columns] = dot_across(low_conv[...], block[...])
        hat = (mixed_ref[...] - mean) * rstd
        gain_row = gain_line(lines_ref, 5)
        z = hat * gain_row + bias_line(lines_ref, 5)
        gate = jax.nn.sigmoid(z)
        grad_z = hat_grad[...] * gate * (1.0 + z * (1.0 - gate))
        grad_hat = grad_z * gain_row
        hat_grad[...] = grad_hat
        flow.put(8)
        put_rows(
            sums_batch,
            jnp.sum(grad_hat, axis=0, keepdims=True),
            jnp.sum(grad_hat * hat, axis=0, keepdims=True),
            jnp.sum(grad_z * hat, axis=0, keepdims=True),
            jnp.sum(grad_z, axis=0, keepdims=True),
        )
        flow.put(11)

    return fused(
        body,
        small,
        large,
        results,
        order,
        scratch,
        size=size,
        collective_id=collective_id,
        pulls=(2, 3, 4),
        pulls_stay=True,
    )[0]


def back_front(
    hat_grad,
    gated,
    gate,
    mixed,
    totals,
    back,
    grad,
    x2,
    x1,
    lines,
    bias_table,
    lengths,
    taps,
    packed,
    w_conv,
    w_out,
    w_qkv,
    collective_id,
    **jobs,
):
    frames, width = x1.shape
    count = len(w_conv)
    heads = bias_table.shape[0]
    head = width // heads
    flip = (
        jnp.arange(frames)[:, None] + jnp.arange(frames)[None, :] == frames - 1
    ).astype(jnp.bfloat16)
    small = [totals, back, lengths, lines, bias_table, flip]
    large = [(array, width) for array in (hat_grad, mixed, gated, gate)]
    large += [(block, width) for block in w_conv]
    large += [(array, width) for array in (x2, grad)]
    large += [(block, width) for block in w_out]
    large += [(array, width) for array in packed]
    large += [(block, width) for block in w_qkv]
    large += [(x1, width)]
    conv = list(range(4, 4 + count))
    place_x2 = 4 + count
    out = list(range(place_x2 + 2, place_x2 + 2 + count))
    place_packed = out[-1] + 1
    qkv = list(range(place_packed + 3, place_packed + 3 + count))
    order = None
    low, full = jnp.bfloat16, jnp.float32
    results = [((frames, width), low)] * 7 + [((frames, width), full)]
    results += [((8, width), full)] * 3 + [(bias_table.shape, full)]
    scratch = [
        pltpu.VMEM((frames, width), full),
        pltpu.VMEM((frames, width), full),
        pltpu.VMEM((frames, width), low),
    ]

    def body(flow, small_refs, rest):
        (
            totals_ref,
            back_ref,
            lengths_ref,
            lines_ref,
            bias_ref,
            flip_ref,
        ) = small_refs
        valid, marks = frame_marks(lengths_ref, frames, taps)
        normed_grad, grad_mixed_ref, grad_context = rest
        one, two, low_attn, *grad_refs = flow.staged[:6]
        low_one, grad_ref, sums_kernel, sums_conv, sums_attn, sums_rel = flow.staged[6:]
        valid_count, mean, rstd = batch_stats(totals_ref)
        grad_var = -0.5 * rstd * rstd * back_ref[1:2, :]
        grad_mean = -rstd * back_ref[0:1, :] - 2.0 * mean * grad_var
        hat_ref, mixed_ref = flow.take(0), flow.take(1)
        grad_mixed_ref[...] = (
            hat_ref[...] * rstd
            + valid * (grad_mean + 2.0 * mixed_ref[...] * grad_var) / valid_count
        )
        gated_ref = flow.take(2)
        normed_grad[...] = jnp.zeros_like(normed_grad)
        kernel_grads = []
        for tap in range(taps):
            offset = tap - taps // 2
            masked = grad_mixed_ref[...] * marks[tap]
            gated = gated_ref[...]
            moved = gated if offset == 0 else pltpu.roll(gated, -offset % frames, 0)
            kernel_grads.append(jnp.sum(masked * moved, axis=0, keepdims=True))
            moved = masked if offset == 0 else pltpu.roll(masked, offset % frames, 0)
            normed_grad[...] += tap_line(lines_ref, tap) * moved
        put_rows(sums_kernel, *kernel_grads)
        flow.put(8)
        gate_now = flow.take(3)[...]
        grad_gated = normed_grad[...]
        one[...] = (grad_gated * gate_now).astype(jnp.bfloat16)
        flow.put(0)
        if count > 1:
            flow.share(0)
        two[...] = (grad_gated * gated_ref[...] * (1.0 - gate_now)).astype(jnp.bfloat16)
        flow.put(1)
        if count > 1:
            flow.share(1)
        normed_grad[...] = jnp.zeros_like(normed_grad)
        for part, ref in enumerate((one, two)):
            add_back(normed_grad, ref[...], [flow.take(index, part) for index in conv])
        branch, grad_gain, grad_bias = norm_grad(
            normed_grad[...], flow.take(place_x2)[...], gain_line(lines_ref, 2)
        )
        total = flow.take(place_x2 + 1)[...] + branch
        grad_ref[...] = total
        low_attn[...] = total.astype(jnp.bfloat16)
        flow.put(2)
        if count > 1:
            flow.share(2)
        put_rows(sums_conv, grad_gain, grad_bias)
        flow.put(9)

        for place, index in enumerate(out):
            block = flow.take(index)
            columns = own_columns(count, place, block.shape[0])
            grad_context[:, columns] = dot_across(low_attn[...], block[...]).astype(jnp.bfloat16)
        packed_refs = [flow.take(place_packed + part) for part in range(3)]
        same = same_segment(lengths_ref, frames)
        scale = head**-0.5
        reach = bias_ref.shape[1]
        for place in range(heads):
            columns = slice(place * head, (place + 1) * head)
            query, key, value = (ref[:, columns] for ref in packed_refs)
            bias_row = bias_ref[place : place + 1, :]
            attend = softmax_rows(head_scores(query, key, bias_row, same, scale))
            context = grad_context[:, columns]
            grad_attend = dot_across(context, value)
            grad_value = dot_down(attend.astype(jnp.bfloat16), context)
            grad_scores = attend * (
                grad_attend - jnp.sum(grad_attend * attend, axis=-1, keepdims=True)
            )
            grad_low = grad_scores.astype(jnp.bfloat16)
            padded = jnp.concatenate(
                [dot(grad_low, flip_ref[...]), jnp.zeros((frames, reach - frames), jnp.float32)],
                axis=1,
            )
            skewed = pltpu.roll(padded, 0, 1, stride=1, stride_axis=0)
            sums_rel[place : place + 1, :] = jnp.sum(skewed, axis=0, keepdims=True)
            grad_query = dot(grad_low, key) * scale
            grad_key = dot_down(grad_low, query) * scale
            for ref, part in zip(grad_refs, (grad_query, grad_key, grad_value)):
                ref[:, columns] = part.astype(jnp.bfloat16)
        flow.put(11)
        normed_grad[...] = jnp.zeros_like(normed_grad)
        for part, ref in enumerate(grad_refs):
            flow.put(3 + part)
            if count > 1:
                flow.share(3 + part)
            add_back(normed_grad, ref[...], [flow.take(index, part) for index in qkv])
        branch, grad_gain, grad_bias = norm_grad(
            normed_grad[...], flow.take(len(large) - 1)[...], gain_line(lines_ref, 1)
        )
        total = grad_ref[...] + branch
        grad_ref[...] = total
        flow.put(7)
        low_one[...] = (0.5 * total).astype(jnp.bfloat16)
        flow.put(6)
        if count > 1:
            flow.share(6)
        put_rows(sums_attn, grad_gain, grad_bias)
        flow.put(10)

    shares = {0: "all", 1: "all", 2: "all", 3: "all", 4: "all", 5: "all", 6: "columns"}
    return fused(
        body, small, large, results, order, scratch, shares, count, collective_id, **jobs
    )


def back_end(low, grad, x, lines, slope, w_in, w_out, collective_id, **jobs):
    frames, width = x.shape
    inner, count = w_in[0].shape[1], len(w_in)
    large = [(low, width)] + [(block, TILE) for block in w_out + w_in]
    large += [(slope, TILE), (x, width), (grad, width)]
    groups = split(range(1, 1 + 2 * count), count)
    place_slope = 1 + 2 * count
    order = [(0, 0)]
    for part in range(inner // TILE):
        order += [(index, part) for index in groups[0]] + [(place_slope, part)]
        order += [(index, part) for index in groups[1]]
    order += [(place_slope + 1, 0), (place_slope + 2, 0)]
    results = [
        ((frames, inner), jnp.bfloat16),
        ((frames, width), jnp.bfloat16),
        ((8, width), jnp.float32),
    ]

    def body(flow, small_refs, rest):
        (lines_ref,), (normed_grad,) = small_refs, rest
        before, out_ref, sums_ref = flow.staged

        def w_out_part(part):
            blocks = [flow.take(index, part) for index in groups[0]]
            flow.take(place_slope, part)
            return blocks

        def w_in_part(part):
            return [flow.take(index, part) for index in groups[1]]

        feed_forward_back(
            w_in_part, w_out_part, flow.take(0), flow.held[place_slope], flow, 0, normed_grad
        )
        if count > 1:
            flow.share(0)
        values = flow.take(place_slope + 1)[...].astype(jnp.float32)
        branch, grad_gain, grad_bias = norm_grad(normed_grad[...], values, gain_line(lines_ref, 0))
        out_ref[...] = (flow.take(place_slope + 2)[...] + branch).astype(jnp.bfloat16)
        flow.put(1)
        put_rows(sums_ref, grad_gain, grad_bias)
        flow.put(2)

    scratch = [pltpu.VMEM((frames, width), jnp.float32)]
    shares = {0: "all"}
    return fused(
        body, [lines], large, results, order, scratch, shares, count, collective_id, **jobs
    )


def halves_plainly(jobs, bits):
    products = {}
    for lefts, rights, first, columns, key in jobs:
        rows = lefts[0].shape[1] // len(lefts)
        own = lax.dynamic_slice_in_dim(lefts[0], lax.axis_index("fsdp") * rows, rows, axis=1)
        left = jnp.concatenate([own, *lefts[1:]])
        right = jnp.concatenate(rights)[:, first : first + columns]
        products.setdefault(key, []).append(dot_down(left, right).astype(jnp.bfloat16))
    halves = {}
    for key, parts in products.items():
        product = jnp.concatenate(parts, axis=1)
        half = product.shape[0] // 2
        upper = lax.rem(lax.axis_index("dp") // bits[key[1]], 2)
        halves[key] = tuple(
            lax.dynamic_slice_in_dim(product, part * half, half, axis=0)
            for part in (1 - upper, upper)
        )
    return halves


def join_body(bits, counts, *refs):
    step = pl.program_id(0)
    out_ref = refs[-1]
    half = refs[0].shape[0]
    first = 0
    for index, (bit, count) in enumerate(zip(bits, counts)):
        upper = lax.rem(lax.axis_index("dp") // bit, 2)

        @pl.when((step >= first) & (step < first + count))
        def _(index=index, upper=upper):
            for ref, part in zip(refs[2 * index : 2 * index + 2], (upper, 1 - upper)):
                rows = pl.ds(pl.multiple_of(part * half, half), half)
                out_ref[rows, :] = ref[...].astype(jnp.float32)

        first += count


def join(parts, tile=512):
    counts = [columns // tile for _, _, _, _, columns in parts]
    rows = 2 * parts[0][1].shape[0]
    specs, flat, first = [], [], 0
    for (_, mine, other, start, _), count in zip(parts, counts):

        def index(step, first=first, count=count, start=start // tile):
            return (0, start + jnp.clip(step - first, 0, count - 1))

        specs += [pl.BlockSpec((rows // 2, tile), index)] * 2
        flat += [mine, other]
        first += count
    return pl.pallas_call(
        functools.partial(join_body, [part[0] for part in parts], counts),
        grid=(first,),
        out_shape=jax.ShapeDtypeStruct((rows, first * tile), jnp.float32),
        in_specs=specs,
        out_specs=pl.BlockSpec((rows, tile), lambda step: (0, step)),
        compiler_params=pltpu.CompilerParams(vmem_limit_bytes=60 * 2**20),
    )(*flat)


def bias_lines(table, frames):
    heads, middle = table.shape[0], (table.shape[1] - 1) // 2
    half = -(-frames // 64) * 64
    above = jnp.broadcast_to(table[:, -1:], (heads, half - middle - 1))
    below = jnp.broadcast_to(table[:, :1], (heads, half - middle))
    return jnp.concatenate([table[:, middle:], above, below, table[:, :middle]], axis=1)


def bias_lines_back(sums, frames, reach):
    return jnp.concatenate(
        [
            jnp.sum(sums[:, frames - 1 + reach :], axis=1, keepdims=True),
            sums[:, frames - reach : frames - 1 + reach][:, ::-1],
            jnp.sum(sums[:, : frames - reach], axis=1, keepdims=True),
        ],
        axis=1,
    )


def eight_lines(*lines):
    lines = list(lines)
    return jnp.stack(lines + [jnp.zeros_like(lines[0])] * (-len(lines) % 8))


def per_device(
    sizes,
    inputs,
    cotangent,
    lengths,
    ffn1_in,
    ffn1_out,
    attn_qkv,
    attn_out,
    rel_table,
    conv_in,
    depth_kernel,
    conv_out,
    ffn2_in,
    ffn2_out,
    gains,
    biases,
    inner_biases,
):
    dp_size, fsdp_size = sizes
    axes = (("fsdp", fsdp_size), ("dp", dp_size))
    rows = Rows(fsdp_size)
    groups = Groups(axes)
    frames, width = inputs.shape
    taps = depth_kernel.shape[1]

    own_lines = jnp.concatenate([gains, biases, inner_biases, depth_kernel], axis=1)
    own_lines = jnp.pad(own_lines, ((0, 0), (0, -own_lines.shape[1] % 8))).astype(jnp.float32).T
    own_bias = bias_lines(rel_table.astype(jnp.float32), frames)
    own_bias = jnp.pad(own_bias, ((0, -own_bias.shape[0] % 8), (0, 0)))
    heads = rel_table.shape[0] * fsdp_size

    (
        (
            normed_one,
            hidden_one,
            slope_one,
            x1,
            normed_attn,
            *packed,
            context,
            x2,
            normed_conv,
            gated,
            gate,
            mixed,
            sums,
            lines,
            bias_table,
        ),
        (w_ffn1_in, w_ffn1_out, w_qkv, w_attn_out, w_conv_in),
    ) = front(
        inputs,
        own_lines,
        own_bias,
        lengths,
        heads,
        taps,
        (ffn1_in, ffn1_out, attn_qkv, attn_out, conv_in),
        fsdp_size,
        6,
    )
    totals, _ = sum_and_share(rows, axes, sums, [], 0)
    (
        swish,
        normed_two,
        hidden_two,
        layer_out,
        low_two,
        before_two,
        low_conv,
        grad,
        hat_grad,
        sums_final,
        sums_two,
        sums_batch,
    ) = turn(
        x2,
        mixed,
        totals,
        cotangent,
        lengths,
        lines,
        conv_out,
        ffn2_in,
        ffn2_out,
        fsdp_size,
        7,
    )
    arrays = (low_two, normed_two, swish, hidden_two, before_two, low_conv)
    modes = ("columns",) * 3 + ("all",) * 3
    back, shared = sum_and_share(rows, axes, sums_batch, list(zip(arrays, modes)), 1)
    left_low_two, left_normed_two, left_swish, right_hidden_two, right_before_two, right_low_conv = [
        [own, *others] for own, others in zip(arrays, shared)
    ]

    inner = hidden_two.shape[1]
    main, half, rest = inner * 3 // 4, inner * 3 // 8, inner // 4
    jobs = [
        (left_low_two, right_hidden_two, 0, main, (0, 0)),
        (left_normed_two, right_before_two, 0, main, (0, 1)),
        (left_low_two, right_hidden_two, main, rest, (0, 2)),
        (left_swish, right_low_conv, 0, width, (0, 2)),
        (left_normed_two, right_before_two, main, rest, (0, 3)),
    ]
    arrays = (normed_conv, context, normed_attn, normed_one)
    results, shared, bundles = groups.along(
        jobs,
        functools.partial(
            back_front,
            hat_grad,
            gated,
            gate,
            mixed,
            totals,
            back,
            grad,
            x2,
            x1,
            lines,
            bias_table,
            lengths,
            taps,
            packed,
            w_conv_in,
            w_attn_out,
            w_qkv,
            3,
            spread=True,
            carried=[(array, "columns") for array in arrays] + [(hidden_one, "all")],
        ),
    )
    two = bundles[0]
    *back_lefts, low_one, grad, sums_kernel, sums_conv, sums_attn, sums_rel = results
    right_one, right_two, right_low_attn, right_q, right_k, right_v, left_low_one = [
        [own, *others] for own, others in zip((*back_lefts, low_one), shared)
    ]
    left_normed_conv, left_context, left_normed_attn, left_normed_one, right_hidden_one = [
        [own, *others] for own, others in zip((*arrays, hidden_one), shared[7:])
    ]

    jobs = [
        (left_normed_conv, right_one, 0, width, (0, 0)),
        (left_normed_conv, right_two, 0, width, (0, 1)),
        (left_context, right_low_attn, 0, width, (0, 3)),
        (left_normed_attn, right_q, 0, width, (0, 0)),
        (left_normed_attn, right_k, 0, width, (0, 1)),
        (left_normed_attn, right_v, 0, width, (0, 3)),
        (left_low_one, right_hidden_one, 0, half, (1, 0)),
        (left_low_one, right_hidden_one, half, half, (1, 1)),
        (left_low_one, right_hidden_one, main, rest, (1, 2)),
    ]
    (before_one, input_grad, sums_one), shared, bundles = groups.along(
        jobs,
        functools.partial(
            back_end, low_one, grad, inputs, lines, slope_one, w_ffn1_in, w_ffn1_out, 4
        ),
    )
    mid, out = bundles[0], bundles[1]
    right_before_one = [before_one, *shared[0]]

    jobs = [
        (left_normed_one, right_before_one, 0, half, (0, 0)),
        (left_normed_one, right_before_one, half, half, (0, 1)),
        (left_normed_one, right_before_one, main, rest, (0, 3)),
    ]
    _, _, bundles = groups.along(
        jobs, functools.partial(fused, None, [], [], [], collective_id=5, spread=True)
    )
    end = bundles[0]

    bundles = (two, mid, out, end)
    middle, sums = groups.middle(
        [[bundle[kind] for bundle in bundles if kind in bundle] for kind in range(4)],
        (
            sums_one,
            sums_attn,
            sums_conv,
            sums_two,
            sums_final,
            sums_batch,
            sums_kernel,
            sums_rel,
        ),
        [(0, 1)] * 5 + [(2, 3), tuple(range(taps)), tuple(range(heads))],
        width,
        2,
    )
    middle = [iter(arrays) for arrays in middle]
    two, mid, out, end = [
        {kind: next(middle[kind]) for kind in range(4) if kind in bundle} for bundle in bundles
    ]
    two, mid = groups.finish(two), groups.finish(mid)
    sum_ffn2_out = groups.join((two[0], 0, main), (two[2], 0, rest))
    sum_ffn2_in = groups.join((two[1], 0, main), (two[3], 0, rest))
    sum_conv_out = groups.join((two[2], rest, width))
    out, end, sum_ffn2_out, sum_ffn2_in, sum_conv_out = lax.optimization_barrier(
        (out, end, sum_ffn2_out, sum_ffn2_in, sum_conv_out)
    )
    out, end = groups.finish(out), groups.finish(end)
    sum_qkv = groups.join(*[(mid[kind], width, width) for kind in (0, 1, 3)])
    sum_conv_in = groups.join((mid[0], 0, width), (mid[1], 0, width))
    sum_attn_out = groups.join((mid[3], 0, width))
    sum_ffn1_out = groups.join((out[0], 0, half), (out[1], 0, half), (out[2], 0, rest))
    sum_ffn1_in = groups.join((end[0], 0, half), (end[1], 0, half), (end[3], 0, rest))
    own = lax.dynamic_slice_in_dim(sums, rows.me * gains.shape[0], gains.shape[0], axis=1)
    first = 12 + taps
    rel_sum = lax.dynamic_slice_in_dim(
        sums, first + rows.me * rel_table.shape[0], rel_table.shape[0], axis=0
    )
    rel_sum = bias_lines_back(
        rel_sum[:, : sums_rel.shape[1]], frames, (rel_table.shape[1] - 1) // 2
    )
    return (
        layer_out,
        input_grad,
        sum_ffn1_in,
        sum_ffn1_out,
        sum_qkv,
        sum_attn_out,
        rel_sum,
        sum_conv_in,
        own[12:first].T,
        sum_conv_out,
        sum_ffn2_in,
        sum_ffn2_out,
        own[0:12:2].T,
        jnp.stack([own[1], own[3], own[9]], axis=1),
        jnp.stack([own[5], own[7], own[11]], axis=1),
    )


def solution(mesh):
    frame_spec = P(("dp", "fsdp"), None)
    row_spec = P("fsdp", None)
    sizes = (mesh.shape["dp"], mesh.shape["fsdp"])
    return jax.shard_map(
        functools.partial(per_device, sizes),
        mesh=mesh,
        in_specs=(frame_spec,) * 3 + (row_spec,) * 13,
        out_specs=(frame_spec,) * 2 + (row_spec,) * 13,
        check_vma=False,
    )
```

```python
import functools

import jax
import jax.numpy as jnp
from jax import lax
from jax.experimental import pallas as pl
from jax.experimental.pallas import tpu as pltpu
from jax.sharding import PartitionSpec as P

EPSILON = 1e-05
MASKED = -1000000000.0
AHEAD = 4
DOWN_DIMS = (((0,), (0,)), ((), ()))
ACROSS_DIMS = (((1,), (1,)), ((), ()))


def pair_partners(axes):
    partners = []
    for name, size in axes:
        me = lax.axis_index(name)
        bit = 1
        while bit < size:
            partners.append({name: me + bit * (1 - 2 * ((me // bit) % 2))})
            bit *= 2
    return partners


def sum_stages(axes):
    near = [(name, 1 << k) for name, size in axes for k in range(size.bit_length() - 1)]
    stages = []
    while near:
        count = 3 if len(near) in (3, 5) or len(near) > 6 else 2
        stages.append(near[:count])
        near = near[count:]
    return stages


def stage_partners(bits):
    uppers = [lax.rem(lax.axis_index(name) // bit, 2) for name, bit in bits]
    place = sum(upper << k for k, upper in enumerate(uppers))
    devices = []
    for other in range(1 << len(bits)):
        device = {}
        for k, (name, bit) in enumerate(bits):
            start = device.get(name, lax.axis_index(name))
            device[name] = start + bit * (((other >> k) & 1) - uppers[k])
        devices.append(device)
    return place, devices


def pair_kernel(axes, modes, lines, *refs):
    refs = list(refs)

    def pick(count):
        picked = refs[:count]
        del refs[:count]
        return picked

    size = dict(axes)["fsdp"]
    (x_ref,), shared, (o_ref,) = pick(1), pick(len(modes)), pick(1)
    outs = [pick(size - 1) for _ in modes]
    slots, packed, send_sems, recv_sems, share_send, share_recv = refs
    tiles = x_ref.shape[1] // 128

    def lanes(index):
        return pl.ds(index // tiles, 1), pl.ds(index % tiles * 128, 128)

    stages = [stage_partners(bits) for bits in sum_stages(axes)]
    me = lax.axis_index("fsdp")
    peers = [{"fsdp": lax.rem(me + size - step, size)} for step in range(1, size)]
    barrier = pltpu.get_barrier_semaphore()
    greeted = 0
    for place, devices in stages:
        for other, device in enumerate(devices):

            @pl.when(other != place)
            def _(device=device):
                pl.semaphore_signal(
                    barrier, inc=1, device_id=device, device_id_type=pl.DeviceIdType.MESH
                )

        greeted += len(devices) - 1
    if modes and size > 2:
        for peer in peers:
            pl.semaphore_signal(barrier, inc=1, device_id=peer, device_id_type=pl.DeviceIdType.MESH)
        greeted += size - 1
    pl.semaphore_wait(barrier, greeted)
    copies = []
    for index, (mode, source) in enumerate(zip(modes, shared)):
        for step, peer in enumerate(peers):
            if mode == "columns":
                width = source.shape[1] // size
                start = pl.multiple_of(peer["fsdp"] * width, width)
                source_now = source.at[:, pl.ds(start, width)]
            else:
                source_now = source
            copies.append(
                pltpu.make_async_remote_copy(
                    src_ref=source_now,
                    dst_ref=outs[index][step],
                    send_sem=share_send.at[index, step],
                    recv_sem=share_recv.at[index, step],
                    device_id=peer,
                    device_id_type=pl.DeviceIdType.MESH,
                )
            )
    for index in range(packed.shape[0]):
        row, columns = lanes(index)
        packed[pl.ds(index, 1), :] = x_ref[row, columns]
    for stage, (place, devices) in enumerate(stages):

        def exchange(other, device, stage=stage, place=place):
            return pltpu.make_async_remote_copy(
                src_ref=packed,
                dst_ref=slots.at[stage, place],
                send_sem=send_sems.at[stage, other],
                recv_sem=recv_sems.at[stage, place],
                device_id=device,
                device_id_type=pl.DeviceIdType.MESH,
            )

        def arrival(other, device, stage=stage):
            return pltpu.make_async_remote_copy(
                src_ref=packed,
                dst_ref=slots.at[stage, other],
                send_sem=send_sems.at[stage, other],
                recv_sem=recv_sems.at[stage, other],
                device_id=device,
                device_id_type=pl.DeviceIdType.MESH,
            )

        for other, device in enumerate(devices):
            pl.when(other != place)(exchange(other, device).start)
        if stage == 0:
            for copy in copies:
                copy.start()
        for other, device in enumerate(devices):
            pl.when(other != place)(arrival(other, device).wait)
        slots[stage, pl.ds(place, 1)] = packed[...][None]
        total = slots[stage, 0]
        for other in range(1, len(devices)):
            total += slots[stage, other]
        packed[...] = total
    o_ref[...] = jnp.zeros_like(o_ref)
    for index in range(packed.shape[0]):
        row, columns = lanes(index)
        o_ref[row, columns] = packed[pl.ds(index, 1), :]
    for copy in copies:
        copy.wait()


def sum_and_share(rows, axes, values, lines, shared, collective_id):
    size = dict(axes)["fsdp"]
    stages = len(sum_stages(axes))
    if any(count & (count - 1) for _, count in axes) or stages == 0:
        total = lax.psum(values, tuple(name for name, _ in axes))
        total = jnp.concatenate([total[:lines], jnp.zeros_like(total[lines:])])
        return total, [
            (rows.all_frames if mode == "all" else rows.all_frames_own_columns)(array)[1:]
            for array, mode in shared
        ]
    packed = (lines * values.shape[1] // 128, 128)
    shapes = [
        array.shape if mode == "all" else (array.shape[0], array.shape[1] // size)
        for array, mode in shared
    ]
    out = pl.pallas_call(
        functools.partial(pair_kernel, axes, [mode for _, mode in shared], lines),
        out_shape=[jax.ShapeDtypeStruct(values.shape, values.dtype)]
        + [
            jax.ShapeDtypeStruct(shape, array.dtype)
            for shape, (array, _) in zip(shapes, shared)
            for _ in range(size - 1)
        ],
        in_specs=[pl.BlockSpec(memory_space=pltpu.VMEM)]
        + [pl.BlockSpec(memory_space=pl.ANY)] * len(shared),
        out_specs=[pl.BlockSpec(memory_space=pltpu.VMEM)]
        + [pl.BlockSpec(memory_space=pl.ANY)] * (len(shared) * (size - 1)),
        scratch_shapes=[
            pltpu.VMEM((stages, 8) + packed, values.dtype),
            pltpu.VMEM(packed, values.dtype),
            pltpu.SemaphoreType.DMA((stages, 8)),
            pltpu.SemaphoreType.DMA((stages, 8)),
            pltpu.SemaphoreType.DMA((max(len(shared), 1), max(size - 1, 1))),
            pltpu.SemaphoreType.DMA((max(len(shared), 1), max(size - 1, 1))),
        ],
        compiler_params=pltpu.CompilerParams(
            collective_id=collective_id, has_side_effects=True, vmem_limit_bytes=60 * 2**20
        ),
    )(values, *[array for array, _ in shared])
    return out[0], [
        out[1 + k * (size - 1) : 1 + (k + 1) * (size - 1)] for k in range(len(shared))
    ]


class Rows:
    def __init__(self, size):
        self.size = size
        self.me = lax.axis_index("fsdp")

    def owner(self, step):
        return lax.rem(self.me + step, self.size)

    def shift(self, values, step):
        return lax.ppermute(
            values, "fsdp", [(j, (j - step) % self.size) for j in range(self.size)]
        )

    def gather(self, block):
        return [(self.me, block)] + [
            (self.owner(step), self.shift(block, step)) for step in range(1, self.size)
        ]

    def columns(self, values, owner):
        width = values.shape[1] // self.size
        return lax.dynamic_slice_in_dim(values, owner * width, width, axis=1)

    def order(self, parts, axis):
        if self.size == 1:
            return parts[0]
        width = parts[0].shape[axis]
        twice = jnp.concatenate(parts + parts, axis=axis)
        start = lax.rem(self.size - self.me, self.size) * width
        return lax.dynamic_slice_in_dim(twice, start, width * self.size, axis=axis)

    def all_frames(self, values):
        return [values] + [self.shift(values, step) for step in range(1, self.size)]

    def all_frames_own_columns(self, values):
        return [self.columns(values, self.me)] + [
            self.shift(self.columns(values, self.owner(self.size - step)), step)
            for step in range(1, self.size)
        ]


def cube_rounds(bits, line):
    swaps = bits[:-2] if line and tuple(bits[-2:]) == line else bits
    rounds = tuple(("swap", bit) for bit in swaps)
    return rounds if swaps == bits else rounds + (("give", line[0]), ("mid", line[0]))


def cube_kernel(axes, plan, lines, *refs):
    me = lax.axis_index("dp")
    refs = list(refs)

    def pick(count):
        picked = refs[:count]
        del refs[:count]
        return picked

    arrays = [len(columns) for _, columns, _ in plan]
    inputs, small_refs = pick(2 * sum(arrays)), pick(len(lines))
    outputs, (small_out,) = pick(sum(arrays)), pick(1)
    kinds, first = [], 0
    for rounds, columns, chunk in plan:
        whole, other, result = pick(3)
        sums = pick(len(rounds))
        send_sems, recv_sems = pick(2)
        rows, start, steps = whole.shape[0], 0, []
        for name, bit in rounds:
            step = dict(name=name, rows=rows, before=start)
            if name == "swap":
                step["upper"] = lax.rem(me // bit, 2)
                step["partner"] = me + bit * (1 - 2 * step["upper"])
                step["sends"] = step["takes"] = None
            else:
                place = lax.rem(me // bit, 4)
                inner = (place == 1) | (place == 2)
                if name == "give":
                    step["partner"] = me + bit * (1 - 2 * lax.rem(place, 2))
                    step["sends"], step["takes"] = jnp.logical_not(inner), inner
                else:
                    step["upper"] = place // 2
                    step["partner"] = me + bit * (1 - 2 * step["upper"])
                    step["sends"] = step["takes"] = inner
            if name != "give":
                rows //= 2
                start = start + step["upper"] * rows
            step["after"] = start
            steps.append(step)
        edges = [sum(columns[:k]) for k in range(len(columns) + 1)]
        kinds.append(
            dict(
                steps=steps,
                columns=columns,
                edges=edges,
                chunk=chunk,
                count=edges[-1] // chunk,
                whole=whole,
                other=other,
                result=result,
                sums=sums,
                send=send_sems,
                recv=recv_sems,
                first=first,
            )
        )
        first += len(columns)
    load_sems, store_sems, slots, small_send, small_recv = refs
    partners = pair_partners(axes)

    def loads(kind, place):
        index = kind["first"] + place
        columns = pl.ds(kind["edges"][place], kind["columns"][place])
        return [
            pltpu.make_async_copy(
                inputs[2 * index + term],
                kind[name].at[:, columns],
                load_sems.at[2 * index + term],
            )
            for term, name in enumerate(("whole", "other"))
        ]

    def store(kind, place):
        index = kind["first"] + place
        columns = pl.ds(kind["edges"][place], kind["columns"][place])
        return pltpu.make_async_copy(
            kind["result"].at[:, columns], outputs[index], store_sems.at[index]
        )

    for place in range(max(arrays)):
        for kind in kinds:
            if place < len(kind["columns"]):
                for copy in loads(kind, place):
                    copy.start()
    small_out[...] = jnp.zeros_like(small_out)
    line = 0
    for ref, rows in zip(small_refs, lines):
        for row in rows:
            small_out[line : line + 1, : ref.shape[1]] = ref[row : row + 1, :]
            line += 1
    barrier = pltpu.get_barrier_semaphore()
    lines = sorted({bit for rounds, _, _ in plan for name, bit in rounds if name == "mid"})
    for partner in partners:
        pl.semaphore_signal(barrier, inc=1, device_id=partner, device_id_type=pl.DeviceIdType.MESH)
    if lines:
        (bit,) = lines
        place = lax.rem(me // bit, 4)
        inner = (place == 1) | (place == 2)

        @pl.when(inner)
        def _():
            pl.semaphore_signal(
                barrier,
                inc=1,
                device_id={"dp": me + bit * (1 - 2 * (place // 2))},
                device_id_type=pl.DeviceIdType.MESH,
            )
            pl.semaphore_wait(barrier, len(partners) + 1)

        @pl.when(jnp.logical_not(inner))
        def _():
            pl.semaphore_wait(barrier, len(partners))

    else:
        pl.semaphore_wait(barrier, len(partners))

    def window(kind, index):
        return pl.ds(pl.multiple_of(index * kind["chunk"], kind["chunk"]), kind["chunk"])

    def aligned(start, rows):
        return pl.ds(start if isinstance(start, int) else pl.multiple_of(start, rows), rows)

    def source(kind, number):
        return kind["whole"] if number == 0 else kind["sums"][number - 1]

    def copy_in(kind, number, index):
        step, columns = kind["steps"][number], window(kind, index)
        rows = step["rows"]
        given = pl.ds(0, rows)
        if step["name"] != "give":
            given = aligned((1 - step["upper"]) * (rows // 2), rows // 2)
        return pltpu.make_async_remote_copy(
            src_ref=source(kind, number).at[given, columns],
            dst_ref=kind["sums"][number].at[:, columns],
            send_sem=kind["send"].at[number, index],
            recv_sem=kind["recv"].at[number, index],
            device_id={"dp": step["partner"]},
            device_id_type=pl.DeviceIdType.MESH,
        )

    def copy_out(kind, number, index):
        step = kind["steps"][number]
        rows = step["rows"] if step["name"] == "give" else step["rows"] // 2
        start = step["before"] if step["name"] == "give" else step["after"]
        block = kind["result"].at[aligned(start, rows), window(kind, index)]
        slot = 2 * len(kind["steps"]) - 1 - number
        return pltpu.make_async_remote_copy(
            src_ref=block,
            dst_ref=block,
            send_sem=kind["send"].at[slot, index],
            recv_sem=kind["recv"].at[slot, index],
            device_id={"dp": step["partner"]},
            device_id_type=pl.DeviceIdType.MESH,
        )

    def when(condition, action):
        if condition is None:
            action()
        else:
            pl.when(condition)(action)

    def end_in(kind, number, index):
        step, columns = kind["steps"][number], window(kind, index)
        copy = copy_in(kind, number, index)
        last = number == len(kind["steps"]) - 1

        def add():
            copy.wait_recv()
            rows = step["rows"]
            kept = pl.ds(0, rows)
            if step["name"] != "give":
                rows //= 2
                kept = aligned(step["upper"] * rows, rows)
            total = (
                source(kind, number)[kept, columns].astype(jnp.float32)
                + kind["sums"][number][:, columns].astype(jnp.float32)
            ).astype(kind["whole"].dtype)
            if last:
                kind["result"][aligned(step["after"], rows), columns] = total
            else:
                kind["sums"][number][:, columns] = total

        when(step["sends"], copy.wait_send)
        when(step["takes"], add)

    def advance(kind, stage, index):
        depth = len(kind["steps"])
        if stage == 0:
            for place, edge in enumerate(kind["edges"][:-1]):

                @pl.when(index == edge // kind["chunk"])
                def _(place=place):
                    for copy in loads(kind, place):
                        copy.wait()

            columns = window(kind, index)
            kind["whole"][:, columns] = (
                kind["whole"][:, columns].astype(jnp.float32)
                + kind["other"][:, columns].astype(jnp.float32)
            ).astype(kind["whole"].dtype)
        elif stage <= depth:
            end_in(kind, stage - 1, index)
        else:
            number = 2 * depth - stage
            step = kind["steps"][number]
            copy = copy_out(kind, number, index)
            when(step["takes"], copy.wait_send)
            when(step["sends"], copy.wait_recv)
        if stage < depth:
            when(kind["steps"][stage]["sends"], copy_in(kind, stage, index).start)
        elif stage < 2 * depth:
            number = 2 * depth - 1 - stage
            when(kind["steps"][number]["takes"], copy_out(kind, number, index).start)
        else:
            for place, edge in enumerate(kind["edges"][1:]):

                @pl.when(index == edge // kind["chunk"] - 1)
                def _(place=place):
                    store(kind, place).start()

    def exchange(stage):
        return pltpu.make_async_remote_copy(
            src_ref=small_out,
            dst_ref=slots.at[stage],
            send_sem=small_send.at[stage],
            recv_sem=small_recv.at[stage],
            device_id=partners[stage],
            device_id_type=pl.DeviceIdType.MESH,
        )

    last = max(kind["count"] + 2 * len(kind["steps"]) for kind in kinds)
    last = max(last, len(partners) + 1)

    @pl.loop(0, last)
    def _(tick):
        for stage in range(len(partners) + 1):

            @pl.when(tick == stage)
            def _(stage=stage):
                if stage > 0:
                    exchange(stage - 1).wait()
                    small_out[...] += slots[stage - 1]
                if stage < len(partners):
                    exchange(stage).start()

        for stage in range(2 * max(len(kind["steps"]) for kind in kinds) + 1):
            for kind in kinds:
                if stage <= 2 * len(kind["steps"]):

                    @pl.when((tick >= stage) & (tick < stage + kind["count"]))
                    def _(kind=kind, stage=stage):
                        advance(kind, stage, tick - stage)

    for kind in kinds:
        for place in range(len(kind["columns"])):
            store(kind, place).wait()


def sum_cube(axes, parts, plan, small, lines, width, collective_id):
    shape = (-(-sum(len(rows) for rows in lines) // 8) * 8, width)
    flat = [term for kind in parts for pair in kind for term in pair]
    scratch = []
    for kind, (rounds, columns, chunk) in zip(parts, plan):
        rows, total, dtype = kind[0][0].shape[0], sum(columns), kind[0][0].dtype
        scratch += [pltpu.VMEM((rows, total), dtype)] * 3
        for name, _ in rounds:
            rows = rows if name == "give" else rows // 2
            scratch.append(pltpu.VMEM((rows, total), dtype))
        scratch += [pltpu.SemaphoreType.DMA((2 * len(rounds), total // chunk))] * 2
    stages = sum(size.bit_length() - 1 for _, size in axes)
    scratch += [
        pltpu.SemaphoreType.DMA((len(flat),)),
        pltpu.SemaphoreType.DMA((len(flat) // 2,)),
        pltpu.VMEM((stages,) + shape, jnp.float32),
        pltpu.SemaphoreType.DMA((stages,)),
        pltpu.SemaphoreType.DMA((stages,)),
    ]
    *out, sums = pl.pallas_call(
        functools.partial(cube_kernel, axes, plan, lines),
        out_shape=[jax.ShapeDtypeStruct(own.shape, own.dtype) for kind in parts for own, _ in kind]
        + [jax.ShapeDtypeStruct(shape, jnp.float32)],
        in_specs=[pl.BlockSpec(memory_space=pl.ANY)] * len(flat)
        + [pl.BlockSpec(memory_space=pltpu.VMEM)] * len(small),
        out_specs=[pl.BlockSpec(memory_space=pl.ANY)] * (len(flat) // 2)
        + [pl.BlockSpec(memory_space=pltpu.VMEM)],
        scratch_shapes=scratch,
        compiler_params=pltpu.CompilerParams(
            collective_id=collective_id, has_side_effects=True, vmem_limit_bytes=60 * 2**20
        ),
    )(*flat, *small)
    result = []
    for kind in parts:
        result.append(out[: len(kind)])
        out = out[len(kind) :]
    return result, sums


class Groups:
    def __init__(self, axes):
        self.axes = axes
        self.size = dict(axes)["dp"]
        self.me = lax.axis_index("dp")
        bits = [1 << k for k in range(self.size.bit_length() - 1)]
        self.plain = any(size & (size - 1) for _, size in axes) or not bits
        first, rest = bits[:3], bits[3:]
        self.orders = [[1]] * 4
        if first:
            one, two, three = first[0], first[1 % len(first)], first[2 % len(first)]
            orders = (
                (one, two, three, *rest),
                (two, one, three, *rest),
                (three, one, two, *rest),
                (three, two, one, *rest),
            )
            self.orders = [list(dict.fromkeys(order)) for order in orders]
        self.kinds = range(len(self.orders))
        self.line = tuple(bits[-2:]) if len(bits) > 3 else ()

    def swap(self, values, bit):
        return lax.ppermute(values, "dp", [(j, j ^ bit) for j in range(self.size)])

    def upper(self, bit):
        return lax.rem(self.me // bit, 2)

    def in_order(self, bit, mine, other):
        low = self.upper(bit) == 0
        return jnp.concatenate([jnp.where(low, mine, other), jnp.where(low, other, mine)], axis=0)

    def along(self, jobs, call, **arguments):
        bits = [order[0] for order in self.orders]
        lefts = jobs[0][0]
        if self.plain or lefts[0].shape[1] // len(lefts) % 256:
            results, received, _ = call(**arguments)
            jobs = [
                (lefts, [results[rights], *received[0]] if isinstance(rights, int) else rights, *rest)
                for lefts, rights, *rest in jobs
            ]
            pairs = {
                key: (keep, give if self.plain else self.swap(give, bits[key[1]]))
                for key, (give, keep) in halves_plainly(jobs, bits).items()
            }
        else:
            results, received, pairs = call(**arguments, jobs=jobs, bits=bits)
        bundles = {}
        for (bundle, kind), pair in pairs.items():
            bundles.setdefault(bundle, {})[kind] = pair
        return results, received, bundles

    def middle(self, parts, small, lines, width, collective_id):
        if self.plain:
            sums = self.stacked(small, lines, width)
            return parts, lax.psum(sums, tuple(name for name, _ in self.axes))
        plan, fits = [], True
        for order, arrays in zip(self.orders, parts):
            columns = tuple(own.shape[1] for own, _ in arrays)
            blocks = sum(columns) // 128
            chunk = 512 if blocks >= 48 else 256
            plan.append((cube_rounds(order[1:], self.line), columns, chunk))
            fits &= all(count % chunk == 0 for count in columns)
            fits &= (arrays[0][0].shape[0] >> len(order[1:])) % 16 == 0 and len(order) > 1
        if fits:
            return sum_cube(self.axes, parts, plan, small, lines, width, collective_id)
        sums = [
            [self.rounds(order[1:], own, other) for own, other in arrays]
            for order, arrays in zip(self.orders, parts)
        ]
        small = self.stacked(small, lines, width)
        return sums, sum_and_share(None, self.axes, small, small.shape[0], [], collective_id)[0]

    def stacked(self, small, lines, width):
        rows = [
            jnp.pad(array[row], (0, width - array.shape[1]))
            for array, picked in zip(small, lines)
            for row in picked
        ]
        return eight_lines(*rows)

    def rounds(self, bits, own, other):
        total = (own.astype(jnp.float32) + other.astype(jnp.float32)).astype(jnp.bfloat16)
        for bit in bits:
            count = total.shape[0] // 2
            given = lax.dynamic_slice_in_dim(total, (1 - self.upper(bit)) * count, count, axis=0)
            mine = lax.dynamic_slice_in_dim(total, self.upper(bit) * count, count, axis=0)
            other = self.swap(given, bit)
            total = (mine.astype(jnp.float32) + other.astype(jnp.float32)).astype(jnp.bfloat16)
        for bit in reversed(bits):
            total = self.in_order(bit, total, self.swap(total, bit))
        return total

    def finish(self, bundle):
        if self.plain:
            return {kind: (self.orders[kind][0], *pair) for kind, pair in bundle.items()}
        return {
            kind: (self.orders[kind][0], total, self.swap(total, self.orders[kind][0]))
            for kind, total in bundle.items()
        }

    def join(self, *parts):
        if self.plain:
            return jnp.concatenate(
                [
                    lax.psum(
                        self.in_order(*halves)[:, first : first + columns].astype(jnp.float32),
                        "dp",
                    )
                    for halves, first, columns in parts
                ],
                axis=1,
            )
        return join([(*halves, first, columns) for halves, first, columns in parts])


class Flow:
    def __init__(self, sources, held, in_sems, results, staged, out_sems, chunks):
        self.sources, self.held, self.in_sems = sources, held, in_sems
        self.results, self.staged, self.out_sems = results, staged, out_sems
        self.chunks = chunks
        self.sent, self.shared = [], []

    def copy_in(self, index, part):
        width = self.chunks[index]
        columns = pl.ds(part * width, width)
        first = sum(
            source.shape[1] // chunk for source, chunk in zip(self.sources[:index], self.chunks)
        )
        return pltpu.make_async_copy(
            self.sources[index].at[:, columns],
            self.held[index].at[:, columns],
            self.in_sems.at[first + part],
        )

    def start(self, order):
        for index, part in order:
            self.copy_in(index, part).start()

    def pulls(self, held, outs, sems, small):
        self.pull_held, self.pull_outs, self.pull_sems, self.pull_small = held, outs, sems, small
        self.pull_slots, self.pulled = {}, []

    def push(self, order):
        me = lax.axis_index("fsdp")
        for own, places in self.pull_small:
            for step, peer in enumerate(self.peers):
                self.push_one(("small", id(places)), 0, step, peer, own, places[step])
        for index, part in order:
            if index in self.pull_held:
                columns = pl.ds(part * self.chunks[index], self.chunks[index])
                for step, peer in enumerate(self.peers):
                    target = self.pull_held[index][step].at[:, columns]
                    source = self.sources[index].at[:, columns]
                    self.push_one(index, part, step, peer, source, target)

    def carry(self, sources, modes, outs, sems):
        for index, (source, mode) in enumerate(zip(sources, modes)):
            for step, peer in enumerate(self.peers):
                given = source
                if mode == "columns":
                    width = source.shape[1] // self.size
                    given = source.at[:, pl.ds(pl.multiple_of(peer * width, width), width)]
                copy = pltpu.make_async_remote_copy(
                    src_ref=given,
                    dst_ref=outs[index][step],
                    send_sem=sems[0].at[index, step],
                    recv_sem=sems[1].at[index, step],
                    device_id={"fsdp": peer},
                    device_id_type=pl.DeviceIdType.MESH,
                )
                copy.start()
                self.shared.append(copy)

    def push_one(self, index, part, step, peer, source, target):
        send_sems, recv_sems, _ = self.pull_sems
        slot = len(self.pull_slots)
        copy = pltpu.make_async_remote_copy(
            src_ref=source,
            dst_ref=target,
            send_sem=send_sems.at[slot],
            recv_sem=recv_sems.at[slot],
            device_id={"fsdp": peer},
            device_id_type=pl.DeviceIdType.MESH,
        )
        self.pull_slots[index, part, step] = (slot, copy)
        copy.start()

    def take_small(self, places):
        for step in range(len(self.peers)):
            self.pull_slots[("small", id(places)), 0, step][1].wait_recv()
        return places

    def take_all(self, index, part=0):
        blocks = [self.take(index, part)]
        width = self.chunks[index]
        columns = pl.ds(part * width, width)
        for step in range(len(self.peers)):
            slot, copy = self.pull_slots[index, part, step]
            copy.wait_recv()
            block = self.pull_held[index][step].at[:, columns]
            blocks.append(block)
            if not self.pull_outs:
                continue
            out = pltpu.make_async_copy(
                block, self.pull_outs[index][step].at[:, columns], self.pull_sems[2].at[slot]
            )
            out.start()
            self.pulled.append(out)
        return blocks

    def held_all(self, index, part):
        columns = pl.ds(part * self.chunks[index], self.chunks[index])
        return [block.at[:, columns] for block in [self.held[index], *self.pull_held[index]]]

    def take(self, index, part=0):
        self.copy_in(index, part).wait()
        width = self.chunks[index]
        return self.held[index].at[:, pl.ds(part * width, width)]

    def put(self, index, columns=None):
        columns = slice(None) if columns is None else columns
        copy = pltpu.make_async_copy(
            self.staged[index].at[:, columns],
            self.results[index].at[:, columns],
            self.out_sems.at[len(self.sent)],
        )
        copy.start()
        self.sent.append(copy)

    def greet(self, shares, outs, sems, size):
        me = lax.axis_index("fsdp")
        self.shares, self.share_outs, self.share_sems, self.size = shares, outs, sems, size
        self.peers = [lax.rem(me + size - step, size) for step in range(1, size)]

    def share(self, index):
        place = list(self.shares).index(index)
        send_sems, recv_sems = self.share_sems
        for step, peer in enumerate(self.peers):
            source = self.staged[index]
            if self.shares[index] == "columns":
                width = source.shape[1] // self.size
                source = source.at[:, pl.ds(pl.multiple_of(peer * width, width), width)]
            copy = pltpu.make_async_remote_copy(
                src_ref=source,
                dst_ref=self.share_outs[place][step],
                send_sem=send_sems.at[place, step],
                recv_sem=recv_sems.at[place, step],
                device_id={"fsdp": peer},
                device_id_type=pl.DeviceIdType.MESH,
            )
            copy.start()
            self.shared.append(copy)

    def wait_shared(self):
        for copy in self.shared:
            copy.wait()
        self.shared = []

    def finish(self):
        for copy in self.sent + self.shared + self.pulled:
            copy.wait()
        for _, copy in self.pull_slots.values():
            copy.wait_send()


class Grads:
    AHEAD = 6

    def __init__(self, plan, lefts, rights, outs, lefts_held, scratch):
        self.steps, self.bits, self.count, self.tile = plan
        self.lefts, self.rights, self.outs, self.lefts_held = lefts, rights, outs, lefts_held
        self.rights_held, self.staged, *sems = scratch
        self.left_sems, self.right_sems, self.out_sems, self.send_sems, self.recv_sems = sems
        self.frames, self.rows = lefts[0][0].shape[0], self.staged.shape[0]
        self.half = self.rows // 2
        self.me = lax.axis_index("dp")

    def partners(self):
        bits = sorted({self.bits[step[3][1]] for step in self.steps})
        return [{"dp": self.me + bit * (1 - 2 * lax.rem(self.me // bit, 2))} for bit in bits]

    def left_in(self, group, place):
        source = self.lefts[group][place]
        return pltpu.make_async_copy(
            source.at[:, own_columns(self.count, 0, self.rows)] if place == 0 else source,
            self.lefts_held[group].at[pl.ds(place * self.frames, self.frames)],
            self.left_sems.at[group, place],
        )

    def right_in(self, index, place):
        _, right, first, _, _ = self.steps[index]
        return pltpu.make_async_copy(
            self.rights[right][place].at[:, pl.ds(first, self.tile)],
            self.rights_held.at[index % self.AHEAD, pl.ds(place * self.frames, self.frames)],
            self.right_sems.at[index, place],
        )

    def halves_out(self, index):
        _, _, _, key, start = self.steps[index]
        bit = self.bits[key[1]]
        upper = lax.rem(self.me // bit, 2)
        source, columns = [
            self.staged.at[
                pl.ds(pl.multiple_of(part * self.half, self.half), self.half),
                pl.ds(index * self.tile, self.tile),
            ]
            for part in (1 - upper, upper)
        ], pl.ds(start, self.tile)
        keep, recv = self.outs[key]
        return (
            pltpu.make_async_remote_copy(
                src_ref=source[0],
                dst_ref=recv.at[:, columns],
                send_sem=self.send_sems.at[index],
                recv_sem=self.recv_sems.at[index],
                device_id={"dp": self.me + bit * (1 - 2 * upper)},
                device_id_type=pl.DeviceIdType.MESH,
            ),
            pltpu.make_async_copy(source[1], keep.at[:, columns], self.out_sems.at[index]),
        )

    def begin(self, first, last):
        self.first, self.last, self.loaded = first, last, set()
        for index in range(first, min(first + self.AHEAD, last)):
            self.load(index)

    def load(self, index):
        group = self.steps[index][0]
        for place in range(self.count):
            if group not in self.loaded:
                self.left_in(group, place).start()
            self.right_in(index, place).start()
        self.loaded.add(group)

    def run(self, then):
        waited = set()
        for index in range(self.first, self.last):
            step = self.steps[index]
            for place in range(self.count):
                if step[0] not in waited:
                    self.left_in(step[0], place).wait()
                self.right_in(index, place).wait()
            waited.add(step[0])
            right = self.rights_held[index % self.AHEAD]
            product = dot_down(self.lefts_held[step[0]][...], right)
            self.staged[:, pl.ds(index * self.tile, self.tile)] = product.astype(jnp.bfloat16)
            for copy in self.halves_out(index):
                copy.start()
            if index + self.AHEAD < self.last:
                self.load(index + self.AHEAD)
            if index == max(self.last - self.AHEAD - 1, self.first):
                then()

    def finish(self):
        for index in range(len(self.steps)):
            for copy in self.halves_out(index):
                copy.wait()


def gradient_plan(jobs, tile, spread):
    lefts, rights, steps, totals = [], [], [], {}
    for job_lefts, job_rights, first, columns, key in jobs:
        for known, group in ((lefts, job_lefts), (rights, job_rights)):
            if not any(group is other for other in known):
                known.append(group)
        left = [group is job_lefts for group in lefts].index(True)
        right = [group is job_rights for group in rights].index(True)
        for start in range(0, columns, tile):
            steps.append((left, right, first + start, key, totals.setdefault(key, 0)))
            totals[key] += tile
    turns = {key: 0 for key in totals}
    ranks = []
    for step in steps:
        turns[step[3]] += 1
        ranks.append((turns[step[3]] - 0.5) / (totals[step[3]] // tile))
    late = [isinstance(rights[step[1]], int) for step in steps]
    keys = [(late[k], ranks[k] if spread else k) for k in range(len(steps))]
    steps = [steps[k] for k in sorted(range(len(steps)), key=lambda k: keys[k])]
    return lefts, rights, steps, totals


def fused(
    body,
    small,
    large,
    results,
    order=None,
    scratch=(),
    shares=None,
    size=1,
    collective_id=None,
    jobs=(),
    bits=(),
    pulls=(),
    small_pulls=(),
    carried=(),
    pulls_stay=False,
    spread=False,
):
    shares = {} if shares is None or size == 1 else shares
    chunks = [width for _, width in large]
    parts = [array.shape[1] // width for array, width in large]
    if order is None:
        order = [(index, part) for index, count in enumerate(parts) for part in range(count)]
    share_shapes = [
        (shape if mode == "all" else (shape[0], shape[1] // size), dtype)
        for (shape, dtype), mode in ((results[index], mode) for index, mode in shares.items())
        for _ in range(size - 1)
    ]
    pulls = list(pulls) if size > 1 else []
    pull_shapes = [
        (large[index][0].shape, large[index][0].dtype) for index in pulls for _ in range(size - 1)
    ]
    carried = list(carried) if size > 1 else []
    carry_shapes = [
        (array.shape if mode == "all" else (array.shape[0], array.shape[1] // size), array.dtype)
        for array, mode in carried
        for _ in range(size - 1)
    ]
    pull_count = (sum(parts[index] for index in pulls) + len(small_pulls)) * (size - 1)
    tile = 512
    lefts, rights, steps, totals = gradient_plan(jobs, tile, spread)
    early = len([step for step in steps if not isinstance(rights[step[1]], int)])
    flat = [array for group in lefts + rights if not isinstance(group, int) for array in group]
    half_shapes, grad_scratch = [], []
    if jobs:
        count, frames = len(lefts[0]), lefts[0][0].shape[0]
        rows = lefts[0][0].shape[1] // count
        half_shapes = [
            ((rows // 2, columns), jnp.bfloat16) for columns in totals.values() for _ in range(2)
        ]
        grad_scratch = [pltpu.VMEM((count * frames, rows), jnp.bfloat16) for _ in lefts] + [
            pltpu.VMEM((Grads.AHEAD, count * frames, tile), jnp.bfloat16),
            pltpu.VMEM((rows, len(steps) * tile), jnp.bfloat16),
            pltpu.SemaphoreType.DMA((len(lefts), count)),
            pltpu.SemaphoreType.DMA((len(steps), count)),
        ] + [pltpu.SemaphoreType.DMA((len(steps),))] * 3

    def kernel(*refs):
        refs = list(refs)

        def pick(count):
            picked = refs[:count]
            del refs[:count]
            return picked

        small_refs, sources = pick(len(small)), pick(len(large))
        left_refs = [pick(len(group)) for group in lefts]
        right_refs = [group if isinstance(group, int) else pick(len(group)) for group in rights]
        carry_refs = pick(len(carried))
        outs = pick(len(results))
        share_outs = [pick(size - 1) for _ in shares]
        half_outs = {key: pick(2) for key in totals}
        pull_outs = {} if pulls_stay else {index: pick(size - 1) for index in pulls}
        carry_outs = [pick(size - 1) for _ in carried]
        held, staged, rest = pick(len(large)), pick(len(results)), pick(len(scratch))
        in_sems, out_sems = pick(2)
        share_sems = pick(2) if shares else []
        pull_held = {index: pick(size - 1) for index in pulls}
        pull_small = [(small_refs[index], pick(size - 1)) for index in small_pulls]
        pull_sems = pick(3) if pull_count else []
        carry_sems = pick(2) if carried else []
        flow = Flow(sources, held, in_sems, outs, staged, out_sems, chunks)
        greeted = []
        if jobs:
            plan = (steps, bits, len(lefts[0]), tile)
            for place, group in enumerate(right_refs):
                if isinstance(group, int):
                    others = share_outs[list(shares).index(group)] if shares else []
                    right_refs[place] = [staged[group], *others]
            grads = Grads(plan, left_refs, right_refs, half_outs, pick(len(lefts)), refs)
            grads.begin(0, early)
            greeted = grads.partners()
        flow.greet(shares, share_outs, share_sems, size)
        flow.pulls(pull_held, pull_outs, pull_sems, pull_small)
        if pull_count:
            flow.start(order)
        if shares or pull_count or carried:
            greeted += [{"fsdp": peer} for peer in flow.peers]
        if greeted:
            barrier = pltpu.get_barrier_semaphore()
            for device in greeted:
                pl.semaphore_signal(
                    barrier, inc=1, device_id=device, device_id_type=pl.DeviceIdType.MESH
                )
            pl.semaphore_wait(barrier, len(greeted))
        if carried:
            modes = [mode for _, mode in carried]
            flow.carry(carry_refs, modes, carry_outs, carry_sems)
        if jobs:
            grads.run(functools.partial(flow.start, order))
        elif pull_count:
            flow.push(order)
        else:
            flow.start(order)
        if body is not None:
            body(flow, small_refs, rest)
        if early < len(steps):
            flow.wait_shared()
            grads.begin(early, len(steps))
            grads.run(lambda: None)
        flow.finish()
        if jobs:
            grads.finish()

    semaphores = [
        pltpu.SemaphoreType.DMA((max(sum(parts), 1),)),
        pltpu.SemaphoreType.DMA((64,)),
    ]
    params = dict(vmem_limit_bytes=60 * 2**20)
    if shares:
        semaphores += [pltpu.SemaphoreType.DMA((len(shares), size - 1))] * 2
    pull_scratch = []
    if pull_count:
        pull_scratch = [pltpu.VMEM(shape, dtype) for shape, dtype in pull_shapes] + [
            pltpu.VMEM(small[index].shape, small[index].dtype)
            for index in small_pulls
            for _ in range(size - 1)
        ]
        pull_scratch += [pltpu.SemaphoreType.DMA((pull_count,))] * 3
    if carried:
        pull_scratch += [pltpu.SemaphoreType.DMA((len(carried), size - 1))] * 2
    if shares or jobs or pull_count or carried:
        params.update(collective_id=collective_id, has_side_effects=True)
    pull_results = [] if pulls_stay else pull_shapes
    shapes = results + share_shapes + half_shapes + pull_results + carry_shapes
    out = pl.pallas_call(
        kernel,
        out_shape=[jax.ShapeDtypeStruct(shape, dtype) for shape, dtype in shapes],
        in_specs=[
            pl.BlockSpec(memory_space=pltpu.SMEM if array.dtype == jnp.int32 else pltpu.VMEM)
            for array in small
        ]
        + [pl.BlockSpec(memory_space=pl.ANY)] * (len(large) + len(flat) + len(carried)),
        out_specs=[pl.BlockSpec(memory_space=pl.ANY)] * len(shapes),
        scratch_shapes=[pltpu.VMEM(array.shape, array.dtype) for array, _ in large]
        + [pltpu.VMEM(shape, dtype) for shape, dtype in results]
        + list(scratch)
        + semaphores
        + pull_scratch
        + grad_scratch,
        compiler_params=pltpu.CompilerParams(**params),
    )(*small, *[array for array, _ in large], *flat, *[array for array, _ in carried])
    others = out[len(results) : len(results) + len(share_shapes)]
    received = [others[k * (size - 1) : (k + 1) * (size - 1)] for k in range(len(shares))]
    halves = out[len(results) + len(share_shapes) :]
    others = out[len(shapes) - len(pull_results) - len(carry_shapes) :]
    received += [
        others[k : k + size - 1] for k in range(0, len(others), max(size - 1, 1)) if size > 1
    ]
    return (
        out[: len(results)],
        received or [[] for _ in range(16)],
        {key: (halves[2 * k], halves[2 * k + 1]) for k, key in enumerate(totals)},
    )


def dot(left, right):
    return jnp.dot(left, right, preferred_element_type=jnp.float32)


def dot_across(left, right):
    return lax.dot_general(left, right, ACROSS_DIMS, preferred_element_type=jnp.float32)


def dot_down(left, right):
    return lax.dot_general(left, right, DOWN_DIMS, preferred_element_type=jnp.float32)


def own_columns(size, place, width):
    owner = lax.rem(lax.axis_index("fsdp") + place, size)
    return pl.ds(pl.multiple_of(owner * width, width), width)


def times_blocks(values_ref, blocks):
    total = None
    for place, block in enumerate(blocks):
        columns = own_columns(len(blocks), place, block.shape[0])
        part = dot(values_ref[:, columns], block[...])
        total = part if total is None else total + part
    return total


def add_back(total_ref, values, blocks, scale=None):
    for place, block in enumerate(blocks):
        columns = own_columns(len(blocks), place, block.shape[0])
        part = dot_across(values, block[...])
        total_ref[:, columns] += part if scale is None else scale * part


def centred(values):
    centre = values - jnp.mean(values, axis=-1, keepdims=True)
    spread = jnp.mean(centre * centre, axis=-1, keepdims=True)
    scale = lax.rsqrt(spread + EPSILON)
    return centre * scale, scale


BIAS_LINES = (6, 7, 9, 10, 8, 11)
TAP_LINE = 12


def gain_line(lines_ref, norm):
    return lines_ref[norm : norm + 1, :]


def bias_line(lines_ref, norm):
    return lines_ref[BIAS_LINES[norm] : BIAS_LINES[norm] + 1, :]


def tap_line(lines_ref, tap):
    return lines_ref[TAP_LINE + tap : TAP_LINE + tap + 1, :]


def norm_low(values, lines_ref, norm):
    hat, _ = centred(values)
    return (hat * gain_line(lines_ref, norm) + bias_line(lines_ref, norm)).astype(jnp.bfloat16)


def norm_grad(grad, values, gain_row):
    hat, scale = centred(values)
    inner = grad * gain_row
    first = jnp.mean(inner, axis=-1, keepdims=True)
    second = jnp.mean(inner * hat, axis=-1, keepdims=True)
    return (
        (inner - first - hat * second) * scale,
        jnp.sum(grad * hat, axis=0, keepdims=True),
        jnp.sum(grad, axis=0, keepdims=True),
    )


def put_rows(ref, *lines):
    for place, line in enumerate(lines):
        ref[pl.ds(place, 1), :] = line
    ref[pl.ds(len(lines), ref.shape[0] - len(lines)), :] = jnp.zeros(
        (ref.shape[0] - len(lines), ref.shape[1]), ref.dtype
    )


def segment_of(lengths_ref, places):
    ends = lengths_ref[0, 0]
    segment = (places >= ends).astype(jnp.int32)
    for index in range(1, lengths_ref.shape[1]):
        ends = ends + lengths_ref[0, index]
        segment += (places >= ends).astype(jnp.int32)
    return segment


def frame_marks(lengths_ref, frames, taps=0):
    places = lax.broadcasted_iota(jnp.int32, (frames, 1), 0)
    segment = segment_of(lengths_ref, places)
    valid = (segment < lengths_ref.shape[1]).astype(jnp.float32)
    marks = []
    for tap in range(taps):
        moved = places + (tap - taps // 2)
        same = (segment_of(lengths_ref, moved) == segment) & (moved >= 0) & (moved < frames)
        marks.append(same.astype(jnp.float32))
    return valid, marks


def same_segment(lengths_ref, frames):
    down = segment_of(lengths_ref, lax.broadcasted_iota(jnp.int32, (frames, 1), 0))
    across = segment_of(lengths_ref, lax.broadcasted_iota(jnp.int32, (1, frames), 1))
    return down == across


TILE = 1024


def feed_forward(w_in, w_out, flow, normed_ref, hidden, slope_ref, y_ref):
    inner = slope_ref.shape[1]
    for part in range(inner // TILE):
        columns = pl.ds(part * TILE, TILE)
        before = times_blocks(normed_ref, w_in(part))
        gate = jax.nn.sigmoid(before)
        value = (before * gate).astype(jnp.bfloat16)
        flow.staged[hidden][:, columns] = value
        flow.put(hidden, columns)
        slope_ref[:, columns] = (gate * (1.0 + before * (1.0 - gate))).astype(jnp.bfloat16)
        add_back(y_ref, value, w_out(part), 0.5)


def feed_forward_back(blocks_in, blocks_out, low_ref, slope_ref, flow, result, normed_ref):
    inner = slope_ref.shape[1]
    normed_ref[...] = jnp.zeros_like(normed_ref)
    for part in range(inner // TILE):
        columns = pl.ds(part * TILE, TILE)
        grad = times_blocks(low_ref, blocks_out(part)) * slope_ref[:, columns].astype(jnp.float32)
        grad = grad.astype(jnp.bfloat16)
        flow.staged[result][:, columns] = grad
        flow.put(result, columns)
        add_back(normed_ref, grad, blocks_in(part))


def head_scores(query, key, bias_row, same, scale):
    frames = query.shape[0]
    spread = jnp.broadcast_to(bias_row, (frames, bias_row.shape[1]))
    relative = pltpu.roll(spread, 0, 1, stride=1, stride_axis=0)[:, :frames]
    return jnp.where(same, dot_across(query, key) * scale + relative, MASKED)


def softmax_rows(scores):
    powers = jnp.exp(scores - jnp.max(scores, axis=-1, keepdims=True))
    return powers / jnp.sum(powers, axis=-1, keepdims=True)


def split(items, count):
    items = list(items)
    return [items[k : k + count] for k in range(0, len(items), count)]


def front(
    x, own_lines, own_bias, lengths, heads, taps, weights, size, collective_id
):
    frames, width = x.shape
    inner = weights[0].shape[1]
    head = width // heads
    small = [own_lines, own_bias, lengths]
    large = [(x, width)]
    large += [(block, TILE) for block in weights[:2]] + [(block, width) for block in weights[2:]]
    order = [(0, 0)]
    order += [(index, part) for part in range(inner // TILE) for index in (1, 2)]
    order += [(3, part) for part in range(3)] + [(4, 0), (5, 1), (5, 0)]
    low, full = jnp.bfloat16, jnp.float32
    results = [
        ((frames, width), low),
        ((frames, inner), low),
        ((frames, inner), low),
        ((frames, width), full),
        ((frames, width), low),
        ((frames, width), low),
        ((frames, width), low),
        ((frames, width), low),
        ((frames, width), low),
        ((frames, width), full),
        ((frames, width), low),
        ((frames, width), full),
        ((frames, width), full),
        ((frames, width), full),
        ((8, width), full),
        ((own_lines.shape[0], width), full),
        ((-(-heads // 8) * 8, own_bias.shape[1]), full),
    ]

    def body(flow, small_refs, _):
        own_lines_ref, own_bias_ref, lengths_ref = small_refs
        valid, marks = frame_marks(lengths_ref, frames, taps)
        (
            normed_one,
            hidden,
            slope,
            x1,
            normed_attn,
            query_ref,
            key_ref,
            value_ref,
            context,
            x2,
            normed_conv,
            gated_ref,
            gate_ref,
            mixed_ref,
            sums_ref,
            lines_ref,
            bias_ref,
        ) = flow.staged
        small_places = [places for _, places in flow.pull_small]
        blocks = [own_lines_ref] + (flow.take_small(small_places[0]) if size > 1 else [])
        for place, block in enumerate(blocks):
            lines_ref[:, own_columns(size, place, block.shape[1])] = block[...]
        flow.put(15)
        blocks = [own_bias_ref] + (flow.take_small(small_places[1]) if size > 1 else [])
        for place, block in enumerate(blocks):
            owner = lax.rem(lax.axis_index("fsdp") + place, size)
            for row in range(heads // size):
                bias_ref[pl.ds(owner * (heads // size) + row, 1), :] = block[row : row + 1, :]
        flow.put(16)
        values = flow.take(0)[...].astype(jnp.float32)
        normed_one[...] = norm_low(values, lines_ref, 0)
        flow.put(0)
        x1[...] = values
        feed_forward(
            lambda part: flow.take_all(1, part),
            lambda part: flow.take_all(2, part),
            flow,
            normed_one,
            1,
            slope,
            x1,
        )
        flow.put(2)
        flow.put(3)

        normed_attn[...] = norm_low(x1[...], lines_ref, 1)
        flow.put(4)
        for part, ref in enumerate((query_ref, key_ref, value_ref)):
            ref[...] = times_blocks(normed_attn, flow.take_all(3, part)).astype(jnp.bfloat16)
            flow.put(5 + part)
        same = same_segment(lengths_ref, frames)
        for place in range(heads):
            columns = slice(place * head, (place + 1) * head)
            scores = head_scores(
                query_ref[:, columns],
                key_ref[:, columns],
                bias_ref[place : place + 1, :],
                same,
                head**-0.5,
            )
            attend = softmax_rows(scores).astype(jnp.bfloat16)
            context[:, columns] = dot(attend, value_ref[:, columns]).astype(jnp.bfloat16)
        flow.put(8)
        x2[...] = x1[...] + times_blocks(context, flow.take_all(4))
        flow.put(9)

        normed_conv[...] = norm_low(x2[...], lines_ref, 2)
        flow.put(10)
        gate = jax.nn.sigmoid(times_blocks(normed_conv, flow.take_all(5, 1)))
        gate_ref[...] = gate
        flow.put(12)
        gated_ref[...] = times_blocks(normed_conv, flow.take_all(5, 0)) * gate
        flow.put(11)
        mixed = jnp.zeros((frames, width), jnp.float32)
        for tap in range(taps):
            offset = tap - taps // 2
            gated = gated_ref[...]
            moved = gated if offset == 0 else pltpu.roll(gated, -offset % frames, 0)
            mixed += tap_line(lines_ref, tap) * (moved * marks[tap])
        mixed_ref[...] = mixed
        flow.put(13)
        weighted = valid * mixed
        put_rows(
            sums_ref,
            jnp.sum(weighted, axis=0, keepdims=True),
            jnp.sum(weighted * mixed, axis=0, keepdims=True),
            jnp.broadcast_to(jnp.sum(valid, axis=0, keepdims=True), (1, width)),
        )
        flow.put(14)

    results, pulled, _ = fused(
        body,
        small,
        large,
        results,
        order,
        size=size,
        collective_id=collective_id,
        pulls=range(1, 6),
        small_pulls=(0, 1),
    )
    return results, [[own, *others] for own, others in zip(weights, pulled)]


def batch_stats(totals_ref):
    count = totals_ref[2:3, :]
    mean = totals_ref[0:1, :] / count
    rstd = lax.rsqrt(totals_ref[1:2, :] / count - mean * mean + EPSILON)
    return count, mean, rstd


def turn(x, mixed, totals, cotangent, lengths, lines, w_conv, w_in, w_out, size, collective_id):
    frames, width = x.shape
    inner = w_in.shape[1]
    small = [totals, lengths, lines]
    large = [(mixed, width), (x, width), (w_conv, width), (w_in, TILE), (w_out, TILE)]
    large += [(cotangent, width)]
    order = [(0, 0), (1, 0), (2, 0)]
    order += [(index, part) for part in range(inner // TILE) for index in (3, 4)]
    order += [(5, 0)]
    low, full = jnp.bfloat16, jnp.float32
    results = [
        ((frames, width), low),
        ((frames, width), low),
        ((frames, inner), low),
        ((frames, width), low),
        ((frames, width), low),
        ((frames, inner), low),
        ((frames, width), low),
        ((frames, width), full),
        ((frames, width), full),
        ((8, width), full),
        ((8, width), full),
        ((8, width), full),
    ]
    scratch = [
        pltpu.VMEM((frames, inner), low),
        pltpu.VMEM((frames, width), full),
        pltpu.VMEM((frames, width), full),
        pltpu.VMEM((frames, width), full),
    ]

    def body(flow, small_refs, rest):
        totals_ref, lengths_ref, lines_ref = small_refs
        valid, _ = frame_marks(lengths_ref, frames)
        slope, x3, x4, normed_grad = rest
        (
            swish,
            normed,
            hidden,
            out_ref,
            low_two,
            before,
            low_conv,
            grad_ref,
            hat_grad,
            sums_final,
            sums_two,
            sums_batch,
        ) = flow.staged
        _, mean, rstd = batch_stats(totals_ref)
        mixed_ref = flow.take(0)
        z = (mixed_ref[...] - mean) * rstd * gain_line(lines_ref, 5) + bias_line(lines_ref, 5)
        swish[...] = (z * jax.nn.sigmoid(z)).astype(jnp.bfloat16)
        flow.put(0)
        x2_ref = flow.take(1)
        conv_blocks = flow.take_all(2)
        x3[...] = x2_ref[...] + times_blocks(swish, conv_blocks)
        normed[...] = norm_low(x3[...], lines_ref, 3)
        flow.put(1)
        x4[...] = x3[...]
        feed_forward(
            functools.partial(flow.take_all, 3),
            functools.partial(flow.take_all, 4),
            flow,
            normed,
            2,
            slope,
            x4,
        )
        if size > 1:
            for index in (2, 1, 0):
                flow.share(index)

        gain_row = gain_line(lines_ref, 4)
        hat, _ = centred(x4[...])
        out_ref[...] = (valid * (hat * gain_row + bias_line(lines_ref, 4))).astype(jnp.bfloat16)
        flow.put(3)
        grad = valid * flow.take(len(large) - 1)[...].astype(jnp.float32)
        grad_values, grad_gain, grad_bias = norm_grad(grad, x4[...], gain_row)
        grad_ref[...] = grad_values
        low_two[...] = (0.5 * grad_values).astype(jnp.bfloat16)
        flow.put(4)
        if size > 1:
            flow.share(4)
        put_rows(sums_final, grad_gain, grad_bias)
        flow.put(9)

        feed_forward_back(
            functools.partial(flow.held_all, 3),
            functools.partial(flow.held_all, 4),
            low_two,
            slope,
            flow,
            5,
            normed_grad,
        )
        if size > 1:
            flow.share(5)
        branch, grad_gain, grad_bias = norm_grad(
            normed_grad[...], x3[...], gain_line(lines_ref, 3)
        )
        total = grad_ref[...] + branch
        grad_ref[...] = total
        flow.put(7)
        low_conv[...] = total.astype(jnp.bfloat16)
        flow.put(6)
        if size > 1:
            flow.share(6)
        put_rows(sums_two, grad_gain, grad_bias)
        flow.put(10)

        for place, block in enumerate(conv_blocks):
            columns = own_columns(size, place, block.shape[0])
            hat_grad[:, columns] = dot_across(low_conv[...], block[...])
        hat = (mixed_ref[...] - mean) * rstd
        gain_row = gain_line(lines_ref, 5)
        z = hat * gain_row + bias_line(lines_ref, 5)
        gate = jax.nn.sigmoid(z)
        grad_z = hat_grad[...] * gate * (1.0 + z * (1.0 - gate))
        grad_hat = grad_z * gain_row
        hat_grad[...] = grad_hat
        flow.put(8)
        put_rows(
            sums_batch,
            jnp.sum(grad_hat, axis=0, keepdims=True),
            jnp.sum(grad_hat * hat, axis=0, keepdims=True),
            jnp.sum(grad_z * hat, axis=0, keepdims=True),
            jnp.sum(grad_z, axis=0, keepdims=True),
        )
        flow.put(11)

    return fused(
        body,
        small,
        large,
        results,
        order,
        scratch,
        shares={0: "columns", 1: "columns", 2: "all", 4: "columns", 5: "all", 6: "all"},
        size=size,
        collective_id=collective_id,
        pulls=(2, 3, 4),
        pulls_stay=True,
    )[:2]


def back_front(
    hat_grad,
    gated,
    gate,
    mixed,
    totals,
    back,
    grad,
    x2,
    x1,
    lines,
    bias_table,
    lengths,
    taps,
    packed,
    w_conv,
    w_out,
    w_qkv,
    collective_id,
    **jobs,
):
    frames, width = x1.shape
    count = len(w_conv)
    heads = bias_table.shape[0]
    head = width // heads
    flip = (
        jnp.arange(frames)[:, None] + jnp.arange(frames)[None, :] == frames - 1
    ).astype(jnp.bfloat16)
    small = [totals, back, lengths, lines, bias_table, flip]
    large = [(array, width) for array in (hat_grad, mixed, gated, gate)]
    large += [(block, width) for block in w_conv]
    large += [(array, width) for array in (x2, grad)]
    large += [(block, width) for block in w_out]
    large += [(array, width) for array in packed]
    large += [(block, width) for block in w_qkv]
    large += [(x1, width)]
    conv = list(range(4, 4 + count))
    place_x2 = 4 + count
    out = list(range(place_x2 + 2, place_x2 + 2 + count))
    place_packed = out[-1] + 1
    qkv = list(range(place_packed + 3, place_packed + 3 + count))
    order = None
    low, full = jnp.bfloat16, jnp.float32
    results = [((frames, width), low)] * 7 + [((frames, width), full)]
    results += [((8, width), full)] * 3 + [(bias_table.shape, full)]
    scratch = [
        pltpu.VMEM((frames, width), full),
        pltpu.VMEM((frames, width), full),
        pltpu.VMEM((frames, width), low),
    ]

    def body(flow, small_refs, rest):
        (
            totals_ref,
            back_ref,
            lengths_ref,
            lines_ref,
            bias_ref,
            flip_ref,
        ) = small_refs
        valid, marks = frame_marks(lengths_ref, frames, taps)
        normed_grad, grad_mixed_ref, grad_context = rest
        one, two, low_attn, *grad_refs = flow.staged[:6]
        low_one, grad_ref, sums_kernel, sums_conv, sums_attn, sums_rel = flow.staged[6:]
        valid_count, mean, rstd = batch_stats(totals_ref)
        grad_var = -0.5 * rstd * rstd * back_ref[1:2, :]
        grad_mean = -rstd * back_ref[0:1, :] - 2.0 * mean * grad_var
        hat_ref, mixed_ref = flow.take(0), flow.take(1)
        grad_mixed_ref[...] = (
            hat_ref[...] * rstd
            + valid * (grad_mean + 2.0 * mixed_ref[...] * grad_var) / valid_count
        )
        gated_ref = flow.take(2)
        normed_grad[...] = jnp.zeros_like(normed_grad)
        kernel_grads = []
        for tap in range(taps):
            offset = tap - taps // 2
            masked = grad_mixed_ref[...] * marks[tap]
            gated = gated_ref[...]
            moved = gated if offset == 0 else pltpu.roll(gated, -offset % frames, 0)
            kernel_grads.append(jnp.sum(masked * moved, axis=0, keepdims=True))
            moved = masked if offset == 0 else pltpu.roll(masked, offset % frames, 0)
            normed_grad[...] += tap_line(lines_ref, tap) * moved
        put_rows(sums_kernel, *kernel_grads)
        flow.put(8)
        gate_now = flow.take(3)[...]
        grad_gated = normed_grad[...]
        one[...] = (grad_gated * gate_now).astype(jnp.bfloat16)
        flow.put(0)
        if count > 1:
            flow.share(0)
        two[...] = (grad_gated * gated_ref[...] * (1.0 - gate_now)).astype(jnp.bfloat16)
        flow.put(1)
        if count > 1:
            flow.share(1)
        normed_grad[...] = jnp.zeros_like(normed_grad)
        for part, ref in enumerate((one, two)):
            add_back(normed_grad, ref[...], [flow.take(index, part) for index in conv])
        branch, grad_gain, grad_bias = norm_grad(
            normed_grad[...], flow.take(place_x2)[...], gain_line(lines_ref, 2)
        )
        total = flow.take(place_x2 + 1)[...] + branch
        grad_ref[...] = total
        low_attn[...] = total.astype(jnp.bfloat16)
        flow.put(2)
        if count > 1:
            flow.share(2)
        put_rows(sums_conv, grad_gain, grad_bias)
        flow.put(9)

        for place, index in enumerate(out):
            block = flow.take(index)
            columns = own_columns(count, place, block.shape[0])
            grad_context[:, columns] = dot_across(low_attn[...], block[...]).astype(jnp.bfloat16)
        packed_refs = [flow.take(place_packed + part) for part in range(3)]
        same = same_segment(lengths_ref, frames)
        scale = head**-0.5
        reach = bias_ref.shape[1]
        for place in range(heads):
            columns = slice(place * head, (place + 1) * head)
            query, key, value = (ref[:, columns] for ref in packed_refs)
            bias_row = bias_ref[place : place + 1, :]
            attend = softmax_rows(head_scores(query, key, bias_row, same, scale))
            context = grad_context[:, columns]
            grad_attend = dot_across(context, value)
            grad_value = dot_down(attend.astype(jnp.bfloat16), context)
            grad_scores = attend * (
                grad_attend - jnp.sum(grad_attend * attend, axis=-1, keepdims=True)
            )
            grad_low = grad_scores.astype(jnp.bfloat16)
            padded = jnp.concatenate(
                [dot(grad_low, flip_ref[...]), jnp.zeros((frames, reach - frames), jnp.float32)],
                axis=1,
            )
            skewed = pltpu.roll(padded, 0, 1, stride=1, stride_axis=0)
            sums_rel[place : place + 1, :] = jnp.sum(skewed, axis=0, keepdims=True)
            grad_query = dot(grad_low, key) * scale
            grad_key = dot_down(grad_low, query) * scale
            for ref, part in zip(grad_refs, (grad_query, grad_key, grad_value)):
                ref[:, columns] = part.astype(jnp.bfloat16)
        flow.put(11)
        normed_grad[...] = jnp.zeros_like(normed_grad)
        for part, ref in enumerate(grad_refs):
            flow.put(3 + part)
            if count > 1:
                flow.share(3 + part)
            add_back(normed_grad, ref[...], [flow.take(index, part) for index in qkv])
        branch, grad_gain, grad_bias = norm_grad(
            normed_grad[...], flow.take(len(large) - 1)[...], gain_line(lines_ref, 1)
        )
        total = grad_ref[...] + branch
        grad_ref[...] = total
        flow.put(7)
        low_one[...] = (0.5 * total).astype(jnp.bfloat16)
        flow.put(6)
        if count > 1:
            flow.share(6)
        put_rows(sums_attn, grad_gain, grad_bias)
        flow.put(10)

    shares = {0: "all", 1: "all", 2: "all", 3: "all", 4: "all", 5: "all", 6: "columns"}
    return fused(
        body, small, large, results, order, scratch, shares, count, collective_id, **jobs
    )


def back_end(low, grad, x, lines, slope, w_in, w_out, collective_id, **jobs):
    frames, width = x.shape
    inner, count = w_in[0].shape[1], len(w_in)
    large = [(low, width)] + [(block, TILE) for block in w_out + w_in]
    large += [(slope, TILE), (x, width), (grad, width)]
    groups = split(range(1, 1 + 2 * count), count)
    place_slope = 1 + 2 * count
    order = [(0, 0)]
    for part in range(inner // TILE):
        order += [(index, part) for index in groups[0]] + [(place_slope, part)]
        order += [(index, part) for index in groups[1]]
    order += [(place_slope + 1, 0), (place_slope + 2, 0)]
    results = [
        ((frames, inner), jnp.bfloat16),
        ((frames, width), jnp.bfloat16),
        ((8, width), jnp.float32),
    ]

    def body(flow, small_refs, rest):
        (lines_ref,), (normed_grad,) = small_refs, rest
        before, out_ref, sums_ref = flow.staged

        def w_out_part(part):
            blocks = [flow.take(index, part) for index in groups[0]]
            flow.take(place_slope, part)
            return blocks

        def w_in_part(part):
            return [flow.take(index, part) for index in groups[1]]

        feed_forward_back(
            w_in_part, w_out_part, flow.take(0), flow.held[place_slope], flow, 0, normed_grad
        )
        if count > 1:
            flow.share(0)
        values = flow.take(place_slope + 1)[...].astype(jnp.float32)
        branch, grad_gain, grad_bias = norm_grad(normed_grad[...], values, gain_line(lines_ref, 0))
        out_ref[...] = (flow.take(place_slope + 2)[...] + branch).astype(jnp.bfloat16)
        flow.put(1)
        put_rows(sums_ref, grad_gain, grad_bias)
        flow.put(2)

    scratch = [pltpu.VMEM((frames, width), jnp.float32)]
    shares = {0: "all"}
    return fused(
        body, [lines], large, results, order, scratch, shares, count, collective_id, **jobs
    )


def halves_plainly(jobs, bits):
    products = {}
    for lefts, rights, first, columns, key in jobs:
        rows = lefts[0].shape[1] // len(lefts)
        own = lax.dynamic_slice_in_dim(lefts[0], lax.axis_index("fsdp") * rows, rows, axis=1)
        left = jnp.concatenate([own, *lefts[1:]])
        right = jnp.concatenate(rights)[:, first : first + columns]
        products.setdefault(key, []).append(dot_down(left, right).astype(jnp.bfloat16))
    halves = {}
    for key, parts in products.items():
        product = jnp.concatenate(parts, axis=1)
        half = product.shape[0] // 2
        upper = lax.rem(lax.axis_index("dp") // bits[key[1]], 2)
        halves[key] = tuple(
            lax.dynamic_slice_in_dim(product, part * half, half, axis=0)
            for part in (1 - upper, upper)
        )
    return halves


def join_body(bits, counts, *refs):
    step = pl.program_id(0)
    out_ref = refs[-1]
    half = refs[0].shape[0]
    first = 0
    for index, (bit, count) in enumerate(zip(bits, counts)):
        upper = lax.rem(lax.axis_index("dp") // bit, 2)

        @pl.when((step >= first) & (step < first + count))
        def _(index=index, upper=upper):
            for ref, part in zip(refs[2 * index : 2 * index + 2], (upper, 1 - upper)):
                rows = pl.ds(pl.multiple_of(part * half, half), half)
                out_ref[rows, :] = ref[...].astype(jnp.float32)

        first += count


def join(parts, tile=512):
    counts = [columns // tile for _, _, _, _, columns in parts]
    rows = 2 * parts[0][1].shape[0]
    specs, flat, first = [], [], 0
    for (_, mine, other, start, _), count in zip(parts, counts):

        def index(step, first=first, count=count, start=start // tile):
            return (0, start + jnp.clip(step - first, 0, count - 1))

        specs += [pl.BlockSpec((rows // 2, tile), index)] * 2
        flat += [mine, other]
        first += count
    return pl.pallas_call(
        functools.partial(join_body, [part[0] for part in parts], counts),
        grid=(first,),
        out_shape=jax.ShapeDtypeStruct((rows, first * tile), jnp.float32),
        in_specs=specs,
        out_specs=pl.BlockSpec((rows, tile), lambda step: (0, step)),
        compiler_params=pltpu.CompilerParams(vmem_limit_bytes=60 * 2**20),
    )(*flat)


def bias_lines(table, frames):
    heads, middle = table.shape[0], (table.shape[1] - 1) // 2
    half = -(-frames // 64) * 64
    above = jnp.broadcast_to(table[:, -1:], (heads, half - middle - 1))
    below = jnp.broadcast_to(table[:, :1], (heads, half - middle))
    return jnp.concatenate([table[:, middle:], above, below, table[:, :middle]], axis=1)


def bias_lines_back(sums, frames, reach):
    return jnp.concatenate(
        [
            jnp.sum(sums[:, frames - 1 + reach :], axis=1, keepdims=True),
            sums[:, frames - reach : frames - 1 + reach][:, ::-1],
            jnp.sum(sums[:, : frames - reach], axis=1, keepdims=True),
        ],
        axis=1,
    )


def eight_lines(*lines):
    lines = list(lines)
    return jnp.stack(lines + [jnp.zeros_like(lines[0])] * (-len(lines) % 8))


def per_device(
    sizes,
    inputs,
    cotangent,
    lengths,
    ffn1_in,
    ffn1_out,
    attn_qkv,
    attn_out,
    rel_table,
    conv_in,
    depth_kernel,
    conv_out,
    ffn2_in,
    ffn2_out,
    gains,
    biases,
    inner_biases,
):
    dp_size, fsdp_size = sizes
    axes = (("fsdp", fsdp_size), ("dp", dp_size))
    rows = Rows(fsdp_size)
    groups = Groups(axes)
    frames, width = inputs.shape
    taps = depth_kernel.shape[1]

    own_lines = jnp.concatenate([gains, biases, inner_biases, depth_kernel], axis=1)
    own_lines = jnp.pad(own_lines, ((0, 0), (0, -own_lines.shape[1] % 8))).astype(jnp.float32).T
    own_bias = bias_lines(rel_table.astype(jnp.float32), frames)
    own_bias = jnp.pad(own_bias, ((0, -own_bias.shape[0] % 8), (0, 0)))
    heads = rel_table.shape[0] * fsdp_size

    (
        (
            normed_one,
            hidden_one,
            slope_one,
            x1,
            normed_attn,
            *packed,
            context,
            x2,
            normed_conv,
            gated,
            gate,
            mixed,
            sums,
            lines,
            bias_table,
        ),
        (w_ffn1_in, w_ffn1_out, w_qkv, w_attn_out, w_conv_in),
    ) = front(
        inputs,
        own_lines,
        own_bias,
        lengths,
        heads,
        taps,
        (ffn1_in, ffn1_out, attn_qkv, attn_out, conv_in),
        fsdp_size,
        6,
    )
    totals, _ = sum_and_share(rows, axes, sums, 3, [], 0)
    results, shared = turn(
        x2,
        mixed,
        totals,
        cotangent,
        lengths,
        lines,
        conv_out,
        ffn2_in,
        ffn2_out,
        fsdp_size,
        7,
    )
    swish, normed_two, hidden_two, layer_out, low_two, before_two, low_conv = results[:7]
    grad, hat_grad, sums_final, sums_two, sums_batch = results[7:]
    arrays = (swish, normed_two, hidden_two, low_two, before_two, low_conv)
    left_swish, left_normed_two, right_hidden_two, left_low_two, right_before_two, right_low_conv = [
        [own, *others] for own, others in zip(arrays, shared)
    ]
    back, _ = sum_and_share(rows, axes, sums_batch, 2, [], 1)

    inner = hidden_two.shape[1]
    main, half, rest = inner * 3 // 4, inner * 3 // 8, inner // 4
    jobs = [
        (left_low_two, right_hidden_two, 0, main, (0, 0)),
        (left_normed_two, right_before_two, 0, main, (0, 1)),
        (left_low_two, right_hidden_two, main, rest, (0, 2)),
        (left_swish, right_low_conv, 0, width, (0, 2)),
        (left_normed_two, right_before_two, main, rest, (0, 3)),
    ]
    arrays = (normed_conv, context, normed_attn, normed_one)
    results, shared, bundles = groups.along(
        jobs,
        functools.partial(
            back_front,
            hat_grad,
            gated,
            gate,
            mixed,
            totals,
            back,
            grad,
            x2,
            x1,
            lines,
            bias_table,
            lengths,
            taps,
            packed,
            w_conv_in,
            w_attn_out,
            w_qkv,
            3,
            spread=True,
            carried=[(array, "columns") for array in arrays] + [(hidden_one, "all")],
        ),
    )
    two = bundles[0]
    *back_lefts, low_one, grad, sums_kernel, sums_conv, sums_attn, sums_rel = results
    right_one, right_two, right_low_attn, right_q, right_k, right_v, left_low_one = [
        [own, *others] for own, others in zip((*back_lefts, low_one), shared)
    ]
    left_normed_conv, left_context, left_normed_attn, left_normed_one, right_hidden_one = [
        [own, *others] for own, others in zip((*arrays, hidden_one), shared[7:])
    ]

    jobs = [
        (left_normed_conv, right_one, 0, width, (0, 0)),
        (left_normed_conv, right_two, 0, width, (0, 1)),
        (left_context, right_low_attn, 0, width, (0, 3)),
        (left_normed_attn, right_q, 0, width, (0, 0)),
        (left_normed_attn, right_k, 0, width, (0, 1)),
        (left_normed_attn, right_v, 0, width, (0, 3)),
        (left_low_one, right_hidden_one, 0, half, (1, 0)),
        (left_low_one, right_hidden_one, half, half, (1, 1)),
        (left_low_one, right_hidden_one, main, rest, (1, 2)),
        (left_normed_one, 0, 0, half, (2, 0)),
        (left_normed_one, 0, half, half, (2, 1)),
        (left_normed_one, 0, main, rest, (2, 3)),
    ]
    (_, input_grad, sums_one), _, bundles = groups.along(
        jobs,
        functools.partial(
            back_end, low_one, grad, inputs, lines, slope_one, w_ffn1_in, w_ffn1_out, 4
        ),
    )
    mid, out, end = bundles[0], bundles[1], bundles[2]

    bundles = (two, mid, out, end)
    middle, sums = groups.middle(
        [[bundle[kind] for bundle in bundles if kind in bundle] for kind in groups.kinds],
        (
            sums_one,
            sums_attn,
            sums_conv,
            sums_two,
            sums_final,
            sums_batch,
            sums_kernel,
            sums_rel,
        ),
        [(0, 1)] * 5 + [(2, 3), tuple(range(taps)), tuple(range(heads))],
        width,
        2,
    )
    middle = [iter(arrays) for arrays in middle]
    two, mid, out, end = [
        {kind: next(middle[kind]) for kind in groups.kinds if kind in bundle} for bundle in bundles
    ]
    two, mid = groups.finish(two), groups.finish(mid)
    sum_ffn2_out = groups.join((two[0], 0, main), (two[2], 0, rest))
    sum_ffn2_in = groups.join((two[1], 0, main), (two[3], 0, rest))
    sum_conv_out = groups.join((two[2], rest, width))
    out, sum_ffn2_out, sum_conv_out = lax.optimization_barrier((out, sum_ffn2_out, sum_conv_out))
    out = groups.finish(out)
    sum_qkv = groups.join(*[(mid[kind], width, width) for kind in (0, 1, 3)])
    sum_conv_in = groups.join((mid[0], 0, width), (mid[1], 0, width))
    sum_attn_out = groups.join((mid[3], 0, width))
    end, sum_qkv = lax.optimization_barrier((end, sum_qkv))
    end = groups.finish(end)
    sum_ffn1_out = groups.join((out[0], 0, half), (out[1], 0, half), (out[2], 0, rest))
    sum_ffn1_in = groups.join((end[0], 0, half), (end[1], 0, half), (end[3], 0, rest))
    own = lax.dynamic_slice_in_dim(sums, rows.me * gains.shape[0], gains.shape[0], axis=1)
    first = 12 + taps
    rel_sum = lax.dynamic_slice_in_dim(
        sums, first + rows.me * rel_table.shape[0], rel_table.shape[0], axis=0
    )
    rel_sum = bias_lines_back(
        rel_sum[:, : sums_rel.shape[1]], frames, (rel_table.shape[1] - 1) // 2
    )
    return (
        layer_out,
        input_grad,
        sum_ffn1_in,
        sum_ffn1_out,
        sum_qkv,
        sum_attn_out,
        rel_sum,
        sum_conv_in,
        own[12:first].T,
        sum_conv_out,
        sum_ffn2_in,
        sum_ffn2_out,
        own[0:12:2].T,
        jnp.stack([own[1], own[3], own[9]], axis=1),
        jnp.stack([own[5], own[7], own[11]], axis=1),
    )


def solution(mesh):
    frame_spec = P(("dp", "fsdp"), None)
    row_spec = P("fsdp", None)
    sizes = (mesh.shape["dp"], mesh.shape["fsdp"])
    return jax.shard_map(
        functools.partial(per_device, sizes),
        mesh=mesh,
        in_specs=(frame_spec,) * 3 + (row_spec,) * 13,
        out_specs=(frame_spec,) * 2 + (row_spec,) * 13,
        check_vma=False,
    )
```

```python
import functools

import jax
import jax.numpy as jnp
from jax import lax
from jax.experimental import pallas as pl
from jax.experimental.pallas import tpu as pltpu
from jax.sharding import PartitionSpec as P

EPSILON = 1e-05
MASKED = -1000000000.0
AHEAD = 4
DOWN_DIMS = (((0,), (0,)), ((), ()))
ACROSS_DIMS = (((1,), (1,)), ((), ()))


def pair_partners(axes):
    partners = []
    for name, size in axes:
        me = lax.axis_index(name)
        bit = 1
        while bit < size:
            partners.append({name: me + bit * (1 - 2 * ((me // bit) % 2))})
            bit *= 2
    return partners


def sum_stages(axes):
    near = [(name, 1 << k) for name, size in axes for k in range(size.bit_length() - 1)]
    stages = []
    while near:
        count = 3 if len(near) in (3, 5) or len(near) > 6 else 2
        stages.append(near[:count])
        near = near[count:]
    return stages


def stage_partners(bits):
    uppers = [lax.rem(lax.axis_index(name) // bit, 2) for name, bit in bits]
    place = sum(upper << k for k, upper in enumerate(uppers))
    devices = []
    for other in range(1 << len(bits)):
        device = {}
        for k, (name, bit) in enumerate(bits):
            start = device.get(name, lax.axis_index(name))
            device[name] = start + bit * (((other >> k) & 1) - uppers[k])
        devices.append(device)
    return place, devices


def pair_kernel(axes, modes, lines, *refs):
    refs = list(refs)

    def pick(count):
        picked = refs[:count]
        del refs[:count]
        return picked

    size = dict(axes)["fsdp"]
    (x_ref,), shared, (o_ref,) = pick(1), pick(len(modes)), pick(1)
    outs = [pick(size - 1) for _ in modes]
    slots, packed, send_sems, recv_sems, share_send, share_recv = refs
    tiles = x_ref.shape[1] // 128

    def lanes(index):
        return pl.ds(index // tiles, 1), pl.ds(index % tiles * 128, 128)

    stages = [stage_partners(bits) for bits in sum_stages(axes)]
    me = lax.axis_index("fsdp")
    peers = [{"fsdp": lax.rem(me + size - step, size)} for step in range(1, size)]
    barrier = pltpu.get_barrier_semaphore()
    greeted = 0
    for place, devices in stages:
        for other, device in enumerate(devices):

            @pl.when(other != place)
            def _(device=device):
                pl.semaphore_signal(
                    barrier, inc=1, device_id=device, device_id_type=pl.DeviceIdType.MESH
                )

        greeted += len(devices) - 1
    if modes and size > 2:
        for peer in peers:
            pl.semaphore_signal(barrier, inc=1, device_id=peer, device_id_type=pl.DeviceIdType.MESH)
        greeted += size - 1
    pl.semaphore_wait(barrier, greeted)
    copies = []
    for index, (mode, source) in enumerate(zip(modes, shared)):
        for step, peer in enumerate(peers):
            if mode == "columns":
                width = source.shape[1] // size
                start = pl.multiple_of(peer["fsdp"] * width, width)
                source_now = source.at[:, pl.ds(start, width)]
            else:
                source_now = source
            copies.append(
                pltpu.make_async_remote_copy(
                    src_ref=source_now,
                    dst_ref=outs[index][step],
                    send_sem=share_send.at[index, step],
                    recv_sem=share_recv.at[index, step],
                    device_id=peer,
                    device_id_type=pl.DeviceIdType.MESH,
                )
            )
    for index in range(packed.shape[0]):
        row, columns = lanes(index)
        packed[pl.ds(index, 1), :] = x_ref[row, columns]
    for stage, (place, devices) in enumerate(stages):

        def exchange(other, device, stage=stage, place=place):
            return pltpu.make_async_remote_copy(
                src_ref=packed,
                dst_ref=slots.at[stage, place],
                send_sem=send_sems.at[stage, other],
                recv_sem=recv_sems.at[stage, place],
                device_id=device,
                device_id_type=pl.DeviceIdType.MESH,
            )

        def arrival(other, device, stage=stage):
            return pltpu.make_async_remote_copy(
                src_ref=packed,
                dst_ref=slots.at[stage, other],
                send_sem=send_sems.at[stage, other],
                recv_sem=recv_sems.at[stage, other],
                device_id=device,
                device_id_type=pl.DeviceIdType.MESH,
            )

        for other, device in enumerate(devices):
            pl.when(other != place)(exchange(other, device).start)
        if stage == 0:
            for copy in copies:
                copy.start()
        for other, device in enumerate(devices):
            pl.when(other != place)(arrival(other, device).wait)
        slots[stage, pl.ds(place, 1)] = packed[...][None]
        total = slots[stage, 0]
        for other in range(1, len(devices)):
            total += slots[stage, other]
        packed[...] = total
    o_ref[...] = jnp.zeros_like(o_ref)
    for index in range(packed.shape[0]):
        row, columns = lanes(index)
        o_ref[row, columns] = packed[pl.ds(index, 1), :]
    for copy in copies:
        copy.wait()


def sum_and_share(rows, axes, values, lines, shared, collective_id):
    size = dict(axes)["fsdp"]
    stages = len(sum_stages(axes))
    if any(count & (count - 1) for _, count in axes) or stages == 0:
        total = lax.psum(values, tuple(name for name, _ in axes))
        total = jnp.concatenate([total[:lines], jnp.zeros_like(total[lines:])])
        return total, [
            (rows.all_frames if mode == "all" else rows.all_frames_own_columns)(array)[1:]
            for array, mode in shared
        ]
    packed = (lines * values.shape[1] // 128, 128)
    shapes = [
        array.shape if mode == "all" else (array.shape[0], array.shape[1] // size)
        for array, mode in shared
    ]
    out = pl.pallas_call(
        functools.partial(pair_kernel, axes, [mode for _, mode in shared], lines),
        out_shape=[jax.ShapeDtypeStruct(values.shape, values.dtype)]
        + [
            jax.ShapeDtypeStruct(shape, array.dtype)
            for shape, (array, _) in zip(shapes, shared)
            for _ in range(size - 1)
        ],
        in_specs=[pl.BlockSpec(memory_space=pltpu.VMEM)]
        + [pl.BlockSpec(memory_space=pl.ANY)] * len(shared),
        out_specs=[pl.BlockSpec(memory_space=pltpu.VMEM)]
        + [pl.BlockSpec(memory_space=pl.ANY)] * (len(shared) * (size - 1)),
        scratch_shapes=[
            pltpu.VMEM((stages, 8) + packed, values.dtype),
            pltpu.VMEM(packed, values.dtype),
            pltpu.SemaphoreType.DMA((stages, 8)),
            pltpu.SemaphoreType.DMA((stages, 8)),
            pltpu.SemaphoreType.DMA((max(len(shared), 1), max(size - 1, 1))),
            pltpu.SemaphoreType.DMA((max(len(shared), 1), max(size - 1, 1))),
        ],
        compiler_params=pltpu.CompilerParams(
            collective_id=collective_id, has_side_effects=True, vmem_limit_bytes=60 * 2**20
        ),
    )(values, *[array for array, _ in shared])
    return out[0], [
        out[1 + k * (size - 1) : 1 + (k + 1) * (size - 1)] for k in range(len(shared))
    ]


class Rows:
    def __init__(self, size):
        self.size = size
        self.me = lax.axis_index("fsdp")

    def owner(self, step):
        return lax.rem(self.me + step, self.size)

    def shift(self, values, step):
        return lax.ppermute(
            values, "fsdp", [(j, (j - step) % self.size) for j in range(self.size)]
        )

    def gather(self, block):
        return [(self.me, block)] + [
            (self.owner(step), self.shift(block, step)) for step in range(1, self.size)
        ]

    def columns(self, values, owner):
        width = values.shape[1] // self.size
        return lax.dynamic_slice_in_dim(values, owner * width, width, axis=1)

    def order(self, parts, axis):
        if self.size == 1:
            return parts[0]
        width = parts[0].shape[axis]
        twice = jnp.concatenate(parts + parts, axis=axis)
        start = lax.rem(self.size - self.me, self.size) * width
        return lax.dynamic_slice_in_dim(twice, start, width * self.size, axis=axis)

    def all_frames(self, values):
        return [values] + [self.shift(values, step) for step in range(1, self.size)]

    def all_frames_own_columns(self, values):
        return [self.columns(values, self.me)] + [
            self.shift(self.columns(values, self.owner(self.size - step)), step)
            for step in range(1, self.size)
        ]


def cube_rounds(bits, line):
    swaps = bits[:-2] if line and tuple(bits[-2:]) == line else bits
    rounds = tuple(("swap", bit) for bit in swaps)
    return rounds if swaps == bits else rounds + (("give", line[0]), ("mid", line[0]))


def cube_kernel(axes, plan, lines, *refs):
    me = lax.axis_index("dp")
    refs = list(refs)

    def pick(count):
        picked = refs[:count]
        del refs[:count]
        return picked

    arrays = [len(columns) for _, columns, _ in plan]
    inputs, small_refs = pick(2 * sum(arrays)), pick(len(lines))
    outputs, (small_out,) = pick(sum(arrays)), pick(1)
    kinds, first = [], 0
    for rounds, columns, chunk in plan:
        whole, other, result = pick(3)
        sums = pick(len(rounds))
        send_sems, recv_sems = pick(2)
        rows, start, steps = whole.shape[0], 0, []
        for name, bit in rounds:
            step = dict(name=name, rows=rows, before=start)
            if name == "swap":
                step["upper"] = lax.rem(me // bit, 2)
                step["partner"] = me + bit * (1 - 2 * step["upper"])
                step["sends"] = step["takes"] = None
            else:
                place = lax.rem(me // bit, 4)
                inner = (place == 1) | (place == 2)
                if name == "give":
                    step["partner"] = me + bit * (1 - 2 * lax.rem(place, 2))
                    step["sends"], step["takes"] = jnp.logical_not(inner), inner
                else:
                    step["upper"] = place // 2
                    step["partner"] = me + bit * (1 - 2 * step["upper"])
                    step["sends"] = step["takes"] = inner
            if name != "give":
                rows //= 2
                start = start + step["upper"] * rows
            step["after"] = start
            steps.append(step)
        edges = [sum(columns[:k]) for k in range(len(columns) + 1)]
        kinds.append(
            dict(
                steps=steps,
                columns=columns,
                edges=edges,
                chunk=chunk,
                count=edges[-1] // chunk,
                whole=whole,
                other=other,
                result=result,
                sums=sums,
                send=send_sems,
                recv=recv_sems,
                first=first,
            )
        )
        first += len(columns)
    load_sems, store_sems, slots, small_send, small_recv = refs
    partners = pair_partners(axes)

    def loads(kind, place):
        index = kind["first"] + place
        columns = pl.ds(kind["edges"][place], kind["columns"][place])
        return [
            pltpu.make_async_copy(
                inputs[2 * index + term],
                kind[name].at[:, columns],
                load_sems.at[2 * index + term],
            )
            for term, name in enumerate(("whole", "other"))
        ]

    def store(kind, place):
        index = kind["first"] + place
        columns = pl.ds(kind["edges"][place], kind["columns"][place])
        return pltpu.make_async_copy(
            kind["result"].at[:, columns], outputs[index], store_sems.at[index]
        )

    for place in range(max(arrays)):
        for kind in kinds:
            if place < len(kind["columns"]):
                for copy in loads(kind, place):
                    copy.start()
    small_out[...] = jnp.zeros_like(small_out)
    line = 0
    for ref, rows in zip(small_refs, lines):
        for row in rows:
            small_out[line : line + 1, : ref.shape[1]] = ref[row : row + 1, :]
            line += 1
    barrier = pltpu.get_barrier_semaphore()
    lines = sorted({bit for rounds, _, _ in plan for name, bit in rounds if name == "mid"})
    for partner in partners:
        pl.semaphore_signal(barrier, inc=1, device_id=partner, device_id_type=pl.DeviceIdType.MESH)
    if lines:
        (bit,) = lines
        place = lax.rem(me // bit, 4)
        inner = (place == 1) | (place == 2)

        @pl.when(inner)
        def _():
            pl.semaphore_signal(
                barrier,
                inc=1,
                device_id={"dp": me + bit * (1 - 2 * (place // 2))},
                device_id_type=pl.DeviceIdType.MESH,
            )
            pl.semaphore_wait(barrier, len(partners) + 1)

        @pl.when(jnp.logical_not(inner))
        def _():
            pl.semaphore_wait(barrier, len(partners))

    else:
        pl.semaphore_wait(barrier, len(partners))

    def window(kind, index):
        return pl.ds(pl.multiple_of(index * kind["chunk"], kind["chunk"]), kind["chunk"])

    def aligned(start, rows):
        return pl.ds(start if isinstance(start, int) else pl.multiple_of(start, rows), rows)

    def source(kind, number):
        return kind["whole"] if number == 0 else kind["sums"][number - 1]

    def copy_in(kind, number, index):
        step, columns = kind["steps"][number], window(kind, index)
        rows = step["rows"]
        given = pl.ds(0, rows)
        if step["name"] != "give":
            given = aligned((1 - step["upper"]) * (rows // 2), rows // 2)
        return pltpu.make_async_remote_copy(
            src_ref=source(kind, number).at[given, columns],
            dst_ref=kind["sums"][number].at[:, columns],
            send_sem=kind["send"].at[number, index],
            recv_sem=kind["recv"].at[number, index],
            device_id={"dp": step["partner"]},
            device_id_type=pl.DeviceIdType.MESH,
        )

    def copy_out(kind, number, index):
        step = kind["steps"][number]
        rows = step["rows"] if step["name"] == "give" else step["rows"] // 2
        start = step["before"] if step["name"] == "give" else step["after"]
        block = kind["result"].at[aligned(start, rows), window(kind, index)]
        slot = 2 * len(kind["steps"]) - 1 - number
        return pltpu.make_async_remote_copy(
            src_ref=block,
            dst_ref=block,
            send_sem=kind["send"].at[slot, index],
            recv_sem=kind["recv"].at[slot, index],
            device_id={"dp": step["partner"]},
            device_id_type=pl.DeviceIdType.MESH,
        )

    def when(condition, action):
        if condition is None:
            action()
        else:
            pl.when(condition)(action)

    def end_in(kind, number, index):
        step, columns = kind["steps"][number], window(kind, index)
        copy = copy_in(kind, number, index)
        last = number == len(kind["steps"]) - 1

        def add():
            copy.wait_recv()
            rows = step["rows"]
            kept = pl.ds(0, rows)
            if step["name"] != "give":
                rows //= 2
                kept = aligned(step["upper"] * rows, rows)
            total = (
                source(kind, number)[kept, columns].astype(jnp.float32)
                + kind["sums"][number][:, columns].astype(jnp.float32)
            ).astype(kind["whole"].dtype)
            if last:
                kind["result"][aligned(step["after"], rows), columns] = total
            else:
                kind["sums"][number][:, columns] = total

        when(step["sends"], copy.wait_send)
        when(step["takes"], add)

    def advance(kind, stage, index):
        depth = len(kind["steps"])
        if stage == 0:
            for place, edge in enumerate(kind["edges"][:-1]):

                @pl.when(index == edge // kind["chunk"])
                def _(place=place):
                    for copy in loads(kind, place):
                        copy.wait()

            columns = window(kind, index)
            kind["whole"][:, columns] = (
                kind["whole"][:, columns].astype(jnp.float32)
                + kind["other"][:, columns].astype(jnp.float32)
            ).astype(kind["whole"].dtype)
        elif stage <= depth:
            end_in(kind, stage - 1, index)
        else:
            number = 2 * depth - stage
            step = kind["steps"][number]
            copy = copy_out(kind, number, index)
            when(step["takes"], copy.wait_send)
            when(step["sends"], copy.wait_recv)
        if stage < depth:
            when(kind["steps"][stage]["sends"], copy_in(kind, stage, index).start)
        elif stage < 2 * depth:
            number = 2 * depth - 1 - stage
            when(kind["steps"][number]["takes"], copy_out(kind, number, index).start)
        else:
            for place, edge in enumerate(kind["edges"][1:]):

                @pl.when(index == edge // kind["chunk"] - 1)
                def _(place=place):
                    store(kind, place).start()

    def exchange(stage):
        return pltpu.make_async_remote_copy(
            src_ref=small_out,
            dst_ref=slots.at[stage],
            send_sem=small_send.at[stage],
            recv_sem=small_recv.at[stage],
            device_id=partners[stage],
            device_id_type=pl.DeviceIdType.MESH,
        )

    last = max(kind["count"] + 2 * len(kind["steps"]) for kind in kinds)
    last = max(last, len(partners) + 1)

    @pl.loop(0, last)
    def _(tick):
        for stage in range(len(partners) + 1):

            @pl.when(tick == stage)
            def _(stage=stage):
                if stage > 0:
                    exchange(stage - 1).wait()
                    small_out[...] += slots[stage - 1]
                if stage < len(partners):
                    exchange(stage).start()

        for stage in range(2 * max(len(kind["steps"]) for kind in kinds) + 1):
            for kind in kinds:
                if stage <= 2 * len(kind["steps"]):

                    @pl.when((tick >= stage) & (tick < stage + kind["count"]))
                    def _(kind=kind, stage=stage):
                        advance(kind, stage, tick - stage)

    for kind in kinds:
        for place in range(len(kind["columns"])):
            store(kind, place).wait()


def sum_cube(axes, parts, plan, small, lines, width, collective_id):
    shape = (-(-sum(len(rows) for rows in lines) // 8) * 8, width)
    flat = [term for kind in parts for pair in kind for term in pair]
    scratch = []
    for kind, (rounds, columns, chunk) in zip(parts, plan):
        rows, total, dtype = kind[0][0].shape[0], sum(columns), kind[0][0].dtype
        scratch += [pltpu.VMEM((rows, total), dtype)] * 3
        for name, _ in rounds:
            rows = rows if name == "give" else rows // 2
            scratch.append(pltpu.VMEM((rows, total), dtype))
        scratch += [pltpu.SemaphoreType.DMA((2 * len(rounds), total // chunk))] * 2
    stages = sum(size.bit_length() - 1 for _, size in axes)
    scratch += [
        pltpu.SemaphoreType.DMA((len(flat),)),
        pltpu.SemaphoreType.DMA((len(flat) // 2,)),
        pltpu.VMEM((stages,) + shape, jnp.float32),
        pltpu.SemaphoreType.DMA((stages,)),
        pltpu.SemaphoreType.DMA((stages,)),
    ]
    *out, sums = pl.pallas_call(
        functools.partial(cube_kernel, axes, plan, lines),
        out_shape=[jax.ShapeDtypeStruct(own.shape, own.dtype) for kind in parts for own, _ in kind]
        + [jax.ShapeDtypeStruct(shape, jnp.float32)],
        in_specs=[pl.BlockSpec(memory_space=pl.ANY)] * len(flat)
        + [pl.BlockSpec(memory_space=pltpu.VMEM)] * len(small),
        out_specs=[pl.BlockSpec(memory_space=pl.ANY)] * (len(flat) // 2)
        + [pl.BlockSpec(memory_space=pltpu.VMEM)],
        scratch_shapes=scratch,
        compiler_params=pltpu.CompilerParams(
            collective_id=collective_id, has_side_effects=True, vmem_limit_bytes=60 * 2**20
        ),
    )(*flat, *small)
    result = []
    for kind in parts:
        result.append(out[: len(kind)])
        out = out[len(kind) :]
    return result, sums


class Groups:
    def __init__(self, axes):
        self.axes = axes
        self.size = dict(axes)["dp"]
        self.me = lax.axis_index("dp")
        bits = [1 << k for k in range(self.size.bit_length() - 1)]
        self.plain = any(size & (size - 1) for _, size in axes) or not bits
        first, rest = bits[:3], bits[3:]
        self.orders = [[1]] * 4
        if first:
            one, two, three = first[0], first[1 % len(first)], first[2 % len(first)]
            orders = (
                (one, two, three, *rest),
                (two, one, three, *rest),
                (three, one, two, *rest),
                (three, two, one, *rest),
            )
            self.orders = [list(dict.fromkeys(order)) for order in orders]
        self.kinds = range(len(self.orders))
        self.line = tuple(bits[-2:]) if len(bits) > 3 else ()

    def swap(self, values, bit):
        return lax.ppermute(values, "dp", [(j, j ^ bit) for j in range(self.size)])

    def upper(self, bit):
        return lax.rem(self.me // bit, 2)

    def in_order(self, bit, mine, other):
        low = self.upper(bit) == 0
        return jnp.concatenate([jnp.where(low, mine, other), jnp.where(low, other, mine)], axis=0)

    def along(self, jobs, call, **arguments):
        bits = [order[0] for order in self.orders]
        lefts = jobs[0][0]
        if self.plain or lefts[0].shape[1] // len(lefts) % 256:
            results, received, _ = call(**arguments)
            jobs = [
                (lefts, [results[rights], *received[0]] if isinstance(rights, int) else rights, *rest)
                for lefts, rights, *rest in jobs
            ]
            pairs = {
                key: (keep, give if self.plain else self.swap(give, bits[key[1]]))
                for key, (give, keep) in halves_plainly(jobs, bits).items()
            }
        else:
            results, received, pairs = call(**arguments, jobs=jobs, bits=bits)
        bundles = {}
        for (bundle, kind), pair in pairs.items():
            bundles.setdefault(bundle, {})[kind] = pair
        return results, received, bundles

    def middle(self, parts, small, lines, width, collective_id):
        if self.plain:
            sums = self.stacked(small, lines, width)
            return parts, lax.psum(sums, tuple(name for name, _ in self.axes))
        plan, fits = [], True
        for order, arrays in zip(self.orders, parts):
            columns = tuple(own.shape[1] for own, _ in arrays)
            blocks = sum(columns) // 128
            chunk = 512 if blocks >= 48 else 256
            plan.append((cube_rounds(order[1:], self.line), columns, chunk))
            fits &= all(count % chunk == 0 for count in columns)
            fits &= (arrays[0][0].shape[0] >> len(order[1:])) % 16 == 0 and len(order) > 1
        if fits:
            return sum_cube(self.axes, parts, plan, small, lines, width, collective_id)
        sums = [
            [self.rounds(order[1:], own, other) for own, other in arrays]
            for order, arrays in zip(self.orders, parts)
        ]
        small = self.stacked(small, lines, width)
        return sums, sum_and_share(None, self.axes, small, small.shape[0], [], collective_id)[0]

    def stacked(self, small, lines, width):
        rows = [
            jnp.pad(array[row], (0, width - array.shape[1]))
            for array, picked in zip(small, lines)
            for row in picked
        ]
        return eight_lines(*rows)

    def rounds(self, bits, own, other):
        total = (own.astype(jnp.float32) + other.astype(jnp.float32)).astype(jnp.bfloat16)
        for bit in bits:
            count = total.shape[0] // 2
            given = lax.dynamic_slice_in_dim(total, (1 - self.upper(bit)) * count, count, axis=0)
            mine = lax.dynamic_slice_in_dim(total, self.upper(bit) * count, count, axis=0)
            other = self.swap(given, bit)
            total = (mine.astype(jnp.float32) + other.astype(jnp.float32)).astype(jnp.bfloat16)
        for bit in reversed(bits):
            total = self.in_order(bit, total, self.swap(total, bit))
        return total

    def finish(self, bundle):
        if self.plain:
            return {kind: (self.orders[kind][0], *pair) for kind, pair in bundle.items()}
        return {
            kind: (self.orders[kind][0], total, self.swap(total, self.orders[kind][0]))
            for kind, total in bundle.items()
        }

    def join(self, *parts):
        if self.plain:
            return jnp.concatenate(
                [
                    lax.psum(
                        self.in_order(*halves)[:, first : first + columns].astype(jnp.float32),
                        "dp",
                    )
                    for halves, first, columns in parts
                ],
                axis=1,
            )
        return join([(*halves, first, columns) for halves, first, columns in parts])


class Flow:
    def __init__(self, sources, held, in_sems, results, staged, out_sems, chunks):
        self.sources, self.held, self.in_sems = sources, held, in_sems
        self.results, self.staged, self.out_sems = results, staged, out_sems
        self.chunks = chunks
        self.sent, self.shared = [], []

    def copy_in(self, index, part):
        width = self.chunks[index]
        columns = pl.ds(part * width, width)
        first = sum(
            source.shape[1] // chunk for source, chunk in zip(self.sources[:index], self.chunks)
        )
        return pltpu.make_async_copy(
            self.sources[index].at[:, columns],
            self.held[index].at[:, columns],
            self.in_sems.at[first + part],
        )

    def start(self, order):
        for index, part in order:
            self.copy_in(index, part).start()

    def pulls(self, held, outs, sems, small):
        self.pull_held, self.pull_outs, self.pull_sems, self.pull_small = held, outs, sems, small
        self.pull_slots, self.pulled = {}, []

    def push(self, order):
        me = lax.axis_index("fsdp")
        for own, places in self.pull_small:
            for step, peer in enumerate(self.peers):
                self.push_one(("small", id(places)), 0, step, peer, own, places[step])
        for index, part in order:
            if index in self.pull_held:
                columns = pl.ds(part * self.chunks[index], self.chunks[index])
                for step, peer in enumerate(self.peers):
                    target = self.pull_held[index][step].at[:, columns]
                    source = self.sources[index].at[:, columns]
                    self.push_one(index, part, step, peer, source, target)

    def carry(self, sources, modes, outs, sems):
        for index, (source, mode) in enumerate(zip(sources, modes)):
            for step, peer in enumerate(self.peers):
                given = source
                if mode == "columns":
                    width = source.shape[1] // self.size
                    given = source.at[:, pl.ds(pl.multiple_of(peer * width, width), width)]
                copy = pltpu.make_async_remote_copy(
                    src_ref=given,
                    dst_ref=outs[index][step],
                    send_sem=sems[0].at[index, step],
                    recv_sem=sems[1].at[index, step],
                    device_id={"fsdp": peer},
                    device_id_type=pl.DeviceIdType.MESH,
                )
                copy.start()
                self.shared.append(copy)

    def push_one(self, index, part, step, peer, source, target):
        send_sems, recv_sems, _ = self.pull_sems
        slot = len(self.pull_slots)
        copy = pltpu.make_async_remote_copy(
            src_ref=source,
            dst_ref=target,
            send_sem=send_sems.at[slot],
            recv_sem=recv_sems.at[slot],
            device_id={"fsdp": peer},
            device_id_type=pl.DeviceIdType.MESH,
        )
        self.pull_slots[index, part, step] = (slot, copy)
        copy.start()

    def take_small(self, places):
        for step in range(len(self.peers)):
            self.pull_slots[("small", id(places)), 0, step][1].wait_recv()
        return places

    def take_all(self, index, part=0):
        blocks = [self.take(index, part)]
        width = self.chunks[index]
        columns = pl.ds(part * width, width)
        for step in range(len(self.peers)):
            slot, copy = self.pull_slots[index, part, step]
            copy.wait_recv()
            block = self.pull_held[index][step].at[:, columns]
            blocks.append(block)
            if not self.pull_outs:
                continue
            out = pltpu.make_async_copy(
                block, self.pull_outs[index][step].at[:, columns], self.pull_sems[2].at[slot]
            )
            out.start()
            self.pulled.append(out)
        return blocks

    def held_all(self, index, part):
        columns = pl.ds(part * self.chunks[index], self.chunks[index])
        return [block.at[:, columns] for block in [self.held[index], *self.pull_held[index]]]

    def take(self, index, part=0):
        self.copy_in(index, part).wait()
        width = self.chunks[index]
        return self.held[index].at[:, pl.ds(part * width, width)]

    def put(self, index, columns=None):
        columns = slice(None) if columns is None else columns
        copy = pltpu.make_async_copy(
            self.staged[index].at[:, columns],
            self.results[index].at[:, columns],
            self.out_sems.at[len(self.sent)],
        )
        copy.start()
        self.sent.append(copy)

    def greet(self, shares, outs, sems, size):
        me = lax.axis_index("fsdp")
        self.shares, self.share_outs, self.share_sems, self.size = shares, outs, sems, size
        self.peers = [lax.rem(me + size - step, size) for step in range(1, size)]

    def share(self, index):
        place = list(self.shares).index(index)
        send_sems, recv_sems = self.share_sems
        for step, peer in enumerate(self.peers):
            source = self.staged[index]
            if self.shares[index] == "columns":
                width = source.shape[1] // self.size
                source = source.at[:, pl.ds(pl.multiple_of(peer * width, width), width)]
            copy = pltpu.make_async_remote_copy(
                src_ref=source,
                dst_ref=self.share_outs[place][step],
                send_sem=send_sems.at[place, step],
                recv_sem=recv_sems.at[place, step],
                device_id={"fsdp": peer},
                device_id_type=pl.DeviceIdType.MESH,
            )
            copy.start()
            self.shared.append(copy)

    def wait_shared(self):
        for copy in self.shared:
            copy.wait()
        self.shared = []

    def finish(self):
        for copy in self.sent + self.shared + self.pulled:
            copy.wait()
        for _, copy in self.pull_slots.values():
            copy.wait_send()


class Grads:
    AHEAD = 6

    def __init__(self, plan, lefts, rights, outs, lefts_held, scratch):
        self.steps, self.bits, self.count, self.tile = plan
        self.lefts, self.rights, self.outs, self.lefts_held = lefts, rights, outs, lefts_held
        self.rights_held, self.staged, *sems = scratch
        self.left_sems, self.right_sems, self.out_sems, self.send_sems, self.recv_sems = sems
        self.frames, self.rows = lefts[0][0].shape[0], self.staged.shape[0]
        self.half = self.rows // 2
        self.me = lax.axis_index("dp")

    def partners(self):
        bits = sorted({self.bits[step[3][1]] for step in self.steps})
        return [{"dp": self.me + bit * (1 - 2 * lax.rem(self.me // bit, 2))} for bit in bits]

    def left_in(self, group, place):
        source = self.lefts[group][place]
        return pltpu.make_async_copy(
            source.at[:, own_columns(self.count, 0, self.rows)] if place == 0 else source,
            self.lefts_held[group].at[pl.ds(place * self.frames, self.frames)],
            self.left_sems.at[group, place],
        )

    def right_in(self, index, place):
        _, right, first, _, _ = self.steps[index]
        return pltpu.make_async_copy(
            self.rights[right][place].at[:, pl.ds(first, self.tile)],
            self.rights_held.at[index % self.AHEAD, pl.ds(place * self.frames, self.frames)],
            self.right_sems.at[index, place],
        )

    def halves_out(self, index):
        _, _, _, key, start = self.steps[index]
        bit = self.bits[key[1]]
        upper = lax.rem(self.me // bit, 2)
        source, columns = [
            self.staged.at[
                pl.ds(pl.multiple_of(part * self.half, self.half), self.half),
                pl.ds(index * self.tile, self.tile),
            ]
            for part in (1 - upper, upper)
        ], pl.ds(start, self.tile)
        keep, recv = self.outs[key]
        return (
            pltpu.make_async_remote_copy(
                src_ref=source[0],
                dst_ref=recv.at[:, columns],
                send_sem=self.send_sems.at[index],
                recv_sem=self.recv_sems.at[index],
                device_id={"dp": self.me + bit * (1 - 2 * upper)},
                device_id_type=pl.DeviceIdType.MESH,
            ),
            pltpu.make_async_copy(source[1], keep.at[:, columns], self.out_sems.at[index]),
        )

    def begin(self, first, last):
        self.first, self.last, self.loaded = first, last, set()
        for index in range(first, min(first + self.AHEAD, last)):
            self.load(index)

    def load(self, index):
        group = self.steps[index][0]
        for place in range(self.count):
            if group not in self.loaded:
                self.left_in(group, place).start()
            self.right_in(index, place).start()
        self.loaded.add(group)

    def run(self, then):
        waited = set()
        for index in range(self.first, self.last):
            step = self.steps[index]
            for place in range(self.count):
                if step[0] not in waited:
                    self.left_in(step[0], place).wait()
                self.right_in(index, place).wait()
            waited.add(step[0])
            right = self.rights_held[index % self.AHEAD]
            product = dot_down(self.lefts_held[step[0]][...], right)
            self.staged[:, pl.ds(index * self.tile, self.tile)] = product.astype(jnp.bfloat16)
            for copy in self.halves_out(index):
                copy.start()
            if index + self.AHEAD < self.last:
                self.load(index + self.AHEAD)
            if index == max(self.last - self.AHEAD - 1, self.first):
                then()

    def finish(self):
        for index in range(len(self.steps)):
            for copy in self.halves_out(index):
                copy.wait()


def gradient_plan(jobs, tile, spread):
    lefts, rights, steps, totals = [], [], [], {}
    for job_lefts, job_rights, first, columns, key in jobs:
        for known, group in ((lefts, job_lefts), (rights, job_rights)):
            if not any(group is other for other in known):
                known.append(group)
        left = [group is job_lefts for group in lefts].index(True)
        right = [group is job_rights for group in rights].index(True)
        for start in range(0, columns, tile):
            steps.append((left, right, first + start, key, totals.setdefault(key, 0)))
            totals[key] += tile
    turns = {key: 0 for key in totals}
    ranks = []
    for step in steps:
        turns[step[3]] += 1
        ranks.append((turns[step[3]] - 0.5) / (totals[step[3]] // tile))
    late = [isinstance(rights[step[1]], int) for step in steps]
    keys = [(late[k], ranks[k] if spread else k) for k in range(len(steps))]
    steps = [steps[k] for k in sorted(range(len(steps)), key=lambda k: keys[k])]
    return lefts, rights, steps, totals


def fused(
    body,
    small,
    large,
    results,
    order=None,
    scratch=(),
    shares=None,
    size=1,
    collective_id=None,
    jobs=(),
    bits=(),
    pulls=(),
    small_pulls=(),
    carried=(),
    pulls_stay=False,
    spread=False,
):
    shares = {} if shares is None or size == 1 else shares
    chunks = [width for _, width in large]
    parts = [array.shape[1] // width for array, width in large]
    if order is None:
        order = [(index, part) for index, count in enumerate(parts) for part in range(count)]
    share_shapes = [
        (shape if mode == "all" else (shape[0], shape[1] // size), dtype)
        for (shape, dtype), mode in ((results[index], mode) for index, mode in shares.items())
        for _ in range(size - 1)
    ]
    pulls = list(pulls) if size > 1 else []
    pull_shapes = [
        (large[index][0].shape, large[index][0].dtype) for index in pulls for _ in range(size - 1)
    ]
    carried = list(carried) if size > 1 else []
    carry_shapes = [
        (array.shape if mode == "all" else (array.shape[0], array.shape[1] // size), array.dtype)
        for array, mode in carried
        for _ in range(size - 1)
    ]
    pull_count = (sum(parts[index] for index in pulls) + len(small_pulls)) * (size - 1)
    tile = 512
    lefts, rights, steps, totals = gradient_plan(jobs, tile, spread)
    early = len([step for step in steps if not isinstance(rights[step[1]], int)])
    flat = [array for group in lefts + rights if not isinstance(group, int) for array in group]
    half_shapes, grad_scratch = [], []
    if jobs:
        count, frames = len(lefts[0]), lefts[0][0].shape[0]
        rows = lefts[0][0].shape[1] // count
        half_shapes = [
            ((rows // 2, columns), jnp.bfloat16) for columns in totals.values() for _ in range(2)
        ]
        grad_scratch = [pltpu.VMEM((count * frames, rows), jnp.bfloat16) for _ in lefts] + [
            pltpu.VMEM((Grads.AHEAD, count * frames, tile), jnp.bfloat16),
            pltpu.VMEM((rows, len(steps) * tile), jnp.bfloat16),
            pltpu.SemaphoreType.DMA((len(lefts), count)),
            pltpu.SemaphoreType.DMA((len(steps), count)),
        ] + [pltpu.SemaphoreType.DMA((len(steps),))] * 3

    def kernel(*refs):
        refs = list(refs)

        def pick(count):
            picked = refs[:count]
            del refs[:count]
            return picked

        small_refs, sources = pick(len(small)), pick(len(large))
        left_refs = [pick(len(group)) for group in lefts]
        right_refs = [group if isinstance(group, int) else pick(len(group)) for group in rights]
        carry_refs = pick(len(carried))
        outs = pick(len(results))
        share_outs = [pick(size - 1) for _ in shares]
        half_outs = {key: pick(2) for key in totals}
        pull_outs = {} if pulls_stay else {index: pick(size - 1) for index in pulls}
        carry_outs = [pick(size - 1) for _ in carried]
        held, staged, rest = pick(len(large)), pick(len(results)), pick(len(scratch))
        in_sems, out_sems = pick(2)
        share_sems = pick(2) if shares else []
        pull_held = {index: pick(size - 1) for index in pulls}
        pull_small = [(small_refs[index], pick(size - 1)) for index in small_pulls]
        pull_sems = pick(3) if pull_count else []
        carry_sems = pick(2) if carried else []
        flow = Flow(sources, held, in_sems, outs, staged, out_sems, chunks)
        greeted = []
        if jobs:
            plan = (steps, bits, len(lefts[0]), tile)
            for place, group in enumerate(right_refs):
                if isinstance(group, int):
                    others = share_outs[list(shares).index(group)] if shares else []
                    right_refs[place] = [staged[group], *others]
            grads = Grads(plan, left_refs, right_refs, half_outs, pick(len(lefts)), refs)
            grads.begin(0, early)
            greeted = grads.partners()
        flow.greet(shares, share_outs, share_sems, size)
        flow.pulls(pull_held, pull_outs, pull_sems, pull_small)
        if pull_count:
            flow.start(order)
        if shares or pull_count or carried:
            greeted += [{"fsdp": peer} for peer in flow.peers]
        if greeted:
            barrier = pltpu.get_barrier_semaphore()
            for device in greeted:
                pl.semaphore_signal(
                    barrier, inc=1, device_id=device, device_id_type=pl.DeviceIdType.MESH
                )
            pl.semaphore_wait(barrier, len(greeted))
        if carried:
            modes = [mode for _, mode in carried]
            flow.carry(carry_refs, modes, carry_outs, carry_sems)
        if jobs:
            grads.run(functools.partial(flow.start, order))
        elif pull_count:
            flow.push(order)
        else:
            flow.start(order)
        if body is not None:
            body(flow, small_refs, rest)
        if early < len(steps):
            flow.wait_shared()
            grads.begin(early, len(steps))
            grads.run(lambda: None)
        flow.finish()
        if jobs:
            grads.finish()

    semaphores = [
        pltpu.SemaphoreType.DMA((max(sum(parts), 1),)),
        pltpu.SemaphoreType.DMA((64,)),
    ]
    params = dict(vmem_limit_bytes=60 * 2**20)
    if shares:
        semaphores += [pltpu.SemaphoreType.DMA((len(shares), size - 1))] * 2
    pull_scratch = []
    if pull_count:
        pull_scratch = [pltpu.VMEM(shape, dtype) for shape, dtype in pull_shapes] + [
            pltpu.VMEM(small[index].shape, small[index].dtype)
            for index in small_pulls
            for _ in range(size - 1)
        ]
        pull_scratch += [pltpu.SemaphoreType.DMA((pull_count,))] * 3
    if carried:
        pull_scratch += [pltpu.SemaphoreType.DMA((len(carried), size - 1))] * 2
    if shares or jobs or pull_count or carried:
        params.update(collective_id=collective_id, has_side_effects=True)
    pull_results = [] if pulls_stay else pull_shapes
    shapes = results + share_shapes + half_shapes + pull_results + carry_shapes
    out = pl.pallas_call(
        kernel,
        out_shape=[jax.ShapeDtypeStruct(shape, dtype) for shape, dtype in shapes],
        in_specs=[
            pl.BlockSpec(memory_space=pltpu.SMEM if array.dtype == jnp.int32 else pltpu.VMEM)
            for array in small
        ]
        + [pl.BlockSpec(memory_space=pl.ANY)] * (len(large) + len(flat) + len(carried)),
        out_specs=[pl.BlockSpec(memory_space=pl.ANY)] * len(shapes),
        scratch_shapes=[pltpu.VMEM(array.shape, array.dtype) for array, _ in large]
        + [pltpu.VMEM(shape, dtype) for shape, dtype in results]
        + list(scratch)
        + semaphores
        + pull_scratch
        + grad_scratch,
        compiler_params=pltpu.CompilerParams(**params),
    )(*small, *[array for array, _ in large], *flat, *[array for array, _ in carried])
    others = out[len(results) : len(results) + len(share_shapes)]
    received = [others[k * (size - 1) : (k + 1) * (size - 1)] for k in range(len(shares))]
    halves = out[len(results) + len(share_shapes) :]
    others = out[len(shapes) - len(pull_results) - len(carry_shapes) :]
    received += [
        others[k : k + size - 1] for k in range(0, len(others), max(size - 1, 1)) if size > 1
    ]
    return (
        out[: len(results)],
        received or [[] for _ in range(16)],
        {key: (halves[2 * k], halves[2 * k + 1]) for k, key in enumerate(totals)},
    )


def dot(left, right):
    return jnp.dot(left, right, preferred_element_type=jnp.float32)


def dot_across(left, right):
    return lax.dot_general(left, right, ACROSS_DIMS, preferred_element_type=jnp.float32)


def dot_down(left, right):
    return lax.dot_general(left, right, DOWN_DIMS, preferred_element_type=jnp.float32)


def own_columns(size, place, width):
    owner = lax.rem(lax.axis_index("fsdp") + place, size)
    return pl.ds(pl.multiple_of(owner * width, width), width)


def times_blocks(values_ref, blocks):
    total = None
    for place, block in enumerate(blocks):
        columns = own_columns(len(blocks), place, block.shape[0])
        part = dot(values_ref[:, columns], block[...])
        total = part if total is None else total + part
    return total


def add_back(total_ref, values, blocks, scale=None):
    for place, block in enumerate(blocks):
        columns = own_columns(len(blocks), place, block.shape[0])
        part = dot_across(values, block[...])
        total_ref[:, columns] += part if scale is None else scale * part


def centred(values):
    centre = values - jnp.mean(values, axis=-1, keepdims=True)
    spread = jnp.mean(centre * centre, axis=-1, keepdims=True)
    scale = lax.rsqrt(spread + EPSILON)
    return centre * scale, scale


BIAS_LINES = (6, 7, 9, 10, 8, 11)
TAP_LINE = 12


def gain_line(lines_ref, norm):
    return lines_ref[norm : norm + 1, :]


def bias_line(lines_ref, norm):
    return lines_ref[BIAS_LINES[norm] : BIAS_LINES[norm] + 1, :]


def tap_line(lines_ref, tap):
    return lines_ref[TAP_LINE + tap : TAP_LINE + tap + 1, :]


def norm_low(values, lines_ref, norm):
    hat, _ = centred(values)
    return (hat * gain_line(lines_ref, norm) + bias_line(lines_ref, norm)).astype(jnp.bfloat16)


def norm_grad(grad, values, gain_row):
    hat, scale = centred(values)
    inner = grad * gain_row
    first = jnp.mean(inner, axis=-1, keepdims=True)
    second = jnp.mean(inner * hat, axis=-1, keepdims=True)
    return (
        (inner - first - hat * second) * scale,
        jnp.sum(grad * hat, axis=0, keepdims=True),
        jnp.sum(grad, axis=0, keepdims=True),
    )


def put_rows(ref, *lines):
    for place, line in enumerate(lines):
        ref[pl.ds(place, 1), :] = line
    ref[pl.ds(len(lines), ref.shape[0] - len(lines)), :] = jnp.zeros(
        (ref.shape[0] - len(lines), ref.shape[1]), ref.dtype
    )


def segment_of(lengths_ref, places):
    ends = lengths_ref[0, 0]
    segment = (places >= ends).astype(jnp.int32)
    for index in range(1, lengths_ref.shape[1]):
        ends = ends + lengths_ref[0, index]
        segment += (places >= ends).astype(jnp.int32)
    return segment


def frame_marks(lengths_ref, frames, taps=0):
    places = lax.broadcasted_iota(jnp.int32, (frames, 1), 0)
    segment = segment_of(lengths_ref, places)
    valid = (segment < lengths_ref.shape[1]).astype(jnp.float32)
    marks = []
    for tap in range(taps):
        moved = places + (tap - taps // 2)
        same = (segment_of(lengths_ref, moved) == segment) & (moved >= 0) & (moved < frames)
        marks.append(same.astype(jnp.float32))
    return valid, marks


def same_segment(lengths_ref, frames):
    down = segment_of(lengths_ref, lax.broadcasted_iota(jnp.int32, (frames, 1), 0))
    across = segment_of(lengths_ref, lax.broadcasted_iota(jnp.int32, (1, frames), 1))
    return down == across


TILE = 1024


def feed_forward(w_in, w_out, flow, normed_ref, hidden, slope_ref, y_ref):
    inner = slope_ref.shape[1]
    for part in range(inner // TILE):
        columns = pl.ds(part * TILE, TILE)
        before = times_blocks(normed_ref, w_in(part))
        gate = jax.nn.sigmoid(before)
        value = (before * gate).astype(jnp.bfloat16)
        flow.staged[hidden][:, columns] = value
        flow.put(hidden, columns)
        slope_ref[:, columns] = (gate * (1.0 + before * (1.0 - gate))).astype(jnp.bfloat16)
        add_back(y_ref, value, w_out(part), 0.5)


def feed_forward_back(blocks_in, blocks_out, low_ref, slope_ref, flow, result, normed_ref):
    inner = slope_ref.shape[1]
    normed_ref[...] = jnp.zeros_like(normed_ref)
    for part in range(inner // TILE):
        columns = pl.ds(part * TILE, TILE)
        grad = times_blocks(low_ref, blocks_out(part)) * slope_ref[:, columns].astype(jnp.float32)
        grad = grad.astype(jnp.bfloat16)
        flow.staged[result][:, columns] = grad
        flow.put(result, columns)
        add_back(normed_ref, grad, blocks_in(part))


def head_scores(query, key, bias_row, same, scale):
    frames = query.shape[0]
    spread = jnp.broadcast_to(bias_row, (frames, bias_row.shape[1]))
    relative = pltpu.roll(spread, 0, 1, stride=1, stride_axis=0)[:, :frames]
    return jnp.where(same, dot_across(query, key) * scale + relative, MASKED)


def softmax_rows(scores):
    powers = jnp.exp(scores - jnp.max(scores, axis=-1, keepdims=True))
    return powers / jnp.sum(powers, axis=-1, keepdims=True)


def split(items, count):
    items = list(items)
    return [items[k : k + count] for k in range(0, len(items), count)]


def front(
    x, own_lines, own_bias, lengths, heads, taps, weights, size, collective_id
):
    frames, width = x.shape
    inner = weights[0].shape[1]
    head = width // heads
    small = [own_lines, own_bias, lengths]
    large = [(x, width)]
    large += [(block, TILE) for block in weights[:2]] + [(block, width) for block in weights[2:]]
    order = [(0, 0)]
    order += [(index, part) for part in range(inner // TILE) for index in (1, 2)]
    order += [(3, part) for part in range(3)] + [(4, 0), (5, 1), (5, 0)]
    low, full = jnp.bfloat16, jnp.float32
    results = [
        ((frames, width), low),
        ((frames, inner), low),
        ((frames, inner), low),
        ((frames, width), full),
        ((frames, width), low),
        ((frames, width), low),
        ((frames, width), low),
        ((frames, width), low),
        ((frames, width), low),
        ((frames, width), full),
        ((frames, width), low),
        ((frames, width), full),
        ((frames, width), full),
        ((frames, width), full),
        ((8, width), full),
        ((own_lines.shape[0], width), full),
        ((-(-heads // 8) * 8, own_bias.shape[1]), full),
    ]

    def body(flow, small_refs, _):
        own_lines_ref, own_bias_ref, lengths_ref = small_refs
        valid, marks = frame_marks(lengths_ref, frames, taps)
        (
            normed_one,
            hidden,
            slope,
            x1,
            normed_attn,
            query_ref,
            key_ref,
            value_ref,
            context,
            x2,
            normed_conv,
            gated_ref,
            gate_ref,
            mixed_ref,
            sums_ref,
            lines_ref,
            bias_ref,
        ) = flow.staged
        small_places = [places for _, places in flow.pull_small]
        blocks = [own_lines_ref] + (flow.take_small(small_places[0]) if size > 1 else [])
        for place, block in enumerate(blocks):
            lines_ref[:, own_columns(size, place, block.shape[1])] = block[...]
        flow.put(15)
        blocks = [own_bias_ref] + (flow.take_small(small_places[1]) if size > 1 else [])
        for place, block in enumerate(blocks):
            owner = lax.rem(lax.axis_index("fsdp") + place, size)
            for row in range(heads // size):
                bias_ref[pl.ds(owner * (heads // size) + row, 1), :] = block[row : row + 1, :]
        flow.put(16)
        values = flow.take(0)[...].astype(jnp.float32)
        normed_one[...] = norm_low(values, lines_ref, 0)
        flow.put(0)
        x1[...] = values
        feed_forward(
            lambda part: flow.take_all(1, part),
            lambda part: flow.take_all(2, part),
            flow,
            normed_one,
            1,
            slope,
            x1,
        )
        flow.put(2)
        flow.put(3)

        normed_attn[...] = norm_low(x1[...], lines_ref, 1)
        flow.put(4)
        for part, ref in enumerate((query_ref, key_ref, value_ref)):
            ref[...] = times_blocks(normed_attn, flow.take_all(3, part)).astype(jnp.bfloat16)
            flow.put(5 + part)
        same = same_segment(lengths_ref, frames)
        for place in range(heads):
            columns = slice(place * head, (place + 1) * head)
            scores = head_scores(
                query_ref[:, columns],
                key_ref[:, columns],
                bias_ref[place : place + 1, :],
                same,
                head**-0.5,
            )
            attend = softmax_rows(scores).astype(jnp.bfloat16)
            context[:, columns] = dot(attend, value_ref[:, columns]).astype(jnp.bfloat16)
        flow.put(8)
        x2[...] = x1[...] + times_blocks(context, flow.take_all(4))
        flow.put(9)

        normed_conv[...] = norm_low(x2[...], lines_ref, 2)
        flow.put(10)
        gate = jax.nn.sigmoid(times_blocks(normed_conv, flow.take_all(5, 1)))
        gate_ref[...] = gate
        flow.put(12)
        gated_ref[...] = times_blocks(normed_conv, flow.take_all(5, 0)) * gate
        flow.put(11)
        mixed = jnp.zeros((frames, width), jnp.float32)
        for tap in range(taps):
            offset = tap - taps // 2
            gated = gated_ref[...]
            moved = gated if offset == 0 else pltpu.roll(gated, -offset % frames, 0)
            mixed += tap_line(lines_ref, tap) * (moved * marks[tap])
        mixed_ref[...] = mixed
        flow.put(13)
        weighted = valid * mixed
        put_rows(
            sums_ref,
            jnp.sum(weighted, axis=0, keepdims=True),
            jnp.sum(weighted * mixed, axis=0, keepdims=True),
            jnp.broadcast_to(jnp.sum(valid, axis=0, keepdims=True), (1, width)),
        )
        flow.put(14)

    results, pulled, _ = fused(
        body,
        small,
        large,
        results,
        order,
        size=size,
        collective_id=collective_id,
        pulls=range(1, 6),
        small_pulls=(0, 1),
    )
    return results, [[own, *others] for own, others in zip(weights, pulled)]


def batch_stats(totals_ref):
    count = totals_ref[2:3, :]
    mean = totals_ref[0:1, :] / count
    rstd = lax.rsqrt(totals_ref[1:2, :] / count - mean * mean + EPSILON)
    return count, mean, rstd


def turn(x, mixed, totals, cotangent, lengths, lines, w_conv, w_in, w_out, size, collective_id):
    frames, width = x.shape
    inner = w_in.shape[1]
    small = [totals, lengths, lines]
    large = [(mixed, width), (x, width), (w_conv, width), (w_in, TILE), (w_out, TILE)]
    large += [(cotangent, width)]
    order = [(0, 0), (1, 0), (2, 0)]
    order += [(index, part) for part in range(inner // TILE) for index in (3, 4)]
    order += [(5, 0)]
    low, full = jnp.bfloat16, jnp.float32
    results = [
        ((frames, width), low),
        ((frames, width), low),
        ((frames, inner), low),
        ((frames, width), low),
        ((frames, width), low),
        ((frames, inner), low),
        ((frames, width), low),
        ((frames, width), full),
        ((frames, width), full),
        ((8, width), full),
        ((8, width), full),
        ((8, width), full),
    ]
    scratch = [
        pltpu.VMEM((frames, inner), low),
        pltpu.VMEM((frames, width), full),
        pltpu.VMEM((frames, width), full),
        pltpu.VMEM((frames, width), full),
    ]

    def body(flow, small_refs, rest):
        totals_ref, lengths_ref, lines_ref = small_refs
        valid, _ = frame_marks(lengths_ref, frames)
        slope, x3, x4, normed_grad = rest
        (
            swish,
            normed,
            hidden,
            out_ref,
            low_two,
            before,
            low_conv,
            grad_ref,
            hat_grad,
            sums_final,
            sums_two,
            sums_batch,
        ) = flow.staged
        _, mean, rstd = batch_stats(totals_ref)
        mixed_ref = flow.take(0)
        z = (mixed_ref[...] - mean) * rstd * gain_line(lines_ref, 5) + bias_line(lines_ref, 5)
        swish[...] = (z * jax.nn.sigmoid(z)).astype(jnp.bfloat16)
        flow.put(0)
        x2_ref = flow.take(1)
        conv_blocks = flow.take_all(2)
        x3[...] = x2_ref[...] + times_blocks(swish, conv_blocks)
        normed[...] = norm_low(x3[...], lines_ref, 3)
        flow.put(1)
        x4[...] = x3[...]
        feed_forward(
            functools.partial(flow.take_all, 3),
            functools.partial(flow.take_all, 4),
            flow,
            normed,
            2,
            slope,
            x4,
        )
        if size > 1:
            for index in (2, 1, 0):
                flow.share(index)

        gain_row = gain_line(lines_ref, 4)
        hat, _ = centred(x4[...])
        out_ref[...] = (valid * (hat * gain_row + bias_line(lines_ref, 4))).astype(jnp.bfloat16)
        flow.put(3)
        grad = valid * flow.take(len(large) - 1)[...].astype(jnp.float32)
        grad_values, grad_gain, grad_bias = norm_grad(grad, x4[...], gain_row)
        grad_ref[...] = grad_values
        low_two[...] = (0.5 * grad_values).astype(jnp.bfloat16)
        flow.put(4)
        if size > 1:
            flow.share(4)
        put_rows(sums_final, grad_gain, grad_bias)
        flow.put(9)

        feed_forward_back(
            functools.partial(flow.held_all, 3),
            functools.partial(flow.held_all, 4),
            low_two,
            slope,
            flow,
            5,
            normed_grad,
        )
        if size > 1:
            flow.share(5)
        branch, grad_gain, grad_bias = norm_grad(
            normed_grad[...], x3[...], gain_line(lines_ref, 3)
        )
        total = grad_ref[...] + branch
        grad_ref[...] = total
        flow.put(7)
        low_conv[...] = total.astype(jnp.bfloat16)
        flow.put(6)
        if size > 1:
            flow.share(6)
        put_rows(sums_two, grad_gain, grad_bias)
        flow.put(10)

        for place, block in enumerate(conv_blocks):
            columns = own_columns(size, place, block.shape[0])
            hat_grad[:, columns] = dot_across(low_conv[...], block[...])
        hat = (mixed_ref[...] - mean) * rstd
        gain_row = gain_line(lines_ref, 5)
        z = hat * gain_row + bias_line(lines_ref, 5)
        gate = jax.nn.sigmoid(z)
        grad_z = hat_grad[...] * gate * (1.0 + z * (1.0 - gate))
        grad_hat = grad_z * gain_row
        hat_grad[...] = grad_hat
        flow.put(8)
        put_rows(
            sums_batch,
            jnp.sum(grad_hat, axis=0, keepdims=True),
            jnp.sum(grad_hat * hat, axis=0, keepdims=True),
            jnp.sum(grad_z * hat, axis=0, keepdims=True),
            jnp.sum(grad_z, axis=0, keepdims=True),
        )
        flow.put(11)

    return fused(
        body,
        small,
        large,
        results,
        order,
        scratch,
        shares={0: "columns", 1: "columns", 2: "all", 4: "columns", 5: "all", 6: "all"},
        size=size,
        collective_id=collective_id,
        pulls=(2, 3, 4),
        pulls_stay=True,
    )[:2]


def back_front(
    hat_grad,
    gated,
    gate,
    mixed,
    totals,
    back,
    grad,
    x2,
    x1,
    lines,
    bias_table,
    lengths,
    taps,
    packed,
    w_conv,
    w_out,
    w_qkv,
    collective_id,
    **jobs,
):
    frames, width = x1.shape
    count = len(w_conv)
    heads = bias_table.shape[0]
    head = width // heads
    flip = (
        jnp.arange(frames)[:, None] + jnp.arange(frames)[None, :] == frames - 1
    ).astype(jnp.bfloat16)
    small = [totals, back, lengths, lines, bias_table, flip]
    large = [(array, width) for array in (hat_grad, mixed, gated, gate)]
    large += [(block, width) for block in w_conv]
    large += [(array, width) for array in (x2, grad)]
    large += [(block, width) for block in w_out]
    large += [(array, width) for array in packed]
    large += [(block, width) for block in w_qkv]
    large += [(x1, width)]
    conv = list(range(4, 4 + count))
    place_x2 = 4 + count
    out = list(range(place_x2 + 2, place_x2 + 2 + count))
    place_packed = out[-1] + 1
    qkv = list(range(place_packed + 3, place_packed + 3 + count))
    order = None
    low, full = jnp.bfloat16, jnp.float32
    results = [((frames, width), low)] * 7 + [((frames, width), full)]
    results += [((8, width), full)] * 3 + [(bias_table.shape, full)]
    scratch = [
        pltpu.VMEM((frames, width), full),
        pltpu.VMEM((frames, width), full),
        pltpu.VMEM((frames, width), low),
    ]

    def body(flow, small_refs, rest):
        (
            totals_ref,
            back_ref,
            lengths_ref,
            lines_ref,
            bias_ref,
            flip_ref,
        ) = small_refs
        valid, marks = frame_marks(lengths_ref, frames, taps)
        normed_grad, grad_mixed_ref, grad_context = rest
        one, two, low_attn, *grad_refs = flow.staged[:6]
        low_one, grad_ref, sums_kernel, sums_conv, sums_attn, sums_rel = flow.staged[6:]
        valid_count, mean, rstd = batch_stats(totals_ref)
        grad_var = -0.5 * rstd * rstd * back_ref[1:2, :]
        grad_mean = -rstd * back_ref[0:1, :] - 2.0 * mean * grad_var
        hat_ref, mixed_ref = flow.take(0), flow.take(1)
        grad_mixed_ref[...] = (
            hat_ref[...] * rstd
            + valid * (grad_mean + 2.0 * mixed_ref[...] * grad_var) / valid_count
        )
        gated_ref = flow.take(2)
        normed_grad[...] = jnp.zeros_like(normed_grad)
        kernel_grads = []
        for tap in range(taps):
            offset = tap - taps // 2
            masked = grad_mixed_ref[...] * marks[tap]
            gated = gated_ref[...]
            moved = gated if offset == 0 else pltpu.roll(gated, -offset % frames, 0)
            kernel_grads.append(jnp.sum(masked * moved, axis=0, keepdims=True))
            moved = masked if offset == 0 else pltpu.roll(masked, offset % frames, 0)
            normed_grad[...] += tap_line(lines_ref, tap) * moved
        put_rows(sums_kernel, *kernel_grads)
        flow.put(8)
        gate_now = flow.take(3)[...]
        grad_gated = normed_grad[...]
        one[...] = (grad_gated * gate_now).astype(jnp.bfloat16)
        flow.put(0)
        if count > 1:
            flow.share(0)
        two[...] = (grad_gated * gated_ref[...] * (1.0 - gate_now)).astype(jnp.bfloat16)
        flow.put(1)
        if count > 1:
            flow.share(1)
        normed_grad[...] = jnp.zeros_like(normed_grad)
        for part, ref in enumerate((one, two)):
            add_back(normed_grad, ref[...], [flow.take(index, part) for index in conv])
        branch, grad_gain, grad_bias = norm_grad(
            normed_grad[...], flow.take(place_x2)[...], gain_line(lines_ref, 2)
        )
        total = flow.take(place_x2 + 1)[...] + branch
        grad_ref[...] = total
        low_attn[...] = total.astype(jnp.bfloat16)
        flow.put(2)
        if count > 1:
            flow.share(2)
        put_rows(sums_conv, grad_gain, grad_bias)
        flow.put(9)

        for place, index in enumerate(out):
            block = flow.take(index)
            columns = own_columns(count, place, block.shape[0])
            grad_context[:, columns] = dot_across(low_attn[...], block[...]).astype(jnp.bfloat16)
        packed_refs = [flow.take(place_packed + part) for part in range(3)]
        same = same_segment(lengths_ref, frames)
        scale = head**-0.5
        reach = bias_ref.shape[1]
        for place in range(heads):
            columns = slice(place * head, (place + 1) * head)
            query, key, value = (ref[:, columns] for ref in packed_refs)
            bias_row = bias_ref[place : place + 1, :]
            attend = softmax_rows(head_scores(query, key, bias_row, same, scale))
            context = grad_context[:, columns]
            grad_attend = dot_across(context, value)
            grad_value = dot_down(attend.astype(jnp.bfloat16), context)
            grad_scores = attend * (
                grad_attend - jnp.sum(grad_attend * attend, axis=-1, keepdims=True)
            )
            grad_low = grad_scores.astype(jnp.bfloat16)
            padded = jnp.concatenate(
                [dot(grad_low, flip_ref[...]), jnp.zeros((frames, reach - frames), jnp.float32)],
                axis=1,
            )
            skewed = pltpu.roll(padded, 0, 1, stride=1, stride_axis=0)
            sums_rel[place : place + 1, :] = jnp.sum(skewed, axis=0, keepdims=True)
            grad_query = dot(grad_low, key) * scale
            grad_key = dot_down(grad_low, query) * scale
            for ref, part in zip(grad_refs, (grad_query, grad_key, grad_value)):
                ref[:, columns] = part.astype(jnp.bfloat16)
        flow.put(11)
        normed_grad[...] = jnp.zeros_like(normed_grad)
        for part, ref in enumerate(grad_refs):
            flow.put(3 + part)
            if count > 1:
                flow.share(3 + part)
            add_back(normed_grad, ref[...], [flow.take(index, part) for index in qkv])
        branch, grad_gain, grad_bias = norm_grad(
            normed_grad[...], flow.take(len(large) - 1)[...], gain_line(lines_ref, 1)
        )
        total = grad_ref[...] + branch
        grad_ref[...] = total
        flow.put(7)
        low_one[...] = (0.5 * total).astype(jnp.bfloat16)
        flow.put(6)
        if count > 1:
            flow.share(6)
        put_rows(sums_attn, grad_gain, grad_bias)
        flow.put(10)

    shares = {0: "all", 1: "all", 2: "all", 3: "all", 4: "all", 5: "all", 6: "columns"}
    return fused(
        body, small, large, results, order, scratch, shares, count, collective_id, **jobs
    )


def back_end(low, grad, x, lines, slope, w_in, w_out, collective_id, **jobs):
    frames, width = x.shape
    inner, count = w_in[0].shape[1], len(w_in)
    large = [(low, width)] + [(block, TILE) for block in w_out + w_in]
    large += [(slope, TILE), (x, width), (grad, width)]
    groups = split(range(1, 1 + 2 * count), count)
    place_slope = 1 + 2 * count
    order = [(0, 0)]
    for part in range(inner // TILE):
        order += [(index, part) for index in groups[0]] + [(place_slope, part)]
        order += [(index, part) for index in groups[1]]
    order += [(place_slope + 1, 0), (place_slope + 2, 0)]
    results = [
        ((frames, inner), jnp.bfloat16),
        ((frames, width), jnp.bfloat16),
        ((8, width), jnp.float32),
    ]

    def body(flow, small_refs, rest):
        (lines_ref,), (normed_grad,) = small_refs, rest
        before, out_ref, sums_ref = flow.staged

        def w_out_part(part):
            blocks = [flow.take(index, part) for index in groups[0]]
            flow.take(place_slope, part)
            return blocks

        def w_in_part(part):
            return [flow.take(index, part) for index in groups[1]]

        feed_forward_back(
            w_in_part, w_out_part, flow.take(0), flow.held[place_slope], flow, 0, normed_grad
        )
        if count > 1:
            flow.share(0)
        values = flow.take(place_slope + 1)[...].astype(jnp.float32)
        branch, grad_gain, grad_bias = norm_grad(normed_grad[...], values, gain_line(lines_ref, 0))
        out_ref[...] = (flow.take(place_slope + 2)[...] + branch).astype(jnp.bfloat16)
        flow.put(1)
        put_rows(sums_ref, grad_gain, grad_bias)
        flow.put(2)

    scratch = [pltpu.VMEM((frames, width), jnp.float32)]
    shares = {0: "all"}
    return fused(
        body, [lines], large, results, order, scratch, shares, count, collective_id, **jobs
    )


def halves_plainly(jobs, bits):
    products = {}
    for lefts, rights, first, columns, key in jobs:
        rows = lefts[0].shape[1] // len(lefts)
        own = lax.dynamic_slice_in_dim(lefts[0], lax.axis_index("fsdp") * rows, rows, axis=1)
        left = jnp.concatenate([own, *lefts[1:]])
        right = jnp.concatenate(rights)[:, first : first + columns]
        products.setdefault(key, []).append(dot_down(left, right).astype(jnp.bfloat16))
    halves = {}
    for key, parts in products.items():
        product = jnp.concatenate(parts, axis=1)
        half = product.shape[0] // 2
        upper = lax.rem(lax.axis_index("dp") // bits[key[1]], 2)
        halves[key] = tuple(
            lax.dynamic_slice_in_dim(product, part * half, half, axis=0)
            for part in (1 - upper, upper)
        )
    return halves


def join_body(bits, counts, *refs):
    step = pl.program_id(0)
    out_ref = refs[-1]
    half = refs[0].shape[0]
    first = 0
    for index, (bit, count) in enumerate(zip(bits, counts)):
        upper = lax.rem(lax.axis_index("dp") // bit, 2)

        @pl.when((step >= first) & (step < first + count))
        def _(index=index, upper=upper):
            for ref, part in zip(refs[2 * index : 2 * index + 2], (upper, 1 - upper)):
                rows = pl.ds(pl.multiple_of(part * half, half), half)
                out_ref[rows, :] = ref[...].astype(jnp.float32)

        first += count


def join(parts):
    tile = 512 if any(part[3] % 1024 or part[4] % 1024 for part in parts) else 1024
    counts = [columns // tile for _, _, _, _, columns in parts]
    rows = 2 * parts[0][1].shape[0]
    specs, flat, first = [], [], 0
    for (_, mine, other, start, _), count in zip(parts, counts):

        def index(step, first=first, count=count, start=start // tile):
            return (0, start + jnp.clip(step - first, 0, count - 1))

        specs += [pl.BlockSpec((rows // 2, tile), index)] * 2
        flat += [mine, other]
        first += count
    return pl.pallas_call(
        functools.partial(join_body, [part[0] for part in parts], counts),
        grid=(first,),
        out_shape=jax.ShapeDtypeStruct((rows, first * tile), jnp.float32),
        in_specs=specs,
        out_specs=pl.BlockSpec((rows, tile), lambda step: (0, step)),
        compiler_params=pltpu.CompilerParams(vmem_limit_bytes=60 * 2**20),
    )(*flat)


def bias_lines(table, frames):
    heads, middle = table.shape[0], (table.shape[1] - 1) // 2
    half = -(-frames // 64) * 64
    above = jnp.broadcast_to(table[:, -1:], (heads, half - middle - 1))
    below = jnp.broadcast_to(table[:, :1], (heads, half - middle))
    return jnp.concatenate([table[:, middle:], above, below, table[:, :middle]], axis=1)


def bias_lines_back(sums, frames, reach):
    return jnp.concatenate(
        [
            jnp.sum(sums[:, frames - 1 + reach :], axis=1, keepdims=True),
            sums[:, frames - reach : frames - 1 + reach][:, ::-1],
            jnp.sum(sums[:, : frames - reach], axis=1, keepdims=True),
        ],
        axis=1,
    )


def eight_lines(*lines):
    lines = list(lines)
    return jnp.stack(lines + [jnp.zeros_like(lines[0])] * (-len(lines) % 8))


def per_device(
    sizes,
    inputs,
    cotangent,
    lengths,
    ffn1_in,
    ffn1_out,
    attn_qkv,
    attn_out,
    rel_table,
    conv_in,
    depth_kernel,
    conv_out,
    ffn2_in,
    ffn2_out,
    gains,
    biases,
    inner_biases,
):
    dp_size, fsdp_size = sizes
    axes = (("fsdp", fsdp_size), ("dp", dp_size))
    rows = Rows(fsdp_size)
    groups = Groups(axes)
    frames, width = inputs.shape
    taps = depth_kernel.shape[1]

    own_lines = jnp.concatenate([gains, biases, inner_biases, depth_kernel], axis=1)
    own_lines = jnp.pad(own_lines, ((0, 0), (0, -own_lines.shape[1] % 8))).astype(jnp.float32).T
    own_bias = bias_lines(rel_table.astype(jnp.float32), frames)
    own_bias = jnp.pad(own_bias, ((0, -own_bias.shape[0] % 8), (0, 0)))
    heads = rel_table.shape[0] * fsdp_size

    (
        (
            normed_one,
            hidden_one,
            slope_one,
            x1,
            normed_attn,
            *packed,
            context,
            x2,
            normed_conv,
            gated,
            gate,
            mixed,
            sums,
            lines,
            bias_table,
        ),
        (w_ffn1_in, w_ffn1_out, w_qkv, w_attn_out, w_conv_in),
    ) = front(
        inputs,
        own_lines,
        own_bias,
        lengths,
        heads,
        taps,
        (ffn1_in, ffn1_out, attn_qkv, attn_out, conv_in),
        fsdp_size,
        6,
    )
    totals, _ = sum_and_share(rows, axes, sums, 3, [], 0)
    results, shared = turn(
        x2,
        mixed,
        totals,
        cotangent,
        lengths,
        lines,
        conv_out,
        ffn2_in,
        ffn2_out,
        fsdp_size,
        7,
    )
    swish, normed_two, hidden_two, layer_out, low_two, before_two, low_conv = results[:7]
    grad, hat_grad, sums_final, sums_two, sums_batch = results[7:]
    arrays = (swish, normed_two, hidden_two, low_two, before_two, low_conv)
    left_swish, left_normed_two, right_hidden_two, left_low_two, right_before_two, right_low_conv = [
        [own, *others] for own, others in zip(arrays, shared)
    ]
    back, _ = sum_and_share(rows, axes, sums_batch, 2, [], 1)

    inner = hidden_two.shape[1]
    main, half, rest = inner * 3 // 4, inner * 3 // 8, inner // 4
    jobs = [
        (left_low_two, right_hidden_two, 0, main, (0, 0)),
        (left_normed_two, right_before_two, 0, main, (0, 1)),
        (left_low_two, right_hidden_two, main, rest, (0, 2)),
        (left_swish, right_low_conv, 0, width, (0, 2)),
        (left_normed_two, right_before_two, main, rest, (0, 3)),
    ]
    arrays = (normed_conv, context, normed_attn, normed_one)
    results, shared, bundles = groups.along(
        jobs,
        functools.partial(
            back_front,
            hat_grad,
            gated,
            gate,
            mixed,
            totals,
            back,
            grad,
            x2,
            x1,
            lines,
            bias_table,
            lengths,
            taps,
            packed,
            w_conv_in,
            w_attn_out,
            w_qkv,
            3,
            spread=True,
            carried=[(array, "columns") for array in arrays] + [(hidden_one, "all")],
        ),
    )
    two = bundles[0]
    *back_lefts, low_one, grad, sums_kernel, sums_conv, sums_attn, sums_rel = results
    right_one, right_two, right_low_attn, right_q, right_k, right_v, left_low_one = [
        [own, *others] for own, others in zip((*back_lefts, low_one), shared)
    ]
    left_normed_conv, left_context, left_normed_attn, left_normed_one, right_hidden_one = [
        [own, *others] for own, others in zip((*arrays, hidden_one), shared[7:])
    ]

    jobs = [
        (left_normed_conv, right_one, 0, width, (0, 0)),
        (left_normed_conv, right_two, 0, width, (0, 1)),
        (left_context, right_low_attn, 0, width, (0, 3)),
        (left_normed_attn, right_q, 0, width, (0, 0)),
        (left_normed_attn, right_k, 0, width, (0, 1)),
        (left_normed_attn, right_v, 0, width, (0, 3)),
        (left_low_one, right_hidden_one, 0, half, (1, 0)),
        (left_low_one, right_hidden_one, half, half, (1, 1)),
        (left_low_one, right_hidden_one, main, rest, (1, 2)),
        (left_normed_one, 0, 0, half, (2, 0)),
        (left_normed_one, 0, half, half, (2, 1)),
        (left_normed_one, 0, main, rest, (2, 3)),
    ]
    (_, input_grad, sums_one), _, bundles = groups.along(
        jobs,
        functools.partial(
            back_end, low_one, grad, inputs, lines, slope_one, w_ffn1_in, w_ffn1_out, 4
        ),
    )
    mid, out, end = bundles[0], bundles[1], bundles[2]

    bundles = (two, mid, out, end)
    middle, sums = groups.middle(
        [[bundle[kind] for bundle in bundles if kind in bundle] for kind in groups.kinds],
        (
            sums_one,
            sums_attn,
            sums_conv,
            sums_two,
            sums_final,
            sums_batch,
            sums_kernel,
            sums_rel,
        ),
        [(0, 1)] * 5 + [(2, 3), tuple(range(taps)), tuple(range(heads))],
        width,
        2,
    )
    middle = [iter(arrays) for arrays in middle]
    two, mid, out, end = [
        {kind: next(middle[kind]) for kind in groups.kinds if kind in bundle} for bundle in bundles
    ]
    mid, two = groups.finish(mid), groups.finish(two)
    sum_qkv = groups.join(*[(mid[kind], width, width) for kind in (0, 1, 3)])
    sum_conv_in = groups.join((mid[0], 0, width), (mid[1], 0, width))
    sum_attn_out = groups.join((mid[3], 0, width))
    out, sum_qkv, sum_conv_in = lax.optimization_barrier((out, sum_qkv, sum_conv_in))
    out = groups.finish(out)
    sum_ffn2_out = groups.join((two[0], 0, main), (two[2], 0, rest))
    sum_ffn2_in = groups.join((two[1], 0, main), (two[3], 0, rest))
    sum_conv_out = groups.join((two[2], rest, width))
    end, sum_ffn2_out = lax.optimization_barrier((end, sum_ffn2_out))
    end = groups.finish(end)
    sum_ffn1_out = groups.join((out[0], 0, half), (out[1], 0, half), (out[2], 0, rest))
    sum_ffn1_in = groups.join((end[0], 0, half), (end[1], 0, half), (end[3], 0, rest))
    own = lax.dynamic_slice_in_dim(sums, rows.me * gains.shape[0], gains.shape[0], axis=1)
    first = 12 + taps
    rel_sum = lax.dynamic_slice_in_dim(
        sums, first + rows.me * rel_table.shape[0], rel_table.shape[0], axis=0
    )
    rel_sum = bias_lines_back(
        rel_sum[:, : sums_rel.shape[1]], frames, (rel_table.shape[1] - 1) // 2
    )
    return (
        layer_out,
        input_grad,
        sum_ffn1_in,
        sum_ffn1_out,
        sum_qkv,
        sum_attn_out,
        rel_sum,
        sum_conv_in,
        own[12:first].T,
        sum_conv_out,
        sum_ffn2_in,
        sum_ffn2_out,
        own[0:12:2].T,
        jnp.stack([own[1], own[3], own[9]], axis=1),
        jnp.stack([own[5], own[7], own[11]], axis=1),
    )


def solution(mesh):
    frame_spec = P(("dp", "fsdp"), None)
    row_spec = P("fsdp", None)
    sizes = (mesh.shape["dp"], mesh.shape["fsdp"])
    return jax.shard_map(
        functools.partial(per_device, sizes),
        mesh=mesh,
        in_specs=(frame_spec,) * 3 + (row_spec,) * 13,
        out_specs=(frame_spec,) * 2 + (row_spec,) * 13,
        check_vma=False,
    )
```

```python
import functools

import jax
import jax.numpy as jnp
from jax import lax
from jax.experimental import pallas as pl
from jax.experimental.pallas import tpu as pltpu
from jax.sharding import PartitionSpec as P

EPSILON = 1e-05
MASKED = -1000000000.0
AHEAD = 4
DOWN_DIMS = (((0,), (0,)), ((), ()))
ACROSS_DIMS = (((1,), (1,)), ((), ()))


def pair_partners(axes):
    partners = []
    for name, size in axes:
        me = lax.axis_index(name)
        bit = 1
        while bit < size:
            partners.append({name: me + bit * (1 - 2 * ((me // bit) % 2))})
            bit *= 2
    return partners


def sum_stages(axes):
    near = [(name, 1 << k) for name, size in axes for k in range(size.bit_length() - 1)]
    stages = []
    while near:
        count = 3 if len(near) in (3, 5) or len(near) > 6 else 2
        stages.append(near[:count])
        near = near[count:]
    return stages


def stage_partners(bits):
    uppers = [lax.rem(lax.axis_index(name) // bit, 2) for name, bit in bits]
    place = sum(upper << k for k, upper in enumerate(uppers))
    devices = []
    for other in range(1 << len(bits)):
        device = {}
        for k, (name, bit) in enumerate(bits):
            start = device.get(name, lax.axis_index(name))
            device[name] = start + bit * (((other >> k) & 1) - uppers[k])
        devices.append(device)
    return place, devices


def pair_kernel(axes, modes, lines, *refs):
    refs = list(refs)

    def pick(count):
        picked = refs[:count]
        del refs[:count]
        return picked

    size = dict(axes)["fsdp"]
    (x_ref,), shared, (o_ref,) = pick(1), pick(len(modes)), pick(1)
    outs = [pick(size - 1) for _ in modes]
    slots, packed, send_sems, recv_sems, share_send, share_recv = refs
    tiles = x_ref.shape[1] // 128

    def lanes(index):
        return pl.ds(index // tiles, 1), pl.ds(index % tiles * 128, 128)

    stages = [stage_partners(bits) for bits in sum_stages(axes)]
    me = lax.axis_index("fsdp")
    peers = [{"fsdp": lax.rem(me + size - step, size)} for step in range(1, size)]
    barrier = pltpu.get_barrier_semaphore()
    greeted = 0
    for place, devices in stages:
        for other, device in enumerate(devices):

            @pl.when(other != place)
            def _(device=device):
                pl.semaphore_signal(
                    barrier, inc=1, device_id=device, device_id_type=pl.DeviceIdType.MESH
                )

        greeted += len(devices) - 1
    if modes and size > 2:
        for peer in peers:
            pl.semaphore_signal(barrier, inc=1, device_id=peer, device_id_type=pl.DeviceIdType.MESH)
        greeted += size - 1
    pl.semaphore_wait(barrier, greeted)
    copies = []
    for index, (mode, source) in enumerate(zip(modes, shared)):
        for step, peer in enumerate(peers):
            if mode == "columns":
                width = source.shape[1] // size
                start = pl.multiple_of(peer["fsdp"] * width, width)
                source_now = source.at[:, pl.ds(start, width)]
            else:
                source_now = source
            copies.append(
                pltpu.make_async_remote_copy(
                    src_ref=source_now,
                    dst_ref=outs[index][step],
                    send_sem=share_send.at[index, step],
                    recv_sem=share_recv.at[index, step],
                    device_id=peer,
                    device_id_type=pl.DeviceIdType.MESH,
                )
            )
    for index in range(packed.shape[0]):
        row, columns = lanes(index)
        packed[pl.ds(index, 1), :] = x_ref[row, columns]
    for stage, (place, devices) in enumerate(stages):

        def exchange(other, device, stage=stage, place=place):
            return pltpu.make_async_remote_copy(
                src_ref=packed,
                dst_ref=slots.at[stage, place],
                send_sem=send_sems.at[stage, other],
                recv_sem=recv_sems.at[stage, place],
                device_id=device,
                device_id_type=pl.DeviceIdType.MESH,
            )

        def arrival(other, device, stage=stage):
            return pltpu.make_async_remote_copy(
                src_ref=packed,
                dst_ref=slots.at[stage, other],
                send_sem=send_sems.at[stage, other],
                recv_sem=recv_sems.at[stage, other],
                device_id=device,
                device_id_type=pl.DeviceIdType.MESH,
            )

        for other, device in enumerate(devices):
            pl.when(other != place)(exchange(other, device).start)
        if stage == 0:
            for copy in copies:
                copy.start()
        for other, device in enumerate(devices):
            pl.when(other != place)(arrival(other, device).wait)
        slots[stage, pl.ds(place, 1)] = packed[...][None]
        total = slots[stage, 0]
        for other in range(1, len(devices)):
            total += slots[stage, other]
        packed[...] = total
    o_ref[...] = jnp.zeros_like(o_ref)
    for index in range(packed.shape[0]):
        row, columns = lanes(index)
        o_ref[row, columns] = packed[pl.ds(index, 1), :]
    for copy in copies:
        copy.wait()


def sum_and_share(rows, axes, values, lines, shared, collective_id):
    size = dict(axes)["fsdp"]
    stages = len(sum_stages(axes))
    if any(count & (count - 1) for _, count in axes) or stages == 0:
        total = lax.psum(values, tuple(name for name, _ in axes))
        total = jnp.concatenate([total[:lines], jnp.zeros_like(total[lines:])])
        return total, [
            (rows.all_frames if mode == "all" else rows.all_frames_own_columns)(array)[1:]
            for array, mode in shared
        ]
    packed = (lines * values.shape[1] // 128, 128)
    shapes = [
        array.shape if mode == "all" else (array.shape[0], array.shape[1] // size)
        for array, mode in shared
    ]
    out = pl.pallas_call(
        functools.partial(pair_kernel, axes, [mode for _, mode in shared], lines),
        out_shape=[jax.ShapeDtypeStruct(values.shape, values.dtype)]
        + [
            jax.ShapeDtypeStruct(shape, array.dtype)
            for shape, (array, _) in zip(shapes, shared)
            for _ in range(size - 1)
        ],
        in_specs=[pl.BlockSpec(memory_space=pltpu.VMEM)]
        + [pl.BlockSpec(memory_space=pl.ANY)] * len(shared),
        out_specs=[pl.BlockSpec(memory_space=pltpu.VMEM)]
        + [pl.BlockSpec(memory_space=pl.ANY)] * (len(shared) * (size - 1)),
        scratch_shapes=[
            pltpu.VMEM((stages, 8) + packed, values.dtype),
            pltpu.VMEM(packed, values.dtype),
            pltpu.SemaphoreType.DMA((stages, 8)),
            pltpu.SemaphoreType.DMA((stages, 8)),
            pltpu.SemaphoreType.DMA((max(len(shared), 1), max(size - 1, 1))),
            pltpu.SemaphoreType.DMA((max(len(shared), 1), max(size - 1, 1))),
        ],
        compiler_params=pltpu.CompilerParams(
            collective_id=collective_id, has_side_effects=True, vmem_limit_bytes=60 * 2**20
        ),
    )(values, *[array for array, _ in shared])
    return out[0], [
        out[1 + k * (size - 1) : 1 + (k + 1) * (size - 1)] for k in range(len(shared))
    ]


class Rows:
    def __init__(self, size):
        self.size = size
        self.me = lax.axis_index("fsdp")

    def owner(self, step):
        return lax.rem(self.me + step, self.size)

    def shift(self, values, step):
        return lax.ppermute(
            values, "fsdp", [(j, (j - step) % self.size) for j in range(self.size)]
        )

    def gather(self, block):
        return [(self.me, block)] + [
            (self.owner(step), self.shift(block, step)) for step in range(1, self.size)
        ]

    def columns(self, values, owner):
        width = values.shape[1] // self.size
        return lax.dynamic_slice_in_dim(values, owner * width, width, axis=1)

    def order(self, parts, axis):
        if self.size == 1:
            return parts[0]
        width = parts[0].shape[axis]
        twice = jnp.concatenate(parts + parts, axis=axis)
        start = lax.rem(self.size - self.me, self.size) * width
        return lax.dynamic_slice_in_dim(twice, start, width * self.size, axis=axis)

    def all_frames(self, values):
        return [values] + [self.shift(values, step) for step in range(1, self.size)]

    def all_frames_own_columns(self, values):
        return [self.columns(values, self.me)] + [
            self.shift(self.columns(values, self.owner(self.size - step)), step)
            for step in range(1, self.size)
        ]


def cube_rounds(bits, line):
    swaps = bits[:-2] if line and tuple(bits[-2:]) == line else bits
    rounds = tuple(("swap", bit) for bit in swaps)
    return rounds if swaps == bits else rounds + (("give", line[0]), ("mid", line[0]))


def cube_kernel(axes, plan, lines, *refs):
    me = lax.axis_index("dp")
    refs = list(refs)

    def pick(count):
        picked = refs[:count]
        del refs[:count]
        return picked

    arrays = [len(columns) for _, columns, _ in plan]
    inputs, small_refs = pick(2 * sum(arrays)), pick(len(lines))
    outputs, (small_out,) = pick(sum(arrays)), pick(1)
    kinds, first = [], 0
    for rounds, columns, chunk in plan:
        whole, other, result = pick(3)
        sums = pick(len(rounds))
        send_sems, recv_sems = pick(2)
        rows, start, steps = whole.shape[0], 0, []
        for name, bit in rounds:
            step = dict(name=name, rows=rows, before=start)
            if name == "swap":
                step["upper"] = lax.rem(me // bit, 2)
                step["partner"] = me + bit * (1 - 2 * step["upper"])
                step["sends"] = step["takes"] = None
            else:
                place = lax.rem(me // bit, 4)
                inner = (place == 1) | (place == 2)
                if name == "give":
                    step["partner"] = me + bit * (1 - 2 * lax.rem(place, 2))
                    step["sends"], step["takes"] = jnp.logical_not(inner), inner
                else:
                    step["upper"] = place // 2
                    step["partner"] = me + bit * (1 - 2 * step["upper"])
                    step["sends"] = step["takes"] = inner
            if name != "give":
                rows //= 2
                start = start + step["upper"] * rows
            step["after"] = start
            steps.append(step)
        edges = [sum(columns[:k]) for k in range(len(columns) + 1)]
        kinds.append(
            dict(
                steps=steps,
                columns=columns,
                edges=edges,
                chunk=chunk,
                count=edges[-1] // chunk,
                whole=whole,
                other=other,
                result=result,
                sums=sums,
                send=send_sems,
                recv=recv_sems,
                first=first,
            )
        )
        first += len(columns)
    load_sems, store_sems, slots, small_send, small_recv = refs
    partners = pair_partners(axes)

    def loads(kind, place):
        index = kind["first"] + place
        columns = pl.ds(kind["edges"][place], kind["columns"][place])
        return [
            pltpu.make_async_copy(
                inputs[2 * index + term],
                kind[name].at[:, columns],
                load_sems.at[2 * index + term],
            )
            for term, name in enumerate(("whole", "other"))
        ]

    def store(kind, place):
        index = kind["first"] + place
        columns = pl.ds(kind["edges"][place], kind["columns"][place])
        return pltpu.make_async_copy(
            kind["result"].at[:, columns], outputs[index], store_sems.at[index]
        )

    for place in range(max(arrays)):
        for kind in kinds:
            if place < len(kind["columns"]):
                for copy in loads(kind, place):
                    copy.start()
    small_out[...] = jnp.zeros_like(small_out)
    line = 0
    for ref, rows in zip(small_refs, lines):
        for row in rows:
            small_out[line : line + 1, : ref.shape[1]] = ref[row : row + 1, :]
            line += 1
    barrier = pltpu.get_barrier_semaphore()
    lines = sorted({bit for rounds, _, _ in plan for name, bit in rounds if name == "mid"})
    for partner in partners:
        pl.semaphore_signal(barrier, inc=1, device_id=partner, device_id_type=pl.DeviceIdType.MESH)
    if lines:
        (bit,) = lines
        place = lax.rem(me // bit, 4)
        inner = (place == 1) | (place == 2)

        @pl.when(inner)
        def _():
            pl.semaphore_signal(
                barrier,
                inc=1,
                device_id={"dp": me + bit * (1 - 2 * (place // 2))},
                device_id_type=pl.DeviceIdType.MESH,
            )
            pl.semaphore_wait(barrier, len(partners) + 1)

        @pl.when(jnp.logical_not(inner))
        def _():
            pl.semaphore_wait(barrier, len(partners))

    else:
        pl.semaphore_wait(barrier, len(partners))

    def window(kind, index):
        return pl.ds(pl.multiple_of(index * kind["chunk"], kind["chunk"]), kind["chunk"])

    def aligned(start, rows):
        return pl.ds(start if isinstance(start, int) else pl.multiple_of(start, rows), rows)

    def source(kind, number):
        return kind["whole"] if number == 0 else kind["sums"][number - 1]

    def copy_in(kind, number, index):
        step, columns = kind["steps"][number], window(kind, index)
        rows = step["rows"]
        given = pl.ds(0, rows)
        if step["name"] != "give":
            given = aligned((1 - step["upper"]) * (rows // 2), rows // 2)
        return pltpu.make_async_remote_copy(
            src_ref=source(kind, number).at[given, columns],
            dst_ref=kind["sums"][number].at[:, columns],
            send_sem=kind["send"].at[number, index],
            recv_sem=kind["recv"].at[number, index],
            device_id={"dp": step["partner"]},
            device_id_type=pl.DeviceIdType.MESH,
        )

    def copy_out(kind, number, index):
        step = kind["steps"][number]
        rows = step["rows"] if step["name"] == "give" else step["rows"] // 2
        start = step["before"] if step["name"] == "give" else step["after"]
        block = kind["result"].at[aligned(start, rows), window(kind, index)]
        slot = 2 * len(kind["steps"]) - 1 - number
        return pltpu.make_async_remote_copy(
            src_ref=block,
            dst_ref=block,
            send_sem=kind["send"].at[slot, index],
            recv_sem=kind["recv"].at[slot, index],
            device_id={"dp": step["partner"]},
            device_id_type=pl.DeviceIdType.MESH,
        )

    def when(condition, action):
        if condition is None:
            action()
        else:
            pl.when(condition)(action)

    def end_in(kind, number, index):
        step, columns = kind["steps"][number], window(kind, index)
        copy = copy_in(kind, number, index)
        last = number == len(kind["steps"]) - 1

        def add():
            copy.wait_recv()
            rows = step["rows"]
            kept = pl.ds(0, rows)
            if step["name"] != "give":
                rows //= 2
                kept = aligned(step["upper"] * rows, rows)
            total = (
                source(kind, number)[kept, columns].astype(jnp.float32)
                + kind["sums"][number][:, columns].astype(jnp.float32)
            ).astype(kind["whole"].dtype)
            if last:
                kind["result"][aligned(step["after"], rows), columns] = total
            else:
                kind["sums"][number][:, columns] = total

        when(step["sends"], copy.wait_send)
        when(step["takes"], add)

    def advance(kind, stage, index):
        depth = len(kind["steps"])
        if stage == 0:
            for place, edge in enumerate(kind["edges"][:-1]):

                @pl.when(index == edge // kind["chunk"])
                def _(place=place):
                    for copy in loads(kind, place):
                        copy.wait()

            columns = window(kind, index)
            kind["whole"][:, columns] = (
                kind["whole"][:, columns].astype(jnp.float32)
                + kind["other"][:, columns].astype(jnp.float32)
            ).astype(kind["whole"].dtype)
        elif stage <= depth:
            end_in(kind, stage - 1, index)
        else:
            number = 2 * depth - stage
            step = kind["steps"][number]
            copy = copy_out(kind, number, index)
            when(step["takes"], copy.wait_send)
            when(step["sends"], copy.wait_recv)
        if stage < depth:
            when(kind["steps"][stage]["sends"], copy_in(kind, stage, index).start)
        elif stage < 2 * depth:
            number = 2 * depth - 1 - stage
            when(kind["steps"][number]["takes"], copy_out(kind, number, index).start)
        else:
            for place, edge in enumerate(kind["edges"][1:]):

                @pl.when(index == edge // kind["chunk"] - 1)
                def _(place=place):
                    store(kind, place).start()

    def exchange(stage):
        return pltpu.make_async_remote_copy(
            src_ref=small_out,
            dst_ref=slots.at[stage],
            send_sem=small_send.at[stage],
            recv_sem=small_recv.at[stage],
            device_id=partners[stage],
            device_id_type=pl.DeviceIdType.MESH,
        )

    last = max(kind["count"] + 2 * len(kind["steps"]) for kind in kinds)
    last = max(last, len(partners) + 1)

    @pl.loop(0, last)
    def _(tick):
        for stage in range(len(partners) + 1):

            @pl.when(tick == stage)
            def _(stage=stage):
                if stage > 0:
                    exchange(stage - 1).wait()
                    small_out[...] += slots[stage - 1]
                if stage < len(partners):
                    exchange(stage).start()

        for stage in range(2 * max(len(kind["steps"]) for kind in kinds) + 1):
            for kind in kinds:
                if stage <= 2 * len(kind["steps"]):

                    @pl.when((tick >= stage) & (tick < stage + kind["count"]))
                    def _(kind=kind, stage=stage):
                        advance(kind, stage, tick - stage)

    for kind in kinds:
        for place in range(len(kind["columns"])):
            store(kind, place).wait()


def sum_cube(axes, parts, plan, small, lines, width, collective_id):
    shape = (-(-sum(len(rows) for rows in lines) // 8) * 8, width)
    flat = [term for kind in parts for pair in kind for term in pair]
    scratch = []
    for kind, (rounds, columns, chunk) in zip(parts, plan):
        rows, total, dtype = kind[0][0].shape[0], sum(columns), kind[0][0].dtype
        scratch += [pltpu.VMEM((rows, total), dtype)] * 3
        for name, _ in rounds:
            rows = rows if name == "give" else rows // 2
            scratch.append(pltpu.VMEM((rows, total), dtype))
        scratch += [pltpu.SemaphoreType.DMA((2 * len(rounds), total // chunk))] * 2
    stages = sum(size.bit_length() - 1 for _, size in axes)
    scratch += [
        pltpu.SemaphoreType.DMA((len(flat),)),
        pltpu.SemaphoreType.DMA((len(flat) // 2,)),
        pltpu.VMEM((stages,) + shape, jnp.float32),
        pltpu.SemaphoreType.DMA((stages,)),
        pltpu.SemaphoreType.DMA((stages,)),
    ]
    *out, sums = pl.pallas_call(
        functools.partial(cube_kernel, axes, plan, lines),
        out_shape=[jax.ShapeDtypeStruct(own.shape, own.dtype) for kind in parts for own, _ in kind]
        + [jax.ShapeDtypeStruct(shape, jnp.float32)],
        in_specs=[pl.BlockSpec(memory_space=pl.ANY)] * len(flat)
        + [pl.BlockSpec(memory_space=pltpu.VMEM)] * len(small),
        out_specs=[pl.BlockSpec(memory_space=pl.ANY)] * (len(flat) // 2)
        + [pl.BlockSpec(memory_space=pltpu.VMEM)],
        scratch_shapes=scratch,
        compiler_params=pltpu.CompilerParams(
            collective_id=collective_id, has_side_effects=True, vmem_limit_bytes=60 * 2**20
        ),
    )(*flat, *small)
    result = []
    for kind in parts:
        result.append(out[: len(kind)])
        out = out[len(kind) :]
    return result, sums


class Groups:
    def __init__(self, axes):
        self.axes = axes
        self.size = dict(axes)["dp"]
        self.me = lax.axis_index("dp")
        bits = [1 << k for k in range(self.size.bit_length() - 1)]
        self.plain = any(size & (size - 1) for _, size in axes) or not bits
        first, rest = bits[:3], bits[3:]
        self.orders = [[1]] * 4
        if first:
            one, two, three = first[0], first[1 % len(first)], first[2 % len(first)]
            orders = (
                (one, two, three, *rest),
                (two, one, three, *rest),
                (three, one, two, *rest),
                (three, two, one, *rest),
            )
            self.orders = [list(dict.fromkeys(order)) for order in orders]
        self.kinds = range(len(self.orders))
        self.line = tuple(bits[-2:]) if len(bits) > 3 else ()

    def swap(self, values, bit):
        return lax.ppermute(values, "dp", [(j, j ^ bit) for j in range(self.size)])

    def upper(self, bit):
        return lax.rem(self.me // bit, 2)

    def in_order(self, bit, mine, other):
        low = self.upper(bit) == 0
        return jnp.concatenate([jnp.where(low, mine, other), jnp.where(low, other, mine)], axis=0)

    def along(self, jobs, call, **arguments):
        bits = [order[0] for order in self.orders]
        lefts = jobs[0][0]
        if self.plain or lefts[0].shape[1] // len(lefts) % 256:
            results, received, _ = call(**arguments)
            jobs = [
                (lefts, [results[rights], *received[0]] if isinstance(rights, int) else rights, *rest)
                for lefts, rights, *rest in jobs
            ]
            pairs = {
                key: (keep, give if self.plain else self.swap(give, bits[key[1]]))
                for key, (give, keep) in halves_plainly(jobs, bits).items()
            }
        else:
            results, received, pairs = call(**arguments, jobs=jobs, bits=bits)
        bundles = {}
        for (bundle, kind), pair in pairs.items():
            bundles.setdefault(bundle, {})[kind] = pair
        return results, received, bundles

    def middle(self, parts, small, lines, width, collective_id):
        if self.plain:
            sums = self.stacked(small, lines, width)
            return parts, lax.psum(sums, tuple(name for name, _ in self.axes))
        plan, fits = [], True
        for order, arrays in zip(self.orders, parts):
            columns = tuple(own.shape[1] for own, _ in arrays)
            blocks = sum(columns) // 128
            chunk = 512 if blocks >= 48 else 256
            plan.append((cube_rounds(order[1:], self.line), columns, chunk))
            fits &= all(count % chunk == 0 for count in columns)
            fits &= (arrays[0][0].shape[0] >> len(order[1:])) % 16 == 0 and len(order) > 1
        if fits:
            return sum_cube(self.axes, parts, plan, small, lines, width, collective_id)
        sums = [
            [self.rounds(order[1:], own, other) for own, other in arrays]
            for order, arrays in zip(self.orders, parts)
        ]
        small = self.stacked(small, lines, width)
        return sums, sum_and_share(None, self.axes, small, small.shape[0], [], collective_id)[0]

    def stacked(self, small, lines, width):
        rows = [
            jnp.pad(array[row], (0, width - array.shape[1]))
            for array, picked in zip(small, lines)
            for row in picked
        ]
        return eight_lines(*rows)

    def rounds(self, bits, own, other):
        total = (own.astype(jnp.float32) + other.astype(jnp.float32)).astype(jnp.bfloat16)
        for bit in bits:
            count = total.shape[0] // 2
            given = lax.dynamic_slice_in_dim(total, (1 - self.upper(bit)) * count, count, axis=0)
            mine = lax.dynamic_slice_in_dim(total, self.upper(bit) * count, count, axis=0)
            other = self.swap(given, bit)
            total = (mine.astype(jnp.float32) + other.astype(jnp.float32)).astype(jnp.bfloat16)
        for bit in reversed(bits):
            total = self.in_order(bit, total, self.swap(total, bit))
        return total

    def finish(self, bundle):
        if self.plain:
            return {kind: (self.orders[kind][0], *pair) for kind, pair in bundle.items()}
        return {
            kind: (self.orders[kind][0], total, self.swap(total, self.orders[kind][0]))
            for kind, total in bundle.items()
        }

    def join(self, *parts):
        if self.plain:
            return jnp.concatenate(
                [
                    lax.psum(
                        self.in_order(*halves)[:, first : first + columns].astype(jnp.float32),
                        "dp",
                    )
                    for halves, first, columns in parts
                ],
                axis=1,
            )
        return join([(*halves, first, columns) for halves, first, columns in parts])


class Flow:
    def __init__(self, sources, held, in_sems, results, staged, out_sems, chunks):
        self.sources, self.held, self.in_sems = sources, held, in_sems
        self.results, self.staged, self.out_sems = results, staged, out_sems
        self.chunks = chunks
        self.sent, self.shared = [], []

    def copy_in(self, index, part):
        width = self.chunks[index]
        columns = pl.ds(part * width, width)
        first = sum(
            source.shape[1] // chunk for source, chunk in zip(self.sources[:index], self.chunks)
        )
        return pltpu.make_async_copy(
            self.sources[index].at[:, columns],
            self.held[index].at[:, columns],
            self.in_sems.at[first + part],
        )

    def start(self, order):
        for index, part in order:
            self.copy_in(index, part).start()

    def pulls(self, held, outs, sems, small):
        self.pull_held, self.pull_outs, self.pull_sems, self.pull_small = held, outs, sems, small
        self.pull_slots, self.pulled = {}, []

    def push(self, order):
        me = lax.axis_index("fsdp")
        for own, places in self.pull_small:
            for step, peer in enumerate(self.peers):
                self.push_one(("small", id(places)), 0, step, peer, own, places[step])
        for index, part in order:
            if index in self.pull_held:
                columns = pl.ds(part * self.chunks[index], self.chunks[index])
                for step, peer in enumerate(self.peers):
                    target = self.pull_held[index][step].at[:, columns]
                    source = self.sources[index].at[:, columns]
                    self.push_one(index, part, step, peer, source, target)

    def carry(self, sources, modes, outs, sems):
        for index, (source, mode) in enumerate(zip(sources, modes)):
            for step, peer in enumerate(self.peers):
                given = source
                if mode == "columns":
                    width = source.shape[1] // self.size
                    given = source.at[:, pl.ds(pl.multiple_of(peer * width, width), width)]
                copy = pltpu.make_async_remote_copy(
                    src_ref=given,
                    dst_ref=outs[index][step],
                    send_sem=sems[0].at[index, step],
                    recv_sem=sems[1].at[index, step],
                    device_id={"fsdp": peer},
                    device_id_type=pl.DeviceIdType.MESH,
                )
                copy.start()
                self.shared.append(copy)

    def push_one(self, index, part, step, peer, source, target):
        send_sems, recv_sems, _ = self.pull_sems
        slot = len(self.pull_slots)
        copy = pltpu.make_async_remote_copy(
            src_ref=source,
            dst_ref=target,
            send_sem=send_sems.at[slot],
            recv_sem=recv_sems.at[slot],
            device_id={"fsdp": peer},
            device_id_type=pl.DeviceIdType.MESH,
        )
        self.pull_slots[index, part, step] = (slot, copy)
        copy.start()

    def take_small(self, places):
        for step in range(len(self.peers)):
            self.pull_slots[("small", id(places)), 0, step][1].wait_recv()
        return places

    def take_all(self, index, part=0):
        blocks = [self.take(index, part)]
        width = self.chunks[index]
        columns = pl.ds(part * width, width)
        for step in range(len(self.peers)):
            slot, copy = self.pull_slots[index, part, step]
            copy.wait_recv()
            block = self.pull_held[index][step].at[:, columns]
            blocks.append(block)
            if not self.pull_outs:
                continue
            out = pltpu.make_async_copy(
                block, self.pull_outs[index][step].at[:, columns], self.pull_sems[2].at[slot]
            )
            out.start()
            self.pulled.append(out)
        return blocks

    def held_all(self, index, part):
        columns = pl.ds(part * self.chunks[index], self.chunks[index])
        return [block.at[:, columns] for block in [self.held[index], *self.pull_held[index]]]

    def take(self, index, part=0):
        self.copy_in(index, part).wait()
        width = self.chunks[index]
        return self.held[index].at[:, pl.ds(part * width, width)]

    def put(self, index, columns=None):
        columns = slice(None) if columns is None else columns
        copy = pltpu.make_async_copy(
            self.staged[index].at[:, columns],
            self.results[index].at[:, columns],
            self.out_sems.at[len(self.sent)],
        )
        copy.start()
        self.sent.append(copy)

    def greet(self, shares, outs, sems, size):
        me = lax.axis_index("fsdp")
        self.shares, self.share_outs, self.share_sems, self.size = shares, outs, sems, size
        self.peers = [lax.rem(me + size - step, size) for step in range(1, size)]

    def share(self, index):
        place = list(self.shares).index(index)
        send_sems, recv_sems = self.share_sems
        for step, peer in enumerate(self.peers):
            source = self.staged[index]
            if self.shares[index] == "columns":
                width = source.shape[1] // self.size
                source = source.at[:, pl.ds(pl.multiple_of(peer * width, width), width)]
            copy = pltpu.make_async_remote_copy(
                src_ref=source,
                dst_ref=self.share_outs[place][step],
                send_sem=send_sems.at[place, step],
                recv_sem=recv_sems.at[place, step],
                device_id={"fsdp": peer},
                device_id_type=pl.DeviceIdType.MESH,
            )
            copy.start()
            self.shared.append(copy)

    def wait_shared(self):
        for copy in self.shared:
            copy.wait()
        self.shared = []

    def finish(self):
        for copy in self.sent + self.shared + self.pulled:
            copy.wait()
        for _, copy in self.pull_slots.values():
            copy.wait_send()


class Grads:
    AHEAD = 6

    def __init__(self, plan, lefts, rights, outs, lefts_held, scratch):
        self.steps, self.bits, self.count, self.tile = plan
        self.lefts, self.rights, self.outs, self.lefts_held = lefts, rights, outs, lefts_held
        self.rights_held, self.staged, *sems = scratch
        self.left_sems, self.right_sems, self.out_sems, self.send_sems, self.recv_sems = sems
        self.frames, self.rows = lefts[0][0].shape[0], self.staged.shape[0]
        self.half = self.rows // 2
        self.me = lax.axis_index("dp")

    def partners(self):
        bits = sorted({self.bits[step[3][1]] for step in self.steps})
        return [{"dp": self.me + bit * (1 - 2 * lax.rem(self.me // bit, 2))} for bit in bits]

    def left_in(self, group, place):
        source = self.lefts[group][place]
        return pltpu.make_async_copy(
            source.at[:, own_columns(self.count, 0, self.rows)] if place == 0 else source,
            self.lefts_held[group].at[pl.ds(place * self.frames, self.frames)],
            self.left_sems.at[group, place],
        )

    def right_in(self, index, place):
        _, right, first, _, _ = self.steps[index]
        return pltpu.make_async_copy(
            self.rights[right][place].at[:, pl.ds(first, self.tile)],
            self.rights_held.at[index % self.AHEAD, pl.ds(place * self.frames, self.frames)],
            self.right_sems.at[index, place],
        )

    def halves_out(self, index):
        _, _, _, key, start = self.steps[index]
        bit = self.bits[key[1]]
        upper = lax.rem(self.me // bit, 2)
        source, columns = [
            self.staged.at[
                pl.ds(pl.multiple_of(part * self.half, self.half), self.half),
                pl.ds(index * self.tile, self.tile),
            ]
            for part in (1 - upper, upper)
        ], pl.ds(start, self.tile)
        keep, recv = self.outs[key]
        return (
            pltpu.make_async_remote_copy(
                src_ref=source[0],
                dst_ref=recv.at[:, columns],
                send_sem=self.send_sems.at[index],
                recv_sem=self.recv_sems.at[index],
                device_id={"dp": self.me + bit * (1 - 2 * upper)},
                device_id_type=pl.DeviceIdType.MESH,
            ),
            pltpu.make_async_copy(source[1], keep.at[:, columns], self.out_sems.at[index]),
        )

    def begin(self, first, last):
        self.first, self.last, self.loaded = first, last, set()
        for index in range(first, min(first + self.AHEAD, last)):
            self.load(index)

    def load(self, index):
        group = self.steps[index][0]
        for place in range(self.count):
            if group not in self.loaded:
                self.left_in(group, place).start()
            self.right_in(index, place).start()
        self.loaded.add(group)

    def run(self, then):
        waited = set()
        for index in range(self.first, self.last):
            step = self.steps[index]
            for place in range(self.count):
                if step[0] not in waited:
                    self.left_in(step[0], place).wait()
                self.right_in(index, place).wait()
            waited.add(step[0])
            right = self.rights_held[index % self.AHEAD]
            product = dot_down(self.lefts_held[step[0]][...], right)
            self.staged[:, pl.ds(index * self.tile, self.tile)] = product.astype(jnp.bfloat16)
            for copy in self.halves_out(index):
                copy.start()
            if index + self.AHEAD < self.last:
                self.load(index + self.AHEAD)
            if index == max(self.last - self.AHEAD - 1, self.first):
                then()

    def finish(self):
        for index in range(len(self.steps)):
            for copy in self.halves_out(index):
                copy.wait()


def gradient_plan(jobs, tile, spread):
    lefts, rights, steps, totals = [], [], [], {}
    for job_lefts, job_rights, first, columns, key in jobs:
        for known, group in ((lefts, job_lefts), (rights, job_rights)):
            if not any(group is other for other in known):
                known.append(group)
        left = [group is job_lefts for group in lefts].index(True)
        right = [group is job_rights for group in rights].index(True)
        for start in range(0, columns, tile):
            steps.append((left, right, first + start, key, totals.setdefault(key, 0)))
            totals[key] += tile
    turns = {key: 0 for key in totals}
    ranks = []
    for step in steps:
        turns[step[3]] += 1
        ranks.append((turns[step[3]] - 0.5) / (totals[step[3]] // tile))
    late = [isinstance(rights[step[1]], int) for step in steps]
    keys = [(late[k], ranks[k] if spread else k) for k in range(len(steps))]
    steps = [steps[k] for k in sorted(range(len(steps)), key=lambda k: keys[k])]
    return lefts, rights, steps, totals


def fused(
    body,
    small,
    large,
    results,
    order=None,
    scratch=(),
    shares=None,
    size=1,
    collective_id=None,
    jobs=(),
    bits=(),
    pulls=(),
    small_pulls=(),
    carried=(),
    pulls_stay=False,
    spread=False,
):
    shares = {} if shares is None or size == 1 else shares
    chunks = [width for _, width in large]
    parts = [array.shape[1] // width for array, width in large]
    if order is None:
        order = [(index, part) for index, count in enumerate(parts) for part in range(count)]
    share_shapes = [
        (shape if mode == "all" else (shape[0], shape[1] // size), dtype)
        for (shape, dtype), mode in ((results[index], mode) for index, mode in shares.items())
        for _ in range(size - 1)
    ]
    pulls = list(pulls) if size > 1 else []
    pull_shapes = [
        (large[index][0].shape, large[index][0].dtype) for index in pulls for _ in range(size - 1)
    ]
    carried = list(carried) if size > 1 else []
    carry_shapes = [
        (array.shape if mode == "all" else (array.shape[0], array.shape[1] // size), array.dtype)
        for array, mode in carried
        for _ in range(size - 1)
    ]
    pull_count = (sum(parts[index] for index in pulls) + len(small_pulls)) * (size - 1)
    tile = 512
    lefts, rights, steps, totals = gradient_plan(jobs, tile, spread)
    early = len([step for step in steps if not isinstance(rights[step[1]], int)])
    flat = [array for group in lefts + rights if not isinstance(group, int) for array in group]
    half_shapes, grad_scratch = [], []
    if jobs:
        count, frames = len(lefts[0]), lefts[0][0].shape[0]
        rows = lefts[0][0].shape[1] // count
        half_shapes = [
            ((rows // 2, columns), jnp.bfloat16) for columns in totals.values() for _ in range(2)
        ]
        grad_scratch = [pltpu.VMEM((count * frames, rows), jnp.bfloat16) for _ in lefts] + [
            pltpu.VMEM((Grads.AHEAD, count * frames, tile), jnp.bfloat16),
            pltpu.VMEM((rows, len(steps) * tile), jnp.bfloat16),
            pltpu.SemaphoreType.DMA((len(lefts), count)),
            pltpu.SemaphoreType.DMA((len(steps), count)),
        ] + [pltpu.SemaphoreType.DMA((len(steps),))] * 3

    def kernel(*refs):
        refs = list(refs)

        def pick(count):
            picked = refs[:count]
            del refs[:count]
            return picked

        small_refs, sources = pick(len(small)), pick(len(large))
        left_refs = [pick(len(group)) for group in lefts]
        right_refs = [group if isinstance(group, int) else pick(len(group)) for group in rights]
        carry_refs = pick(len(carried))
        outs = pick(len(results))
        share_outs = [pick(size - 1) for _ in shares]
        half_outs = {key: pick(2) for key in totals}
        pull_outs = {} if pulls_stay else {index: pick(size - 1) for index in pulls}
        carry_outs = [pick(size - 1) for _ in carried]
        held, staged, rest = pick(len(large)), pick(len(results)), pick(len(scratch))
        in_sems, out_sems = pick(2)
        share_sems = pick(2) if shares else []
        pull_held = {index: pick(size - 1) for index in pulls}
        pull_small = [(small_refs[index], pick(size - 1)) for index in small_pulls]
        pull_sems = pick(3) if pull_count else []
        carry_sems = pick(2) if carried else []
        flow = Flow(sources, held, in_sems, outs, staged, out_sems, chunks)
        greeted = []
        if jobs:
            plan = (steps, bits, len(lefts[0]), tile)
            for place, group in enumerate(right_refs):
                if isinstance(group, int):
                    others = share_outs[list(shares).index(group)] if shares else []
                    right_refs[place] = [staged[group], *others]
            grads = Grads(plan, left_refs, right_refs, half_outs, pick(len(lefts)), refs)
            grads.begin(0, early)
            greeted = grads.partners()
        flow.greet(shares, share_outs, share_sems, size)
        flow.pulls(pull_held, pull_outs, pull_sems, pull_small)
        if pull_count:
            flow.start(order)
        if shares or pull_count or carried:
            greeted += [{"fsdp": peer} for peer in flow.peers]
        if greeted:
            barrier = pltpu.get_barrier_semaphore()
            for device in greeted:
                pl.semaphore_signal(
                    barrier, inc=1, device_id=device, device_id_type=pl.DeviceIdType.MESH
                )
            pl.semaphore_wait(barrier, len(greeted))
        if carried:
            modes = [mode for _, mode in carried]
            flow.carry(carry_refs, modes, carry_outs, carry_sems)
        if jobs:
            grads.run(functools.partial(flow.start, order))
        elif pull_count:
            flow.push(order)
        else:
            flow.start(order)
        if body is not None:
            body(flow, small_refs, rest)
        if early < len(steps):
            flow.wait_shared()
            grads.begin(early, len(steps))
            grads.run(lambda: None)
        flow.finish()
        if jobs:
            grads.finish()

    semaphores = [
        pltpu.SemaphoreType.DMA((max(sum(parts), 1),)),
        pltpu.SemaphoreType.DMA((64,)),
    ]
    params = dict(vmem_limit_bytes=60 * 2**20)
    if shares:
        semaphores += [pltpu.SemaphoreType.DMA((len(shares), size - 1))] * 2
    pull_scratch = []
    if pull_count:
        pull_scratch = [pltpu.VMEM(shape, dtype) for shape, dtype in pull_shapes] + [
            pltpu.VMEM(small[index].shape, small[index].dtype)
            for index in small_pulls
            for _ in range(size - 1)
        ]
        pull_scratch += [pltpu.SemaphoreType.DMA((pull_count,))] * 3
    if carried:
        pull_scratch += [pltpu.SemaphoreType.DMA((len(carried), size - 1))] * 2
    if shares or jobs or pull_count or carried:
        params.update(collective_id=collective_id, has_side_effects=True)
    pull_results = [] if pulls_stay else pull_shapes
    shapes = results + share_shapes + half_shapes + pull_results + carry_shapes
    out = pl.pallas_call(
        kernel,
        out_shape=[jax.ShapeDtypeStruct(shape, dtype) for shape, dtype in shapes],
        in_specs=[
            pl.BlockSpec(memory_space=pltpu.SMEM if array.dtype == jnp.int32 else pltpu.VMEM)
            for array in small
        ]
        + [pl.BlockSpec(memory_space=pl.ANY)] * (len(large) + len(flat) + len(carried)),
        out_specs=[pl.BlockSpec(memory_space=pl.ANY)] * len(shapes),
        scratch_shapes=[pltpu.VMEM(array.shape, array.dtype) for array, _ in large]
        + [pltpu.VMEM(shape, dtype) for shape, dtype in results]
        + list(scratch)
        + semaphores
        + pull_scratch
        + grad_scratch,
        compiler_params=pltpu.CompilerParams(**params),
    )(*small, *[array for array, _ in large], *flat, *[array for array, _ in carried])
    others = out[len(results) : len(results) + len(share_shapes)]
    received = [others[k * (size - 1) : (k + 1) * (size - 1)] for k in range(len(shares))]
    halves = out[len(results) + len(share_shapes) :]
    others = out[len(shapes) - len(pull_results) - len(carry_shapes) :]
    received += [
        others[k : k + size - 1] for k in range(0, len(others), max(size - 1, 1)) if size > 1
    ]
    return (
        out[: len(results)],
        received or [[] for _ in range(16)],
        {key: (halves[2 * k], halves[2 * k + 1]) for k, key in enumerate(totals)},
    )


def dot(left, right):
    return jnp.dot(left, right, preferred_element_type=jnp.float32)


def dot_across(left, right):
    return lax.dot_general(left, right, ACROSS_DIMS, preferred_element_type=jnp.float32)


def dot_down(left, right):
    return lax.dot_general(left, right, DOWN_DIMS, preferred_element_type=jnp.float32)


def own_columns(size, place, width):
    owner = lax.rem(lax.axis_index("fsdp") + place, size)
    return pl.ds(pl.multiple_of(owner * width, width), width)


def times_blocks(values_ref, blocks):
    total = None
    for place, block in enumerate(blocks):
        columns = own_columns(len(blocks), place, block.shape[0])
        part = dot(values_ref[:, columns], block[...])
        total = part if total is None else total + part
    return total


def add_back(total_ref, values, blocks, scale=None):
    for place, block in enumerate(blocks):
        columns = own_columns(len(blocks), place, block.shape[0])
        part = dot_across(values, block[...])
        total_ref[:, columns] += part if scale is None else scale * part


def centred(values):
    centre = values - jnp.mean(values, axis=-1, keepdims=True)
    spread = jnp.mean(centre * centre, axis=-1, keepdims=True)
    scale = lax.rsqrt(spread + EPSILON)
    return centre * scale, scale


BIAS_LINES = (6, 7, 9, 10, 8, 11)
TAP_LINE = 12


def gain_line(lines_ref, norm):
    return lines_ref[norm : norm + 1, :]


def bias_line(lines_ref, norm):
    return lines_ref[BIAS_LINES[norm] : BIAS_LINES[norm] + 1, :]


def tap_line(lines_ref, tap):
    return lines_ref[TAP_LINE + tap : TAP_LINE + tap + 1, :]


def norm_low(values, lines_ref, norm):
    hat, _ = centred(values)
    return (hat * gain_line(lines_ref, norm) + bias_line(lines_ref, norm)).astype(jnp.bfloat16)


def norm_grad(grad, values, gain_row):
    hat, scale = centred(values)
    inner = grad * gain_row
    first = jnp.mean(inner, axis=-1, keepdims=True)
    second = jnp.mean(inner * hat, axis=-1, keepdims=True)
    return (
        (inner - first - hat * second) * scale,
        jnp.sum(grad * hat, axis=0, keepdims=True),
        jnp.sum(grad, axis=0, keepdims=True),
    )


def put_rows(ref, *lines):
    for place, line in enumerate(lines):
        ref[pl.ds(place, 1), :] = line
    ref[pl.ds(len(lines), ref.shape[0] - len(lines)), :] = jnp.zeros(
        (ref.shape[0] - len(lines), ref.shape[1]), ref.dtype
    )


def segment_of(lengths_ref, places):
    ends = lengths_ref[0, 0]
    segment = (places >= ends).astype(jnp.int32)
    for index in range(1, lengths_ref.shape[1]):
        ends = ends + lengths_ref[0, index]
        segment += (places >= ends).astype(jnp.int32)
    return segment


def frame_marks(lengths_ref, frames, taps=0):
    places = lax.broadcasted_iota(jnp.int32, (frames, 1), 0)
    segment = segment_of(lengths_ref, places)
    valid = (segment < lengths_ref.shape[1]).astype(jnp.float32)
    marks = []
    for tap in range(taps):
        moved = places + (tap - taps // 2)
        same = (segment_of(lengths_ref, moved) == segment) & (moved >= 0) & (moved < frames)
        marks.append(same.astype(jnp.float32))
    return valid, marks


def same_segment(lengths_ref, frames):
    down = segment_of(lengths_ref, lax.broadcasted_iota(jnp.int32, (frames, 1), 0))
    across = segment_of(lengths_ref, lax.broadcasted_iota(jnp.int32, (1, frames), 1))
    return down == across


TILE = 1024


def feed_forward(w_in, w_out, flow, normed_ref, hidden, slope_ref, y_ref):
    inner = slope_ref.shape[1]
    for part in range(inner // TILE):
        columns = pl.ds(part * TILE, TILE)
        before = times_blocks(normed_ref, w_in(part))
        gate = jax.nn.sigmoid(before)
        value = (before * gate).astype(jnp.bfloat16)
        flow.staged[hidden][:, columns] = value
        flow.put(hidden, columns)
        slope_ref[:, columns] = (gate * (1.0 + before * (1.0 - gate))).astype(jnp.bfloat16)
        add_back(y_ref, value, w_out(part), 0.5)


def feed_forward_back(blocks_in, blocks_out, low_ref, slope_ref, flow, result, normed_ref):
    inner = slope_ref.shape[1]
    normed_ref[...] = jnp.zeros_like(normed_ref)
    for part in range(inner // TILE):
        columns = pl.ds(part * TILE, TILE)
        grad = times_blocks(low_ref, blocks_out(part)) * slope_ref[:, columns].astype(jnp.float32)
        grad = grad.astype(jnp.bfloat16)
        flow.staged[result][:, columns] = grad
        flow.put(result, columns)
        add_back(normed_ref, grad, blocks_in(part))


def head_scores(query, key, bias_row, same, scale):
    frames = query.shape[0]
    spread = jnp.broadcast_to(bias_row, (frames, bias_row.shape[1]))
    relative = pltpu.roll(spread, 0, 1, stride=1, stride_axis=0)[:, :frames]
    return jnp.where(same, dot_across(query, key) * scale + relative, MASKED)


def softmax_rows(scores):
    powers = jnp.exp(scores - jnp.max(scores, axis=-1, keepdims=True))
    return powers / jnp.sum(powers, axis=-1, keepdims=True)


def split(items, count):
    items = list(items)
    return [items[k : k + count] for k in range(0, len(items), count)]


def front(
    x, own_lines, own_bias, lengths, heads, taps, weights, size, collective_id
):
    frames, width = x.shape
    inner = weights[0].shape[1]
    head = width // heads
    small = [own_lines, own_bias, lengths]
    large = [(x, width)]
    large += [(block, TILE) for block in weights[:2]] + [(block, width) for block in weights[2:]]
    order = [(0, 0)]
    order += [(index, part) for part in range(inner // TILE) for index in (1, 2)]
    order += [(3, part) for part in range(3)] + [(4, 0), (5, 1), (5, 0)]
    low, full = jnp.bfloat16, jnp.float32
    results = [
        ((frames, width), low),
        ((frames, inner), low),
        ((frames, inner), low),
        ((frames, width), full),
        ((frames, width), low),
        ((frames, width), low),
        ((frames, width), low),
        ((frames, width), low),
        ((frames, width), low),
        ((frames, width), full),
        ((frames, width), low),
        ((frames, width), full),
        ((frames, width), full),
        ((frames, width), full),
        ((8, width), full),
        ((own_lines.shape[0], width), full),
        ((-(-heads // 8) * 8, own_bias.shape[1]), full),
    ]

    def body(flow, small_refs, _):
        own_lines_ref, own_bias_ref, lengths_ref = small_refs
        valid, marks = frame_marks(lengths_ref, frames, taps)
        (
            normed_one,
            hidden,
            slope,
            x1,
            normed_attn,
            query_ref,
            key_ref,
            value_ref,
            context,
            x2,
            normed_conv,
            gated_ref,
            gate_ref,
            mixed_ref,
            sums_ref,
            lines_ref,
            bias_ref,
        ) = flow.staged
        small_places = [places for _, places in flow.pull_small]
        blocks = [own_lines_ref] + (flow.take_small(small_places[0]) if size > 1 else [])
        for place, block in enumerate(blocks):
            lines_ref[:, own_columns(size, place, block.shape[1])] = block[...]
        flow.put(15)
        blocks = [own_bias_ref] + (flow.take_small(small_places[1]) if size > 1 else [])
        for place, block in enumerate(blocks):
            owner = lax.rem(lax.axis_index("fsdp") + place, size)
            for row in range(heads // size):
                bias_ref[pl.ds(owner * (heads // size) + row, 1), :] = block[row : row + 1, :]
        flow.put(16)
        values = flow.take(0)[...].astype(jnp.float32)
        normed_one[...] = norm_low(values, lines_ref, 0)
        flow.put(0)
        x1[...] = values
        feed_forward(
            lambda part: flow.take_all(1, part),
            lambda part: flow.take_all(2, part),
            flow,
            normed_one,
            1,
            slope,
            x1,
        )
        flow.put(2)
        flow.put(3)

        normed_attn[...] = norm_low(x1[...], lines_ref, 1)
        flow.put(4)
        for part, ref in enumerate((query_ref, key_ref, value_ref)):
            ref[...] = times_blocks(normed_attn, flow.take_all(3, part)).astype(jnp.bfloat16)
            flow.put(5 + part)
        same = same_segment(lengths_ref, frames)
        for place in range(heads):
            columns = slice(place * head, (place + 1) * head)
            scores = head_scores(
                query_ref[:, columns],
                key_ref[:, columns],
                bias_ref[place : place + 1, :],
                same,
                head**-0.5,
            )
            attend = softmax_rows(scores).astype(jnp.bfloat16)
            context[:, columns] = dot(attend, value_ref[:, columns]).astype(jnp.bfloat16)
        flow.put(8)
        x2[...] = x1[...] + times_blocks(context, flow.take_all(4))
        flow.put(9)

        normed_conv[...] = norm_low(x2[...], lines_ref, 2)
        flow.put(10)
        gate = jax.nn.sigmoid(times_blocks(normed_conv, flow.take_all(5, 1)))
        gate_ref[...] = gate
        flow.put(12)
        gated_ref[...] = times_blocks(normed_conv, flow.take_all(5, 0)) * gate
        flow.put(11)
        mixed = jnp.zeros((frames, width), jnp.float32)
        for tap in range(taps):
            offset = tap - taps // 2
            gated = gated_ref[...]
            moved = gated if offset == 0 else pltpu.roll(gated, -offset % frames, 0)
            mixed += tap_line(lines_ref, tap) * (moved * marks[tap])
        mixed_ref[...] = mixed
        flow.put(13)
        weighted = valid * mixed
        put_rows(
            sums_ref,
            jnp.sum(weighted, axis=0, keepdims=True),
            jnp.sum(weighted * mixed, axis=0, keepdims=True),
            jnp.broadcast_to(jnp.sum(valid, axis=0, keepdims=True), (1, width)),
        )
        flow.put(14)

    results, pulled, _ = fused(
        body,
        small,
        large,
        results,
        order,
        size=size,
        collective_id=collective_id,
        pulls=range(1, 6),
        small_pulls=(0, 1),
    )
    return results, [[own, *others] for own, others in zip(weights, pulled)]


def batch_stats(totals_ref):
    count = totals_ref[2:3, :]
    mean = totals_ref[0:1, :] / count
    rstd = lax.rsqrt(totals_ref[1:2, :] / count - mean * mean + EPSILON)
    return count, mean, rstd


def turn(x, mixed, totals, cotangent, lengths, lines, w_conv, w_in, w_out, size, collective_id):
    frames, width = x.shape
    inner = w_in.shape[1]
    small = [totals, lengths, lines]
    large = [(mixed, width), (x, width), (w_conv, width), (w_in, TILE), (w_out, TILE)]
    large += [(cotangent, width)]
    order = [(0, 0), (1, 0), (2, 0)]
    order += [(index, part) for part in range(inner // TILE) for index in (3, 4)]
    order += [(5, 0)]
    low, full = jnp.bfloat16, jnp.float32
    results = [
        ((frames, width), low),
        ((frames, width), low),
        ((frames, inner), low),
        ((frames, width), low),
        ((frames, width), low),
        ((frames, inner), low),
        ((frames, width), low),
        ((frames, width), full),
        ((frames, width), full),
        ((8, width), full),
        ((8, width), full),
        ((8, width), full),
    ]
    scratch = [
        pltpu.VMEM((frames, inner), low),
        pltpu.VMEM((frames, width), full),
        pltpu.VMEM((frames, width), full),
        pltpu.VMEM((frames, width), full),
    ]

    def body(flow, small_refs, rest):
        totals_ref, lengths_ref, lines_ref = small_refs
        valid, _ = frame_marks(lengths_ref, frames)
        slope, x3, x4, normed_grad = rest
        (
            swish,
            normed,
            hidden,
            out_ref,
            low_two,
            before,
            low_conv,
            grad_ref,
            hat_grad,
            sums_final,
            sums_two,
            sums_batch,
        ) = flow.staged
        _, mean, rstd = batch_stats(totals_ref)
        mixed_ref = flow.take(0)
        z = (mixed_ref[...] - mean) * rstd * gain_line(lines_ref, 5) + bias_line(lines_ref, 5)
        swish[...] = (z * jax.nn.sigmoid(z)).astype(jnp.bfloat16)
        flow.put(0)
        x2_ref = flow.take(1)
        conv_blocks = flow.take_all(2)
        x3[...] = x2_ref[...] + times_blocks(swish, conv_blocks)
        normed[...] = norm_low(x3[...], lines_ref, 3)
        flow.put(1)
        x4[...] = x3[...]
        feed_forward(
            functools.partial(flow.take_all, 3),
            functools.partial(flow.take_all, 4),
            flow,
            normed,
            2,
            slope,
            x4,
        )
        if size > 1:
            for index in (2, 1, 0):
                flow.share(index)

        gain_row = gain_line(lines_ref, 4)
        hat, _ = centred(x4[...])
        out_ref[...] = (valid * (hat * gain_row + bias_line(lines_ref, 4))).astype(jnp.bfloat16)
        flow.put(3)
        grad = valid * flow.take(len(large) - 1)[...].astype(jnp.float32)
        grad_values, grad_gain, grad_bias = norm_grad(grad, x4[...], gain_row)
        grad_ref[...] = grad_values
        low_two[...] = (0.5 * grad_values).astype(jnp.bfloat16)
        flow.put(4)
        if size > 1:
            flow.share(4)
        put_rows(sums_final, grad_gain, grad_bias)
        flow.put(9)

        feed_forward_back(
            functools.partial(flow.held_all, 3),
            functools.partial(flow.held_all, 4),
            low_two,
            slope,
            flow,
            5,
            normed_grad,
        )
        if size > 1:
            flow.share(5)
        branch, grad_gain, grad_bias = norm_grad(
            normed_grad[...], x3[...], gain_line(lines_ref, 3)
        )
        total = grad_ref[...] + branch
        grad_ref[...] = total
        flow.put(7)
        low_conv[...] = total.astype(jnp.bfloat16)
        flow.put(6)
        if size > 1:
            flow.share(6)
        put_rows(sums_two, grad_gain, grad_bias)
        flow.put(10)

        for place, block in enumerate(conv_blocks):
            columns = own_columns(size, place, block.shape[0])
            hat_grad[:, columns] = dot_across(low_conv[...], block[...])
        hat = (mixed_ref[...] - mean) * rstd
        gain_row = gain_line(lines_ref, 5)
        z = hat * gain_row + bias_line(lines_ref, 5)
        gate = jax.nn.sigmoid(z)
        grad_z = hat_grad[...] * gate * (1.0 + z * (1.0 - gate))
        grad_hat = grad_z * gain_row
        hat_grad[...] = grad_hat
        flow.put(8)
        put_rows(
            sums_batch,
            jnp.sum(grad_hat, axis=0, keepdims=True),
            jnp.sum(grad_hat * hat, axis=0, keepdims=True),
            jnp.sum(grad_z * hat, axis=0, keepdims=True),
            jnp.sum(grad_z, axis=0, keepdims=True),
        )
        flow.put(11)

    return fused(
        body,
        small,
        large,
        results,
        order,
        scratch,
        shares={0: "columns", 1: "columns", 2: "all", 4: "columns", 5: "all", 6: "all"},
        size=size,
        collective_id=collective_id,
        pulls=(2, 3, 4),
        pulls_stay=True,
    )[:2]


def back_front(
    hat_grad,
    gated,
    gate,
    mixed,
    totals,
    back,
    grad,
    x2,
    x1,
    lines,
    bias_table,
    lengths,
    taps,
    packed,
    w_conv,
    w_out,
    w_qkv,
    collective_id,
    **jobs,
):
    frames, width = x1.shape
    count = len(w_conv)
    heads = bias_table.shape[0]
    head = width // heads
    flip = (
        jnp.arange(frames)[:, None] + jnp.arange(frames)[None, :] == frames - 1
    ).astype(jnp.bfloat16)
    small = [totals, back, lengths, lines, bias_table, flip]
    large = [(array, width) for array in (hat_grad, mixed, gated, gate)]
    large += [(block, width) for block in w_conv]
    large += [(array, width) for array in (x2, grad)]
    large += [(block, width) for block in w_out]
    large += [(array, width) for array in packed]
    large += [(block, width) for block in w_qkv]
    large += [(x1, width)]
    conv = list(range(4, 4 + count))
    place_x2 = 4 + count
    out = list(range(place_x2 + 2, place_x2 + 2 + count))
    place_packed = out[-1] + 1
    qkv = list(range(place_packed + 3, place_packed + 3 + count))
    order = None
    low, full = jnp.bfloat16, jnp.float32
    results = [((frames, width), low)] * 7 + [((frames, width), full)]
    results += [((8, width), full)] * 3 + [(bias_table.shape, full)]
    scratch = [
        pltpu.VMEM((frames, width), full),
        pltpu.VMEM((frames, width), full),
        pltpu.VMEM((frames, width), low),
    ]

    def body(flow, small_refs, rest):
        (
            totals_ref,
            back_ref,
            lengths_ref,
            lines_ref,
            bias_ref,
            flip_ref,
        ) = small_refs
        valid, marks = frame_marks(lengths_ref, frames, taps)
        normed_grad, grad_mixed_ref, grad_context = rest
        one, two, low_attn, *grad_refs = flow.staged[:6]
        low_one, grad_ref, sums_kernel, sums_conv, sums_attn, sums_rel = flow.staged[6:]
        valid_count, mean, rstd = batch_stats(totals_ref)
        grad_var = -0.5 * rstd * rstd * back_ref[1:2, :]
        grad_mean = -rstd * back_ref[0:1, :] - 2.0 * mean * grad_var
        hat_ref, mixed_ref = flow.take(0), flow.take(1)
        grad_mixed_ref[...] = (
            hat_ref[...] * rstd
            + valid * (grad_mean + 2.0 * mixed_ref[...] * grad_var) / valid_count
        )
        gated_ref = flow.take(2)
        normed_grad[...] = jnp.zeros_like(normed_grad)
        kernel_grads = []
        for tap in range(taps):
            offset = tap - taps // 2
            masked = grad_mixed_ref[...] * marks[tap]
            gated = gated_ref[...]
            moved = gated if offset == 0 else pltpu.roll(gated, -offset % frames, 0)
            kernel_grads.append(jnp.sum(masked * moved, axis=0, keepdims=True))
            moved = masked if offset == 0 else pltpu.roll(masked, offset % frames, 0)
            normed_grad[...] += tap_line(lines_ref, tap) * moved
        put_rows(sums_kernel, *kernel_grads)
        flow.put(8)
        gate_now = flow.take(3)[...]
        grad_gated = normed_grad[...]
        one[...] = (grad_gated * gate_now).astype(jnp.bfloat16)
        flow.put(0)
        if count > 1:
            flow.share(0)
        two[...] = (grad_gated * gated_ref[...] * (1.0 - gate_now)).astype(jnp.bfloat16)
        flow.put(1)
        if count > 1:
            flow.share(1)
        normed_grad[...] = jnp.zeros_like(normed_grad)
        for part, ref in enumerate((one, two)):
            add_back(normed_grad, ref[...], [flow.take(index, part) for index in conv])
        branch, grad_gain, grad_bias = norm_grad(
            normed_grad[...], flow.take(place_x2)[...], gain_line(lines_ref, 2)
        )
        total = flow.take(place_x2 + 1)[...] + branch
        grad_ref[...] = total
        low_attn[...] = total.astype(jnp.bfloat16)
        flow.put(2)
        if count > 1:
            flow.share(2)
        put_rows(sums_conv, grad_gain, grad_bias)
        flow.put(9)

        for place, index in enumerate(out):
            block = flow.take(index)
            columns = own_columns(count, place, block.shape[0])
            grad_context[:, columns] = dot_across(low_attn[...], block[...]).astype(jnp.bfloat16)
        packed_refs = [flow.take(place_packed + part) for part in range(3)]
        same = same_segment(lengths_ref, frames)
        scale = head**-0.5
        reach = bias_ref.shape[1]
        for place in range(heads):
            columns = slice(place * head, (place + 1) * head)
            query, key, value = (ref[:, columns] for ref in packed_refs)
            bias_row = bias_ref[place : place + 1, :]
            attend = softmax_rows(head_scores(query, key, bias_row, same, scale))
            context = grad_context[:, columns]
            grad_attend = dot_across(context, value)
            grad_value = dot_down(attend.astype(jnp.bfloat16), context)
            grad_scores = attend * (
                grad_attend - jnp.sum(grad_attend * attend, axis=-1, keepdims=True)
            )
            grad_low = grad_scores.astype(jnp.bfloat16)
            padded = jnp.concatenate(
                [dot(grad_low, flip_ref[...]), jnp.zeros((frames, reach - frames), jnp.float32)],
                axis=1,
            )
            skewed = pltpu.roll(padded, 0, 1, stride=1, stride_axis=0)
            sums_rel[place : place + 1, :] = jnp.sum(skewed, axis=0, keepdims=True)
            grad_query = dot(grad_low, key) * scale
            grad_key = dot_down(grad_low, query) * scale
            for ref, part in zip(grad_refs, (grad_query, grad_key, grad_value)):
                ref[:, columns] = part.astype(jnp.bfloat16)
        flow.put(11)
        normed_grad[...] = jnp.zeros_like(normed_grad)
        for part, ref in enumerate(grad_refs):
            flow.put(3 + part)
            if count > 1:
                flow.share(3 + part)
            add_back(normed_grad, ref[...], [flow.take(index, part) for index in qkv])
        branch, grad_gain, grad_bias = norm_grad(
            normed_grad[...], flow.take(len(large) - 1)[...], gain_line(lines_ref, 1)
        )
        total = grad_ref[...] + branch
        grad_ref[...] = total
        flow.put(7)
        low_one[...] = (0.5 * total).astype(jnp.bfloat16)
        flow.put(6)
        if count > 1:
            flow.share(6)
        put_rows(sums_attn, grad_gain, grad_bias)
        flow.put(10)

    shares = {0: "all", 1: "all", 2: "all", 3: "all", 4: "all", 5: "all", 6: "columns"}
    return fused(
        body, small, large, results, order, scratch, shares, count, collective_id, **jobs
    )


def back_end(low, grad, x, lines, slope, w_in, w_out, collective_id, **jobs):
    frames, width = x.shape
    inner, count = w_in[0].shape[1], len(w_in)
    large = [(low, width)] + [(block, TILE) for block in w_out + w_in]
    large += [(slope, TILE), (x, width), (grad, width)]
    groups = split(range(1, 1 + 2 * count), count)
    place_slope = 1 + 2 * count
    order = [(0, 0)]
    for part in range(inner // TILE):
        order += [(index, part) for index in groups[0]] + [(place_slope, part)]
        order += [(index, part) for index in groups[1]]
    order += [(place_slope + 1, 0), (place_slope + 2, 0)]
    results = [
        ((frames, inner), jnp.bfloat16),
        ((frames, width), jnp.bfloat16),
        ((8, width), jnp.float32),
    ]

    def body(flow, small_refs, rest):
        (lines_ref,), (normed_grad,) = small_refs, rest
        before, out_ref, sums_ref = flow.staged

        def w_out_part(part):
            blocks = [flow.take(index, part) for index in groups[0]]
            flow.take(place_slope, part)
            return blocks

        def w_in_part(part):
            return [flow.take(index, part) for index in groups[1]]

        feed_forward_back(
            w_in_part, w_out_part, flow.take(0), flow.held[place_slope], flow, 0, normed_grad
        )
        if count > 1:
            flow.share(0)
        values = flow.take(place_slope + 1)[...].astype(jnp.float32)
        branch, grad_gain, grad_bias = norm_grad(normed_grad[...], values, gain_line(lines_ref, 0))
        out_ref[...] = (flow.take(place_slope + 2)[...] + branch).astype(jnp.bfloat16)
        flow.put(1)
        put_rows(sums_ref, grad_gain, grad_bias)
        flow.put(2)

    scratch = [pltpu.VMEM((frames, width), jnp.float32)]
    shares = {0: "all"}
    return fused(
        body, [lines], large, results, order, scratch, shares, count, collective_id, **jobs
    )


def halves_plainly(jobs, bits):
    products = {}
    for lefts, rights, first, columns, key in jobs:
        rows = lefts[0].shape[1] // len(lefts)
        own = lax.dynamic_slice_in_dim(lefts[0], lax.axis_index("fsdp") * rows, rows, axis=1)
        left = jnp.concatenate([own, *lefts[1:]])
        right = jnp.concatenate(rights)[:, first : first + columns]
        products.setdefault(key, []).append(dot_down(left, right).astype(jnp.bfloat16))
    halves = {}
    for key, parts in products.items():
        product = jnp.concatenate(parts, axis=1)
        half = product.shape[0] // 2
        upper = lax.rem(lax.axis_index("dp") // bits[key[1]], 2)
        halves[key] = tuple(
            lax.dynamic_slice_in_dim(product, part * half, half, axis=0)
            for part in (1 - upper, upper)
        )
    return halves


def join_body(bits, counts, *refs):
    step = pl.program_id(0)
    out_ref = refs[-1]
    half = refs[0].shape[0]
    first = 0
    for index, (bit, count) in enumerate(zip(bits, counts)):
        upper = lax.rem(lax.axis_index("dp") // bit, 2)

        @pl.when((step >= first) & (step < first + count))
        def _(index=index, upper=upper):
            for ref, part in zip(refs[2 * index : 2 * index + 2], (upper, 1 - upper)):
                rows = pl.ds(pl.multiple_of(part * half, half), half)
                out_ref[rows, :] = ref[...].astype(jnp.float32)

        first += count


def join(parts):
    tile = 512 if any(part[3] % 1024 or part[4] % 1024 for part in parts) else 1024
    counts = [columns // tile for _, _, _, _, columns in parts]
    rows = 2 * parts[0][1].shape[0]
    specs, flat, first = [], [], 0
    for (_, mine, other, start, _), count in zip(parts, counts):

        def index(step, first=first, count=count, start=start // tile):
            return (0, start + jnp.clip(step - first, 0, count - 1))

        specs += [pl.BlockSpec((rows // 2, tile), index)] * 2
        flat += [mine, other]
        first += count
    return pl.pallas_call(
        functools.partial(join_body, [part[0] for part in parts], counts),
        grid=(first,),
        out_shape=jax.ShapeDtypeStruct((rows, first * tile), jnp.float32),
        in_specs=specs,
        out_specs=pl.BlockSpec((rows, tile), lambda step: (0, step)),
        compiler_params=pltpu.CompilerParams(vmem_limit_bytes=60 * 2**20),
    )(*flat)


def bias_lines(table, frames):
    heads, middle = table.shape[0], (table.shape[1] - 1) // 2
    half = -(-frames // 64) * 64
    above = jnp.broadcast_to(table[:, -1:], (heads, half - middle - 1))
    below = jnp.broadcast_to(table[:, :1], (heads, half - middle))
    return jnp.concatenate([table[:, middle:], above, below, table[:, :middle]], axis=1)


def bias_lines_back(sums, frames, reach):
    return jnp.concatenate(
        [
            jnp.sum(sums[:, frames - 1 + reach :], axis=1, keepdims=True),
            sums[:, frames - reach : frames - 1 + reach][:, ::-1],
            jnp.sum(sums[:, : frames - reach], axis=1, keepdims=True),
        ],
        axis=1,
    )


def eight_lines(*lines):
    lines = list(lines)
    return jnp.stack(lines + [jnp.zeros_like(lines[0])] * (-len(lines) % 8))


def per_device(
    sizes,
    inputs,
    cotangent,
    lengths,
    ffn1_in,
    ffn1_out,
    attn_qkv,
    attn_out,
    rel_table,
    conv_in,
    depth_kernel,
    conv_out,
    ffn2_in,
    ffn2_out,
    gains,
    biases,
    inner_biases,
):
    dp_size, fsdp_size = sizes
    axes = (("fsdp", fsdp_size), ("dp", dp_size))
    rows = Rows(fsdp_size)
    groups = Groups(axes)
    frames, width = inputs.shape
    taps = depth_kernel.shape[1]

    own_lines = jnp.concatenate([gains, biases, inner_biases, depth_kernel], axis=1)
    own_lines = jnp.pad(own_lines, ((0, 0), (0, -own_lines.shape[1] % 8))).astype(jnp.float32).T
    own_bias = bias_lines(rel_table.astype(jnp.float32), frames)
    own_bias = jnp.pad(own_bias, ((0, -own_bias.shape[0] % 8), (0, 0)))
    heads = rel_table.shape[0] * fsdp_size

    (
        (
            normed_one,
            hidden_one,
            slope_one,
            x1,
            normed_attn,
            *packed,
            context,
            x2,
            normed_conv,
            gated,
            gate,
            mixed,
            sums,
            lines,
            bias_table,
        ),
        (w_ffn1_in, w_ffn1_out, w_qkv, w_attn_out, w_conv_in),
    ) = front(
        inputs,
        own_lines,
        own_bias,
        lengths,
        heads,
        taps,
        (ffn1_in, ffn1_out, attn_qkv, attn_out, conv_in),
        fsdp_size,
        6,
    )
    totals, _ = sum_and_share(rows, axes, sums, 3, [], 0)
    results, shared = turn(
        x2,
        mixed,
        totals,
        cotangent,
        lengths,
        lines,
        conv_out,
        ffn2_in,
        ffn2_out,
        fsdp_size,
        7,
    )
    swish, normed_two, hidden_two, layer_out, low_two, before_two, low_conv = results[:7]
    grad, hat_grad, sums_final, sums_two, sums_batch = results[7:]
    arrays = (swish, normed_two, hidden_two, low_two, before_two, low_conv)
    left_swish, left_normed_two, right_hidden_two, left_low_two, right_before_two, right_low_conv = [
        [own, *others] for own, others in zip(arrays, shared)
    ]
    back, _ = sum_and_share(rows, axes, sums_batch, 2, [], 1)

    inner = hidden_two.shape[1]
    main, half, rest = inner * 3 // 4, inner * 3 // 8, inner // 4
    jobs = [
        (left_low_two, right_hidden_two, 0, main, (0, 0)),
        (left_normed_two, right_before_two, 0, main, (0, 1)),
        (left_low_two, right_hidden_two, main, rest, (0, 2)),
        (left_swish, right_low_conv, 0, width, (0, 2)),
        (left_normed_two, right_before_two, main, rest, (0, 3)),
    ]
    arrays = (normed_conv, context, normed_attn, normed_one)
    results, shared, bundles = groups.along(
        jobs,
        functools.partial(
            back_front,
            hat_grad,
            gated,
            gate,
            mixed,
            totals,
            back,
            grad,
            x2,
            x1,
            lines,
            bias_table,
            lengths,
            taps,
            packed,
            w_conv_in,
            w_attn_out,
            w_qkv,
            3,
            spread=True,
            carried=[(array, "columns") for array in arrays] + [(hidden_one, "all")],
        ),
    )
    two = bundles[0]
    *back_lefts, low_one, grad, sums_kernel, sums_conv, sums_attn, sums_rel = results
    right_one, right_two, right_low_attn, right_q, right_k, right_v, left_low_one = [
        [own, *others] for own, others in zip((*back_lefts, low_one), shared)
    ]
    left_normed_conv, left_context, left_normed_attn, left_normed_one, right_hidden_one = [
        [own, *others] for own, others in zip((*arrays, hidden_one), shared[7:])
    ]

    jobs = [
        (left_normed_conv, right_one, 0, width, (0, 0)),
        (left_normed_conv, right_two, 0, width, (0, 1)),
        (left_context, right_low_attn, 0, width, (0, 3)),
        (left_normed_attn, right_q, 0, width, (0, 0)),
        (left_normed_attn, right_k, 0, width, (0, 1)),
        (left_normed_attn, right_v, 0, width, (0, 3)),
        (left_low_one, right_hidden_one, 0, half, (1, 0)),
        (left_low_one, right_hidden_one, half, half, (1, 1)),
        (left_low_one, right_hidden_one, main, rest, (1, 2)),
        (left_normed_one, 0, 0, half, (2, 0)),
        (left_normed_one, 0, half, half, (2, 1)),
        (left_normed_one, 0, main, rest, (2, 3)),
    ]
    (_, input_grad, sums_one), _, bundles = groups.along(
        jobs,
        functools.partial(
            back_end,
            low_one,
            grad,
            inputs,
            lines,
            slope_one,
            w_ffn1_in,
            w_ffn1_out,
            4,
            spread=True,
        ),
    )
    mid, out, end = bundles[0], bundles[1], bundles[2]

    bundles = (out, mid, two, end)
    middle, sums = groups.middle(
        [[bundle[kind] for bundle in bundles if kind in bundle] for kind in groups.kinds],
        (
            sums_one,
            sums_attn,
            sums_conv,
            sums_two,
            sums_final,
            sums_batch,
            sums_kernel,
            sums_rel,
        ),
        [(0, 1)] * 5 + [(2, 3), tuple(range(taps)), tuple(range(heads))],
        width,
        2,
    )
    middle = [iter(arrays) for arrays in middle]
    out, mid, two, end = [
        {kind: next(middle[kind]) for kind in groups.kinds if kind in bundle} for bundle in bundles
    ]
    mid, two = groups.finish(mid), groups.finish(two)
    sum_qkv = groups.join(*[(mid[kind], width, width) for kind in (0, 1, 3)])
    sum_conv_in = groups.join((mid[0], 0, width), (mid[1], 0, width))
    sum_attn_out = groups.join((mid[3], 0, width))
    out, sum_qkv, sum_conv_in = lax.optimization_barrier((out, sum_qkv, sum_conv_in))
    out = groups.finish(out)
    sum_ffn2_out = groups.join((two[0], 0, main), (two[2], 0, rest))
    sum_ffn2_in = groups.join((two[1], 0, main), (two[3], 0, rest))
    sum_conv_out = groups.join((two[2], rest, width))
    end, sum_ffn2_out = lax.optimization_barrier((end, sum_ffn2_out))
    end = groups.finish(end)
    sum_ffn1_out = groups.join((out[0], 0, half), (out[1], 0, half), (out[2], 0, rest))
    sum_ffn1_in = groups.join((end[0], 0, half), (end[1], 0, half), (end[3], 0, rest))
    own = lax.dynamic_slice_in_dim(sums, rows.me * gains.shape[0], gains.shape[0], axis=1)
    first = 12 + taps
    rel_sum = lax.dynamic_slice_in_dim(
        sums, first + rows.me * rel_table.shape[0], rel_table.shape[0], axis=0
    )
    rel_sum = bias_lines_back(
        rel_sum[:, : sums_rel.shape[1]], frames, (rel_table.shape[1] - 1) // 2
    )
    return (
        layer_out,
        input_grad,
        sum_ffn1_in,
        sum_ffn1_out,
        sum_qkv,
        sum_attn_out,
        rel_sum,
        sum_conv_in,
        own[12:first].T,
        sum_conv_out,
        sum_ffn2_in,
        sum_ffn2_out,
        own[0:12:2].T,
        jnp.stack([own[1], own[3], own[9]], axis=1),
        jnp.stack([own[5], own[7], own[11]], axis=1),
    )


def solution(mesh):
    frame_spec = P(("dp", "fsdp"), None)
    row_spec = P("fsdp", None)
    sizes = (mesh.shape["dp"], mesh.shape["fsdp"])
    return jax.shard_map(
        functools.partial(per_device, sizes),
        mesh=mesh,
        in_specs=(frame_spec,) * 3 + (row_spec,) * 13,
        out_specs=(frame_spec,) * 2 + (row_spec,) * 13,
        check_vma=False,
    )
```
